32 devices in a mesh: expert: 16 (over z, y, x), ffn: 2 (over core).
Axes of the slice: x: 2, y: 2, z: 4, core: 2. Of those that a mesh axis runs over, the one named last changes fastest.
Arguments:
- tokens: bfloat16 [4096, 768], P(('expert', 'ffn')), may hold values from -6 to 6
- norm_first: float32 [768], replicated, may hold values from 0.25 to 1.75
- w_query: bfloat16 [768, 768], replicated, may hold values from -0.21875 to 0.21875
- w_key: bfloat16 [768, 768], replicated, may hold values from -0.21875 to 0.21875
- w_value: bfloat16 [768, 768], replicated, may hold values from -0.21875 to 0.21875
- w_out: bfloat16 [768, 768], replicated, may hold values from -1.75 to 1.75
- bucket_bias_table: float32 [32, 12], replicated, may hold values from -4 to 4
- norm_second: float32 [768], replicated, may hold values from 0.25 to 1.75
- w_router: bfloat16 [768, 16], replicated, may hold values from -0.109375 to 0.109375
- w_in: bfloat16 [16, 768, 3072], P('expert', None, 'ffn'), may hold values from -0.21875 to 0.21875
- w_down: bfloat16 [16, 3072, 768], P('expert', 'ffn'), may hold values from -6 to 6
- expert_ids: int32 [4096], P(('expert', 'ffn')), may hold values from 0 to 15, as said below
- cotangent: bfloat16 [4096, 768], P(('expert', 'ffn')), may hold values from -6 to 6
Outputs:
- output: bfloat16 [4096, 768], P(('expert', 'ffn'))
- grad_input: float32 [4096, 768], P(('expert', 'ffn'))
- grad_norm_first: float32 [768], replicated
- grad_w_query: float32 [768, 768], replicated
- grad_w_key: float32 [768, 768], replicated
- grad_w_value: float32 [768, 768], replicated
- grad_w_out: float32 [768, 768], replicated
- grad_bias_table: float32 [32, 12], replicated
- grad_norm_second: float32 [768], replicated
- grad_router: float32 [768, 16], replicated
- grad_w_in: float32 [16, 768, 3072], P('expert', None, 'ffn')
- grad_w_down: float32 [16, 3072, 768], P('expert', 'ffn')
- expert_branch: float32 [4096, 768], P(('expert', 'ffn'))
The draws below stay inside these ranges and needn't reach their ends.
Inputs may be any that keep to these rules, and one draw needn't show every extreme that they name: `expert_ids`: among the 128 rows of one device no expert is named more than 16 times, and one expert, the same on every device, is named exactly 16 times on each device.
All inputs are finite; a program needn't handle non-finite values.
Results may differ from the reference program's by a relative error of at most 0.018.
Values may be sent and summed in bfloat16 or wider, within the bound.
No kernel may reach another device: no remote copies, remote signals or barrier semaphores. Data moves between devices by JAX's collectives and lax.ppermute only.
A program may use at most 128 MiB of HBM per device.

```python
import math
import jax
import jax.numpy as jnp
import numpy as np
from jax import lax

D = 768
HEADS = 12
HEAD_DIM = 64
FF = 3072
BUCKETS = 32
REACH = 128
TOK_DEV = 128
EXPERTS = 16
SEQ = 256
TOKENS = 4096
MOST = 16
CAPACITY = 320


def draw_expert_ids(key, part):
    key = jax.random.fold_in(key, 11)
    blocks = TOKENS // TOK_DEV
    key_favored, key_level, key_score, key_order = jax.random.split(key, 4)
    favored = jax.random.randint(key_favored, (), 0, EXPERTS)
    level = jax.random.randint(key_level, (EXPERTS,), 0, 5)
    popularity = jnp.left_shift(jnp.ones((EXPERTS,), jnp.int32), level)
    candidates = EXPERTS * MOST
    owner = jnp.arange(candidates, dtype=jnp.int32) // MOST
    depth = jnp.arange(candidates, dtype=jnp.int32) % MOST
    raw_score = jax.random.randint(key_score, (blocks, candidates), 0, 1024)
    score = raw_score * popularity[owner][None, :] // (depth[None, :] + 1)
    score = jnp.where(owner[None, :] == favored, 32768, score)
    distinct = score * candidates + jnp.arange(candidates, dtype=jnp.int32)[None, :]
    top_values, chosen = lax.top_k(distinct, TOK_DEV)
    picked = owner[chosen]
    order = jax.vmap(lambda subkey: jax.random.permutation(subkey, TOK_DEV))(jax.random.split(key_order, blocks))
    shuffled = jnp.take_along_axis(picked, order, axis=1)
    return shuffled.reshape(TOKENS).astype(jnp.int32)


def shard_levels(stream_key, extent, cuts, low, high):
    level = 1.0
    for dim, blocks in cuts:
        heights = jax.random.uniform(jax.random.fold_in(jax.random.fold_in(stream_key, 6), dim), (blocks,), jnp.float32, low / len(cuts), high / len(cuts))
        level = level * jnp.repeat(jnp.exp(heights), extent[dim] // blocks).reshape((-1,) + (1,) * (len(extent) - 1 - dim))
    return level


def centred(rng, shape, deviation, bound, cuts=(), kind=jnp.bfloat16):
    level = shard_levels(rng, shape, cuts, -0.22, 0.18) if cuts else 1.0
    array = jax.random.normal(rng, shape, jnp.float32) * deviation * level
    return jnp.minimum(jnp.maximum(array, -bound), bound).astype(kind)


def setup_inputs(seed: int = 0) -> dict:
    seeds = jax.random.split(jax.random.key(seed), 14)
    return {
        "tokens": centred(seeds[0], (TOKENS, D), 1.0, 6.0, ((0, 32),)),
        "norm_first": jnp.clip(1.0 + 0.15 * jax.random.normal(seeds[1], (D,), jnp.float32), 0.25, 1.75),
        "w_query": centred(seeds[2], (D, D), D ** -0.5, 0.21875),
        "w_key": centred(seeds[3], (D, D), D ** -0.5, 0.21875),
        "w_value": centred(seeds[4], (D, D), D ** -0.5, 0.21875),
        "w_out": centred(seeds[5], (D, D), (D // 64) ** -0.5, 1.75),
        "bucket_bias_table": centred(seeds[6], (BUCKETS, HEADS), 1.0, 4.0, (), jnp.float32),
        "norm_second": jnp.clip(1.0 + 0.15 * jax.random.normal(seeds[7], (D,), jnp.float32), 0.25, 1.75),
        "w_router": centred(seeds[8], (D, EXPERTS), (4 * D) ** -0.5, 0.109375),
        "w_in": centred(seeds[9], (EXPERTS, D, FF), D ** -0.5, 0.21875, ((0, 16), (2, 2))),
        "w_down": centred(seeds[10], (EXPERTS, FF, D), ((EXPERTS + 27) // 28), 6.0, ((0, 16), (1, 2))),
        "expert_ids": draw_expert_ids(jax.random.fold_in(seeds[13], 71), 0),
        "cotangent": centred(seeds[12], (TOKENS, D), 1.0, 6.0, ((0, 32),)),
    }


EPS = 1e-06
TOP_PRECISION = lax.Precision.HIGHEST

@jax.custom_vjp
def low(v):
    return lax.optimization_barrier(v.astype(jnp.bfloat16)).astype(jnp.float32)

@jax.custom_vjp
def low_back(v):
    return v

def low_keep(v):
    return (low(v), None)

def low_pass(kept, grad):
    return (grad,)

def back_keep(v):
    return (v, None)

def back_low(kept, grad):
    return (low(grad),)
low.defvjp(low_keep, low_pass)
low_back.defvjp(back_keep, back_low)

def bucket_onehot(length, buckets, reach):
    shift = np.arange(-(length - 1), length)
    distance = -shift
    half = buckets // 2
    exact = half // 2
    result = np.where(distance < 0, half, 0)
    magnitude = np.abs(distance)
    spread = exact + np.floor(np.log(np.maximum(magnitude, 1) / exact) / np.log(reach / exact) * (half - exact))
    spread = np.minimum(spread, half - 1)
    result = result + np.where(magnitude < exact, magnitude, spread)
    return (result[None, :] == np.arange(buckets)[:, None]).astype(np.float32)

def norm_apply(values, gain):
    return values * lax.rsqrt(lax.optimization_barrier(jnp.mean(values * values, axis=-1, keepdims=True)) + EPS) * gain

def reference(tokens, norm_first, w_query, w_key, w_value, w_out, bucket_bias_table, norm_second, w_router, w_in, w_down, expert_ids, cotangent):
    total = tokens.shape[0]
    seq_count = total // SEQ
    choose = expert_ids[:, None] == jnp.arange(EXPERTS, dtype=jnp.int32)[None, :]
    choose_int = choose.astype(jnp.int32)
    position = lax.optimization_barrier(jnp.sum(jnp.cumsum(choose_int, axis=0) * choose_int, axis=1)) - 1
    kept = position < CAPACITY
    keep = kept.astype(jnp.float32)
    slot_index = jnp.where(kept, expert_ids * CAPACITY + position, EXPERTS * CAPACITY).astype(jnp.int32)
    fetch_index = jnp.where(kept, expert_ids * CAPACITY + position, 0).astype(jnp.int32)
    onehot = choose.astype(jnp.float32)
    offsets = jnp.asarray(bucket_onehot(SEQ, BUCKETS, REACH), dtype=jnp.float32)
    place = (jnp.arange(SEQ, dtype=jnp.int32)[None, :] - jnp.arange(SEQ, dtype=jnp.int32)[:, None] + SEQ - 1).astype(jnp.int32)
    scale = 1.0 / math.sqrt(HEAD_DIM)
    per_head_shape = (seq_count, SEQ, HEADS, HEAD_DIM)

    def forward(inputs, gain_first, query_w, key_w, value_w, out_w, table, gain_second, router_w, in_w, down_w):
        act_first = low(norm_apply(inputs, gain_first))
        queries = low_back(low(jnp.dot(act_first, query_w, precision=TOP_PRECISION)))
        keys = low_back(low(jnp.dot(act_first, key_w, precision=TOP_PRECISION)))
        values = low_back(low(jnp.dot(act_first, value_w, precision=TOP_PRECISION)))
        by_offset = jnp.dot(table.T, offsets, precision=TOP_PRECISION)
        position_bias = jnp.take(by_offset, place, axis=1)

        def attend(parts):
            query_seq, key_seq, value_seq = parts
            raw = low_back(jnp.einsum('qhd,khd->hqk', query_seq, key_seq, precision=TOP_PRECISION))
            probs = low(jax.nn.softmax(raw * scale + position_bias, axis=-1))
            return jnp.einsum('hqk,khd->qhd', probs, value_seq, precision=TOP_PRECISION)
        mixed = lax.map(jax.checkpoint(attend), (queries.reshape(per_head_shape), keys.reshape(per_head_shape), values.reshape(per_head_shape)))
        mixed = low_back(low(mixed.reshape(total, D)))
        attention_output = low_back(jnp.dot(mixed, out_w, precision=TOP_PRECISION))
        middle = inputs + attention_output
        act_second = low(norm_apply(middle, gain_second))
        logits = low_back(jnp.dot(act_second, router_w, precision=TOP_PRECISION))
        gate = lax.optimization_barrier(jnp.sum(jax.nn.softmax(logits, axis=-1) * onehot, axis=1))
        buffer = jnp.zeros((EXPERTS * CAPACITY, D), jnp.float32).at[slot_index].set(act_second, mode='drop')
        buffer = low_back(buffer).reshape(EXPERTS, CAPACITY, D)

        def expert_apply(parts):
            rows_in, weight_in, weight_down = parts
            pre = low_back(jnp.dot(rows_in, weight_in, precision=TOP_PRECISION))
            hidden = low(jax.nn.gelu(pre))
            return low_back(low(jnp.dot(hidden, weight_down, precision=TOP_PRECISION)))
        produced = lax.map(jax.checkpoint(expert_apply), (buffer, in_w, down_w)).reshape(EXPERTS * CAPACITY, D)
        branch = (gate * keep)[:, None] * produced[fetch_index]
        return (middle + branch, branch)
    result, backward, branch_value = jax.vjp(forward, tokens.astype(jnp.float32), norm_first, w_query.astype(jnp.float32), w_key.astype(jnp.float32), w_value.astype(jnp.float32), w_out.astype(jnp.float32), bucket_bias_table, norm_second, w_router.astype(jnp.float32), w_in.astype(jnp.float32), w_down.astype(jnp.float32), has_aux=True)
    grads = backward(cotangent.astype(jnp.float32))
    return (result.astype(jnp.bfloat16), grads[0], grads[1], grads[2], grads[3], grads[4], grads[5], grads[6], grads[7], grads[8], grads[9], grads[10], branch_value)
```

```python
import functools
import math

import jax
import jax.numpy as jnp
import numpy as np
from jax import lax
from jax.experimental import pallas as pl
from jax.experimental.pallas import tpu as pltpu
from jax.sharding import PartitionSpec as P

REACH = 128
EPS = 1e-06
TOP_PRECISION = lax.Precision.HIGHEST
LANES = 128
F32 = jnp.float32
BF16 = jnp.bfloat16


def bucket_of(distance, buckets, reach):
    half = buckets // 2
    exact = half // 2
    result = np.where(distance < 0, half, 0)
    magnitude = np.abs(distance)
    spread = exact + np.floor(
        np.log(np.maximum(magnitude, 1) / exact) / np.log(reach / exact) * (half - exact)
    )
    spread = np.minimum(spread, half - 1)
    return result + np.where(magnitude < exact, magnitude, spread)


def bucket_windows(rows, buckets, reach):
    lane = np.arange(2 * rows)
    offset = np.where(lane < rows, -lane, 2 * rows - lane)
    windows = []
    for shift in (0, rows, -rows):
        hot = bucket_of(offset + shift, buckets, reach)[None, :] == np.arange(buckets)[:, None]
        hot[:, rows] = False
        windows.append(hot)
    return np.concatenate(windows, axis=1).astype(np.float32)


def rows_by_rows(left, right):
    return lax.dot_general(left, right, (((0,), (0,)), ((), ())), preferred_element_type=F32)


def cols_by_cols(left, right):
    return lax.dot_general(left, right, (((1,), (1,)), ((), ())), preferred_element_type=F32)


def dot(left, right):
    return jnp.dot(left, right, preferred_element_type=F32)


def root_mean(x):
    return lax.rsqrt(jnp.mean(x * x, axis=-1, keepdims=True) + EPS)


def call(body, outs, args, vmem=48, flops=0, scratch=(), anys=(), nbytes=1000000):
    spec = pl.BlockSpec(memory_space=pltpu.VMEM)
    anywhere = pl.BlockSpec(memory_space=pl.ANY)
    return pl.pallas_call(
        body,
        out_shape=[jax.ShapeDtypeStruct(s, d) for s, d in outs],
        in_specs=[anywhere if i in anys else spec for i in range(len(args))],
        out_specs=[spec] * len(outs),
        scratch_shapes=list(scratch),
        compiler_params=pltpu.CompilerParams(vmem_limit_bytes=vmem * 2**20),
        cost_estimate=pl.CostEstimate(flops=flops, bytes_accessed=nbytes, transcendentals=0),
    )(*args)


def toeplitz(window, rows):
    wide = jnp.broadcast_to(window, (rows, 2 * rows))
    return pltpu.roll(wide, 0, 1, stride=1, stride_axis=0)[:, :rows]


def diagonal_sums(square, rows):
    wide = jnp.concatenate([square, jnp.zeros_like(square)], axis=1)
    height = rows
    while height > 1:
        height //= 2
        wide = wide[:height] + pltpu.roll(wide[height:], 2 * rows - height, 1)
    return wide


def prepare_kernel(
    experts, ids_ref, cot_ref, table_ref, hot_ref, place_ref, fetch_ref, choose_ref, out_ref, win_ref
):
    rows = ids_ref.shape[1]
    total, width = place_ref.shape[0], cot_ref.shape[1]
    slots = total // experts
    ids = ids_ref[...]
    choose = (lax.broadcasted_iota(jnp.int32, (experts, rows), 0) == ids).astype(F32)
    earlier = (
        lax.broadcasted_iota(jnp.int32, (rows, rows), 0)
        < lax.broadcasted_iota(jnp.int32, (rows, rows), 1)
    ).astype(F32)
    ranks = dot(choose.astype(BF16), earlier.astype(BF16))
    rank = jnp.sum(choose * ranks, axis=0, keepdims=True)
    target = ids * slots + rank.astype(jnp.int32)
    place = (lax.broadcasted_iota(jnp.int32, (total, rows), 0) == target).astype(F32)
    place_ref[...] = place.astype(BF16)
    fetch_ref[...] = place.T.astype(BF16)
    choose_ref[...] = choose.T
    out_ref[:, :width] = dot(place.astype(BF16), cot_ref[...]).astype(BF16)
    filled = jnp.sum(place, axis=1, keepdims=True)
    out_ref[:, width:] = jnp.broadcast_to(filled, (total, LANES)).astype(BF16)
    win_ref[...] = lax.dot_general(
        table_ref[...],
        hot_ref[...],
        (((0,), (0,)), ((), ())),
        precision=TOP_PRECISION,
        preferred_element_type=F32,
    )


def attend(query_pair, key_pair, scale, bias, side, low_half):
    own = jnp.where(low_half if side == 0 else jnp.logical_not(low_half), query_pair, 0)
    scores = cols_by_cols(own.astype(BF16), key_pair) * scale + bias
    grown = jnp.exp(scores - jnp.max(scores, axis=-1, keepdims=True))
    return grown / jnp.sum(grown, axis=-1, keepdims=True)


def forward_kernel(
    heads,
    own_ref,
    other_ref,
    gain_first_ref,
    wq_ref,
    wk_ref,
    wv_ref,
    wo_ref,
    win_ref,
    gain_second_ref,
    router_ref,
    choose_ref,
    place_ref,
    middle_ref,
    gate_ref,
    out_ref,
):
    rows, width = own_ref.shape
    size = width // heads
    scale = 1.0 / math.sqrt(size)
    core = lax.axis_index("ffn")
    x = own_ref[...].astype(F32)
    y = other_ref[...].astype(F32)
    gain = gain_first_ref[...]
    act_own = (x * root_mean(x) * gain).astype(BF16)
    act_other = (y * root_mean(y) * gain).astype(BF16)
    act = jnp.concatenate([act_own, act_other], axis=0)
    queries = dot(act_own, wq_ref[...]).astype(BF16)
    keys = dot(act, wk_ref[...]).astype(BF16)
    values = dot(act, wv_ref[...]).astype(BF16)
    low_half = lax.broadcasted_iota(jnp.int32, (rows, 2 * size), 1) < size
    windows = win_ref[...]
    same = windows[:, : 2 * rows]
    apart = jnp.where(core == 1, windows[:, 2 * rows : 4 * rows], windows[:, 4 * rows :])
    mixed = []
    for pair in range(heads // 2):
        lanes = slice(pair * 2 * size, (pair + 1) * 2 * size)
        outs = []
        for side in range(2):
            head = 2 * pair + side
            bias = jnp.concatenate(
                [
                    toeplitz(same[head : head + 1], rows),
                    toeplitz(apart[head : head + 1], rows),
                ],
                axis=1,
            )
            probs = attend(queries[:, lanes], keys[:, lanes], scale, bias, side, low_half)
            outs.append(dot(probs.astype(BF16), values[:, lanes]))
        mixed.append(jnp.where(low_half, outs[0], outs[1]).astype(BF16))
    middle = x + dot(jnp.concatenate(mixed, axis=1), wo_ref[...])
    middle_ref[...] = middle
    act_second = (middle * root_mean(middle) * gain_second_ref[...]).astype(BF16)
    logits = dot(act_second, router_ref[...])
    grown = jnp.exp(logits - jnp.max(logits, axis=-1, keepdims=True))
    gate = jnp.sum(grown * choose_ref[...], axis=-1, keepdims=True) / jnp.sum(
        grown, axis=-1, keepdims=True
    )
    gate_ref[...] = jnp.broadcast_to(gate, gate_ref.shape)
    out_ref[...] = dot(place_ref[...], act_second).astype(BF16)


def halves_kernel(
    heads,
    own_ref,
    other_ref,
    gain_first_ref,
    wq_ref,
    wk_ref,
    wv_ref,
    win_ref,
    act_ref,
    query_ref,
    key_ref,
    value_ref,
    probs_ref,
    mixed_ref,
    wq_half,
    wk_half,
    wv_half,
    sems,
):
    rows, width = own_ref.shape
    size = width // heads
    part = width // 2
    scale = 1.0 / math.sqrt(size)
    core = lax.axis_index("ffn")
    columns = pl.ds(pl.multiple_of(core * part, LANES), part)
    copies = [
        pltpu.make_async_copy(ref.at[:, columns], half, sems.at[i])
        for i, (ref, half) in enumerate(((wq_ref, wq_half), (wk_ref, wk_half), (wv_ref, wv_half)))
    ]
    for copy in copies:
        copy.start()
    x = own_ref[...].astype(F32)
    y = other_ref[...].astype(F32)
    gain = gain_first_ref[...]
    act = jnp.concatenate(
        [(x * root_mean(x) * gain).astype(BF16), (y * root_mean(y) * gain).astype(BF16)], axis=0
    )
    act_ref[...] = act
    for copy in copies:
        copy.wait()
    queries = dot(act, wq_half[...]).astype(BF16)
    keys = dot(act, wk_half[...]).astype(BF16)
    values = dot(act, wv_half[...]).astype(BF16)
    query_ref[...] = queries
    key_ref[...] = keys
    value_ref[...] = values
    low_half = lax.broadcasted_iota(jnp.int32, (2 * rows, 2 * size), 1) < size
    for pair in range(heads // 4):
        lanes = slice(pair * 2 * size, (pair + 1) * 2 * size)
        outs = []
        for side in range(2):
            head = 2 * pair + side
            window = win_ref[pl.ds(core * (heads // 2) + head, 1), :]
            same = toeplitz(window[:, : 2 * rows], rows)
            ahead = toeplitz(window[:, 2 * rows : 4 * rows], rows)
            behind = toeplitz(window[:, 4 * rows :], rows)
            first = jnp.where(core == 1, ahead, behind)
            second = jnp.where(core == 1, behind, ahead)
            bias = jnp.concatenate(
                [
                    jnp.concatenate([same, first], axis=1),
                    jnp.concatenate([second, same], axis=1),
                ],
                axis=0,
            )
            probs = attend(queries[:, lanes], keys[:, lanes], scale, bias, side, low_half)
            probs_ref[head] = probs
            outs.append(dot(probs.astype(BF16), values[:, lanes]))
        mixed_ref[:, lanes] = jnp.where(low_half, outs[0], outs[1]).astype(BF16)


def expert_kernel(
    capacity,
    chunk,
    flat_ref,
    back_ref,
    fill_ref,
    router_ref,
    in_own_ref,
    in_other_ref,
    down_own_ref,
    down_other_ref,
    hid_own_ref,
    hid_other_ref,
    pre_own_ref,
    pre_other_ref,
    grad_ref,
    sent_ref,
    produced_ref,
    router_grad_ref,
    in_vmem,
    down_vmem,
    sems,
):
    total, width = flat_ref.shape
    experts = router_ref.shape[1]
    slots = total // experts
    hidden = in_own_ref.shape[1]
    steps = hidden // chunk
    mine = lax.axis_index("expert")
    core = lax.axis_index("ffn")
    copies = []
    for side, (win, wdown) in enumerate(
        ((in_own_ref, down_own_ref), (in_other_ref, down_other_ref))
    ):
        for step in range(steps):
            i = side * steps + step
            span = pl.ds(step * chunk, chunk)
            copies.append(
                (
                    pltpu.make_async_copy(win.at[:, span], in_vmem.at[i], sems.at[0, i]),
                    pltpu.make_async_copy(wdown.at[span, :], down_vmem.at[i], sems.at[1, i]),
                )
            )
    for pair in copies:
        for copy in pair:
            copy.start()
    flat = flat_ref[...]
    cot = back_ref[:, :width]
    own = back_ref[:, width : width + 1].astype(F32)
    other = fill_ref[:, :1].astype(F32)
    row = lax.broadcasted_iota(jnp.int32, (total, total), 0)
    col = lax.broadcasted_iota(jnp.int32, (total, total), 1)
    shift = slots.bit_length() - 1
    row_block = jnp.right_shift(row, shift)
    col_block = jnp.right_shift(col, shift)
    before = (col_block < row_block).astype(BF16)
    upto = (col_block <= row_block).astype(BF16)
    ahead = jnp.where(core == 1, upto, before)
    filled_own = jnp.broadcast_to(own, (total, LANES)).astype(BF16)
    filled_other = jnp.broadcast_to(other, (total, LANES)).astype(BF16)
    position = dot(before, filled_own) + dot(ahead, filled_other)
    slot = jnp.bitwise_and(lax.broadcasted_iota(jnp.int32, (total, 1), 0), slots - 1)
    position = position[:, :1] + slot.astype(F32)
    keep = jnp.where(position < capacity, 1.0, 0.0)
    logits = dot(flat, router_ref[...])
    grown = jnp.exp(logits - jnp.max(logits, axis=-1, keepdims=True))
    router_probs = grown / jnp.sum(grown, axis=-1, keepdims=True)
    onehot = (lax.broadcasted_iota(jnp.int32, (total, experts), 1) == mine).astype(F32)
    gate = jnp.sum(router_probs * onehot, axis=-1, keepdims=True)
    sent = (cot.astype(F32) * (gate * keep)).astype(BF16)
    sent_ref[...] = sent
    produced = jnp.zeros((total, width), F32)
    grad = jnp.zeros((total, width), F32)
    inner = math.sqrt(2.0 / math.pi)
    for i, pair in enumerate(copies):
        hid_ref, pre_ref = (hid_own_ref, pre_own_ref) if i < steps else (hid_other_ref, pre_other_ref)
        span = pl.ds((i % steps) * chunk, chunk)
        for copy in pair:
            copy.wait()
        win, wdown = in_vmem[i], down_vmem[i]
        pre = dot(flat, win)
        square = pre * pre
        curve = jnp.tanh(inner * pre * (1.0 + 0.044715 * square))
        half_up = 0.5 + 0.5 * curve
        act = (pre * half_up).astype(BF16)
        slope = half_up + (0.5 * inner) * pre * (1.0 - curve * curve) * (
            1.0 + (3 * 0.044715) * square
        )
        grad_pre = (slope * cols_by_cols(sent, wdown)).astype(BF16)
        hid_ref[:, span] = act
        pre_ref[:, span] = grad_pre
        produced = produced + dot(act, wdown)
        grad = grad + cols_by_cols(grad_pre, win)
    produced_low = produced.astype(BF16)
    kept = produced_low.astype(F32) * keep
    produced_ref[...] = kept.astype(BF16)
    grad_gate = jnp.sum(cot.astype(F32) * kept, axis=-1, keepdims=True)
    grad_logits = ((grad_gate * gate) * (onehot - router_probs)).astype(BF16)
    grad_ref[...] = (grad * keep + cols_by_cols(grad_logits, router_ref[...])).astype(BF16)
    router_grad_ref[...] = rows_by_rows(flat, grad_logits)


def expert_weights_kernel(
    flat_own, flat_other, sent_own, sent_other, hid_own, hid_other, pre_own, pre_other, in_ref, down_ref
):
    in_ref[0] = rows_by_rows(flat_own[...], pre_own[...]) + rows_by_rows(
        flat_other[...], pre_other[...]
    )
    down_ref[0] = rows_by_rows(hid_own[...], sent_own[...]) + rows_by_rows(
        hid_other[...], sent_other[...]
    )


def expert_weights(flat, flat_other, sent, sent_other, hid, hid_other, pre, pre_other, chunk):
    total, width = flat.shape
    hidden = hid.shape[1]
    whole = pl.BlockSpec((total, width), lambda i: (0, 0))
    part = pl.BlockSpec((total, chunk), lambda i: (0, i))
    return pl.pallas_call(
        expert_weights_kernel,
        grid=(hidden // chunk,),
        out_shape=[
            jax.ShapeDtypeStruct((1, width, hidden), F32),
            jax.ShapeDtypeStruct((1, hidden, width), F32),
        ],
        in_specs=[whole] * 4 + [part] * 4,
        out_specs=[
            pl.BlockSpec((1, width, chunk), lambda i: (0, 0, i)),
            pl.BlockSpec((1, chunk, width), lambda i: (0, i, 0)),
        ],
        compiler_params=pltpu.CompilerParams(vmem_limit_bytes=32 * 2**20),
        cost_estimate=pl.CostEstimate(
            flops=8 * total * width * hidden, bytes_accessed=14000000, transcendentals=0
        ),
    )(flat, flat_other, sent, sent_other, hid, hid_other, pre, pre_other)


def middle_kernel(returned_ref, fetch_ref, middle_ref, gain_ref, cot_ref, grad_ref, low_ref, gain_grad_ref):
    grad = dot(fetch_ref[...], returned_ref[...])
    middle = middle_ref[...]
    root = root_mean(middle)
    scaled = middle * root
    gain_grad_ref[...] = jnp.sum(grad * scaled, axis=0, keepdims=True)
    up = gain_ref[...] * grad
    grad_middle = cot_ref[...].astype(F32) + root * (
        up - scaled * jnp.mean(up * scaled, axis=-1, keepdims=True)
    )
    grad_ref[...] = grad_middle
    low_ref[...] = grad_middle.astype(BF16)


def backward_kernel(
    heads,
    grad_own_ref,
    grad_other_ref,
    own_ref,
    other_ref,
    act_ref,
    query_ref,
    key_ref,
    value_ref,
    probs_ref,
    mixed_ref,
    hot_ref,
    wq_ref,
    wk_ref,
    wv_ref,
    wo_ref,
    packed_ref,
    input_own_ref,
    input_other_ref,
    gain_grad_ref,
    table_ref,
    wq_half,
    wk_half,
    wv_half,
    wo_half,
    sems,
):
    rows, width = own_ref.shape
    size = width // heads
    part = width // 2
    scale = 1.0 / math.sqrt(size)
    core = lax.axis_index("ffn")
    span = pl.ds(pl.multiple_of(core * part, LANES), part)
    copies = [
        pltpu.make_async_copy(src, half, sems.at[i])
        for i, (src, half) in enumerate(
            (
                (wo_ref.at[span, :], wo_half),
                (wq_ref.at[:, span], wq_half),
                (wk_ref.at[:, span], wk_half),
                (wv_ref.at[:, span], wv_half),
            )
        )
    ]
    for copy in copies:
        copy.start()
    grad_low = jnp.concatenate([grad_own_ref[...], grad_other_ref[...]], axis=0)
    grad_out = rows_by_rows(mixed_ref[...], grad_low).astype(BF16)
    packed_ref[3 * width : 3 * width + part] = grad_out[:, :part]
    packed_ref[3 * width + part :] = grad_out[:, part:]
    for copy in copies:
        copy.wait()
    grad_mixed = cols_by_cols(grad_low, wo_half[...]).astype(BF16)
    low_half = lax.broadcasted_iota(jnp.int32, (2 * rows, 2 * size), 1) < size
    grad_q, grad_k, grad_v = [], [], []
    same, ahead, behind = [], [], []
    for pair in range(heads // 4):
        lanes = slice(pair * 2 * size, (pair + 1) * 2 * size)
        query, key, value = query_ref[:, lanes], key_ref[:, lanes], value_ref[:, lanes]
        grad_pair = grad_mixed[:, lanes]
        got_q, got_k, got_v = [], [], []
        for side in range(2):
            probs = probs_ref[2 * pair + side]
            keep_lanes = low_half if side == 0 else jnp.logical_not(low_half)
            own_grad = jnp.where(keep_lanes, grad_pair, 0).astype(BF16)
            grad_probs = cols_by_cols(own_grad, value)
            got_v.append(rows_by_rows(probs.astype(BF16), grad_pair))
            inner = jnp.sum(probs * grad_probs, axis=-1, keepdims=True)
            grad_scores = probs * (grad_probs - inner)
            same.append(
                diagonal_sums(grad_scores[:rows, :rows] + grad_scores[rows:, rows:], rows)
            )
            first = diagonal_sums(grad_scores[:rows, rows:], rows)
            second = diagonal_sums(grad_scores[rows:, :rows], rows)
            ahead.append(jnp.where(core == 1, first, second))
            behind.append(jnp.where(core == 1, second, first))
            grad_raw = (grad_scores * scale).astype(BF16)
            got_q.append(dot(grad_raw, key))
            got_k.append(rows_by_rows(grad_raw, query))
        grad_q.append(jnp.where(low_half, got_q[0], got_q[1]).astype(BF16))
        grad_k.append(jnp.where(low_half, got_k[0], got_k[1]).astype(BF16))
        grad_v.append(jnp.where(low_half, got_v[0], got_v[1]).astype(BF16))
    grad_q = jnp.concatenate(grad_q, axis=1)
    grad_k = jnp.concatenate(grad_k, axis=1)
    grad_v = jnp.concatenate(grad_v, axis=1)
    act = act_ref[...]
    packed_ref[:width] = rows_by_rows(act, grad_q).astype(BF16)
    packed_ref[width : 2 * width] = rows_by_rows(act, grad_k).astype(BF16)
    packed_ref[2 * width : 3 * width] = rows_by_rows(act, grad_v).astype(BF16)
    sums = jnp.concatenate(
        [jnp.concatenate(part_sums, axis=0) for part_sums in (same, ahead, behind)], axis=1
    )
    table_ref[...] = lax.dot_general(
        sums,
        hot_ref[...],
        (((1,), (1,)), ((), ())),
        precision=TOP_PRECISION,
        preferred_element_type=F32,
    )
    grad_act = (
        cols_by_cols(grad_q, wq_half[...])
        + cols_by_cols(grad_k, wk_half[...])
        + cols_by_cols(grad_v, wv_half[...])
    )
    x = own_ref[...].astype(F32)
    y = other_ref[...].astype(F32)
    gain_grad_ref[...] = jnp.sum(
        grad_act[:rows] * (x * root_mean(x)) + grad_act[rows:] * (y * root_mean(y)),
        axis=0,
        keepdims=True,
    )
    input_own_ref[...] = grad_act[:rows]
    input_other_ref[...] = grad_act[rows:].astype(BF16)


def swap(x):
    return lax.ppermute(x, "ffn", [(0, 1), (1, 0)])


def flip(x, bit):
    peers = lax.axis_size("expert")
    return lax.ppermute(x, "expert", [(i, i ^ (1 << bit)) for i in range(peers)])


def scatter_sum(x, order):
    mine = lax.axis_index("expert")
    for bit in order:
        half = x.shape[0] // 2
        upper = (mine >> bit) & 1
        send = lax.dynamic_slice_in_dim(x, (1 - upper) * half, half, 0)
        keep = lax.dynamic_slice_in_dim(x, upper * half, half, 0)
        x = (keep.astype(F32) + flip(send, bit).astype(F32)).astype(BF16)
    return x


def gather_back(x, order):
    mine = lax.axis_index("expert")
    for bit in reversed(order):
        upper = (mine >> bit) & 1
        got = flip(x, bit)
        x = jnp.where(upper == 1, jnp.concatenate([got, x]), jnp.concatenate([x, got]))
    return x


def shards(
    tokens,
    norm_first,
    w_query,
    w_key,
    w_value,
    w_out,
    bucket_bias_table,
    norm_second,
    w_router,
    w_in,
    w_down,
    expert_ids,
    cotangent,
):
    rows, width = tokens.shape
    buckets, heads = bucket_bias_table.shape
    pair = lax.axis_size("ffn")
    experts = w_router.shape[1]
    total = 2 * rows
    capacity = 5 * rows * pair // 4
    hidden = w_in.shape[2]
    part = width // 2
    bits = experts.bit_length() - 1
    core = lax.axis_index("ffn")
    gain_first = norm_first.reshape(1, width)
    gain_second = norm_second.reshape(1, width)
    hot = jnp.asarray(bucket_windows(rows, buckets, REACH))

    other = swap(tokens)
    in_own, down_own = w_in[0], w_down[0]
    in_other, down_other = swap(in_own), swap(down_own)
    place, fetch, choose, cot_out, windows = call(
        functools.partial(prepare_kernel, experts),
        [
            ((total, rows), BF16),
            ((rows, total), BF16),
            ((rows, experts), F32),
            ((total, width + LANES), BF16),
            ((heads, 6 * rows), F32),
        ],
        (expert_ids.reshape(1, rows), cotangent, bucket_bias_table, hot),
        flops=100000000,
    )
    back = lax.all_to_all(cot_out, "expert", 0, 0, tiled=True)
    middle, gate, outgoing = call(
        functools.partial(forward_kernel, heads),
        [((rows, width), F32), ((rows, LANES), F32), ((total, width), BF16)],
        (
            tokens,
            other,
            gain_first,
            w_query,
            w_key,
            w_value,
            w_out,
            windows,
            gain_second,
            w_router,
            choose,
            place,
        ),
        flops=3000000000,
    )
    flat = lax.all_to_all(outgoing, "expert", 0, 0, tiled=True)
    act, queries, keys, values, probs, mixed = call(
        functools.partial(halves_kernel, heads),
        [
            ((2 * rows, width), BF16),
            ((2 * rows, part), BF16),
            ((2 * rows, part), BF16),
            ((2 * rows, part), BF16),
            ((heads // 2, 2 * rows, 2 * rows), F32),
            ((2 * rows, part), BF16),
        ],
        (tokens, other, gain_first, w_query, w_key, w_value, windows),
        flops=3000000000,
        anys=(3, 4, 5),
        scratch=[pltpu.VMEM((width, part), BF16)] * 3 + [pltpu.SemaphoreType.DMA((3,))],
    )
    fill_other = swap(back[:, width:])
    chunk = 512
    steps = 2 * hidden // chunk
    hid_own, hid_other, pre_own, pre_other, grad_slots, sent, produced, router_part = call(
        functools.partial(expert_kernel, capacity, chunk),
        [
            ((total, hidden), BF16),
            ((total, hidden), BF16),
            ((total, hidden), BF16),
            ((total, hidden), BF16),
            ((total, width), BF16),
            ((total, width), BF16),
            ((total, width), BF16),
            ((width, experts), F32),
        ],
        (flat, back, fill_other, w_router, in_own, in_other, down_own, down_other),
        flops=6000000000,
        anys=(4, 5, 6, 7),
        scratch=[
            pltpu.VMEM((steps, width, chunk), BF16),
            pltpu.VMEM((steps, chunk, width), BF16),
            pltpu.SemaphoreType.DMA((2, steps)),
        ],
    )
    grad_returned = lax.all_to_all(grad_slots, "expert", 0, 0, tiled=True)
    produced_returned = lax.all_to_all(produced, "expert", 0, 0, tiled=True)
    grad_w_in, grad_w_down = expert_weights(
        flat,
        swap(flat),
        sent,
        swap(sent),
        hid_own,
        swap(hid_other),
        pre_own,
        swap(pre_other),
        256,
    )
    grad_middle, grad_low, gain_second_part = call(
        middle_kernel,
        [((rows, width), F32), ((rows, width), BF16), ((1, width), F32)],
        (grad_returned, fetch, middle, gain_second, cotangent),
        flops=100000000,
    )
    packed, input_own, input_other, gain_first_part, table_part = call(
        functools.partial(backward_kernel, heads),
        [
            ((4 * width, part), BF16),
            ((rows, width), F32),
            ((rows, width), BF16),
            ((1, width), F32),
            ((heads // 2, buckets), F32),
        ],
        (
            grad_low,
            swap(grad_low),
            tokens,
            other,
            act,
            queries,
            keys,
            values,
            probs,
            mixed,
            hot,
            w_query,
            w_key,
            w_value,
            w_out,
        ),
        flops=4000000000,
        anys=(11, 12, 13, 14),
        scratch=[pltpu.VMEM((width, part), BF16)] * 3
        + [pltpu.VMEM((part, width), BF16), pltpu.SemaphoreType.DMA((4,))],
    )
    expert_branch = gate[:, :1] * dot(fetch, produced_returned)
    output = (middle + expert_branch).astype(BF16)
    inputs = tokens.astype(F32)
    root = root_mean(inputs)
    up = norm_first * (input_own + swap(input_other).astype(F32))
    grad_input = grad_middle + root * up - inputs * root**3 * jnp.mean(
        up * inputs, axis=-1, keepdims=True
    )
    table_full = lax.dynamic_update_slice_in_dim(
        jnp.zeros((buckets, heads), F32), table_part.T, core * (heads // 2), 1
    )
    small = jnp.concatenate(
        [
            gain_first_part.reshape(-1),
            gain_second_part.reshape(-1),
            table_full.reshape(-1),
            router_part.reshape(-1),
        ]
    )
    count = small.shape[0]
    small_rows = -(-count // (part * 128)) * 128
    small = jnp.pad(small, (0, small_rows * part - count)).reshape(small_rows, part).astype(BF16)
    third = 4 * width // 3
    orders = [list(range(bits)), [1, 2, 0] + list(range(3, bits)), [2, 0, 1] + list(range(3, bits))]
    pieces = [
        packed[:third],
        packed[third : 2 * third],
        jnp.concatenate([packed[2 * third :], small]),
    ]
    pieces = [scatter_sum(piece, order) for piece, order in zip(pieces, orders)]
    pieces = [gather_back(piece, order) for piece, order in zip(pieces, orders)]
    mine = jnp.concatenate(pieces)
    theirs = swap(mine)
    first = jnp.where(core == 0, mine, theirs)
    second = jnp.where(core == 0, theirs, mine)
    summed = []
    for i in range(3):
        span = slice(i * width, (i + 1) * width)
        summed.append(jnp.concatenate([first[span], second[span]], axis=1).astype(F32))
    blocks = [
        jnp.concatenate(
            [half[3 * width : 3 * width + part], half[3 * width + part : 4 * width]], axis=1
        )
        for half in (first, second)
    ]
    summed.append(jnp.concatenate(blocks, axis=0).astype(F32))
    tail = (first[4 * width :].astype(F32) + second[4 * width :].astype(F32)).reshape(-1)
    ends = np.cumsum([width, width, buckets * heads, width * experts])
    return (
        output,
        grad_input,
        tail[: ends[0]],
        summed[0],
        summed[1],
        summed[2],
        summed[3],
        tail[ends[1] : ends[2]].reshape(buckets, heads),
        tail[ends[0] : ends[1]],
        tail[ends[2] : ends[3]].reshape(width, experts),
        grad_w_in,
        grad_w_down,
        expert_branch,
    )


def solution(mesh):
    placed = (
        P(("expert", "ffn"), None),
        P(),
        P(),
        P(),
        P(),
        P(),
        P(),
        P(),
        P(),
        P("expert", None, "ffn"),
        P("expert", "ffn", None),
        P(("expert", "ffn")),
        P(("expert", "ffn"), None),
    )
    return jax.shard_map(
        shards,
        mesh=mesh,
        in_specs=placed,
        out_specs=(
            P(("expert", "ffn"), None),
            P(("expert", "ffn"), None),
            P(),
            P(),
            P(),
            P(),
            P(),
            P(),
            P(),
            P(),
            P("expert", None, "ffn"),
            P("expert", "ffn", None),
            P(("expert", "ffn"), None),
        ),
        check_vma=False,
    )
```

```python
import functools
import math

import jax
import jax.numpy as jnp
import numpy as np
from jax import lax
from jax.experimental import pallas as pl
from jax.experimental.pallas import tpu as pltpu
from jax.sharding import PartitionSpec as P

REACH = 128
EPS = 1e-06
TOP_PRECISION = lax.Precision.HIGHEST
LANES = 128
F32 = jnp.float32
BF16 = jnp.bfloat16


def bucket_of(distance, buckets, reach):
    half = buckets // 2
    exact = half // 2
    result = np.where(distance < 0, half, 0)
    magnitude = np.abs(distance)
    spread = exact + np.floor(
        np.log(np.maximum(magnitude, 1) / exact) / np.log(reach / exact) * (half - exact)
    )
    spread = np.minimum(spread, half - 1)
    return result + np.where(magnitude < exact, magnitude, spread)


def bucket_windows(rows, buckets, reach):
    lane = np.arange(2 * rows)
    offset = np.where(lane < rows, -lane, 2 * rows - lane)
    windows = []
    for shift in (0, rows, -rows):
        hot = bucket_of(offset + shift, buckets, reach)[None, :] == np.arange(buckets)[:, None]
        hot[:, rows] = False
        windows.append(hot)
    return np.concatenate(windows, axis=1).astype(np.float32)


def rows_by_rows(left, right):
    return lax.dot_general(left, right, (((0,), (0,)), ((), ())), preferred_element_type=F32)


def cols_by_cols(left, right):
    return lax.dot_general(left, right, (((1,), (1,)), ((), ())), preferred_element_type=F32)


def dot(left, right):
    return jnp.dot(left, right, preferred_element_type=F32)


def root_mean(x):
    return lax.rsqrt(jnp.mean(x * x, axis=-1, keepdims=True) + EPS)


def call(body, outs, args, modes, vmem=16, flops=0, scratch=(), aliases=None, nbytes=1000000):
    count, total = len(args), len(args) + len(outs)
    shapes = [(a.shape, a.dtype) for a in args] + list(outs)
    spaces = [pltpu.VMEM if m == "v" else pltpu.HBM for m in modes]
    moved = [i for i in range(total) if modes[i] in "hl"]
    buffers = [pltpu.VMEM(*shapes[i]) for i in moved]

    def kernel(*refs):
        bodies = list(refs[:total])
        for i, ref in zip(moved, refs[total : total + len(moved)]):
            bodies[i] = ref
        extra = refs[total + len(moved) : -1]
        sems = refs[-1]
        copies = {}
        for i in moved:
            ends = (refs[i], bodies[i]) if i < count else (bodies[i], refs[i])
            copies[i] = pltpu.make_async_copy(*ends, sems.at[i])
        for i in moved:
            if i < count:
                copies[i].start()
        flushed = set()

        def wait(i):
            copies[i].wait()

        def flush(i):
            flushed.add(i)
            copies[count + i].start()

        for i in moved:
            if i < count and modes[i] == "h":
                wait(i)
        body(wait, flush, *bodies, *extra)
        for i in moved:
            if i >= count and i - count not in flushed:
                copies[i].start()
        for i in moved:
            if i >= count:
                copies[i].wait()

    specs = [pl.BlockSpec(memory_space=space) for space in spaces]
    return pl.pallas_call(
        kernel,
        out_shape=[jax.ShapeDtypeStruct(s, d) for s, d in outs],
        in_specs=specs[:count],
        out_specs=specs[count:],
        scratch_shapes=buffers + list(scratch) + [pltpu.SemaphoreType.DMA((total,))],
        input_output_aliases=aliases or {},
        compiler_params=pltpu.CompilerParams(vmem_limit_bytes=vmem * 2**20),
        cost_estimate=pl.CostEstimate(flops=flops, bytes_accessed=nbytes, transcendentals=0),
    )(*args)


def toeplitz(window, rows):
    wide = jnp.broadcast_to(window, (rows, 2 * rows))
    return pltpu.roll(wide, 0, 1, stride=1, stride_axis=0)[:, :rows]


def diagonal_sums(square, rows):
    wide = jnp.concatenate([square, jnp.zeros_like(square)], axis=1)
    height = rows
    while height > 1:
        height //= 2
        wide = wide[:height] + pltpu.roll(wide[height:], 2 * rows - height, 1)
    return wide


def placement(ids, experts, total):
    rows = ids.shape[1]
    slots = total // experts
    choose = (lax.broadcasted_iota(jnp.int32, (experts, rows), 0) == ids).astype(F32)
    earlier = (
        lax.broadcasted_iota(jnp.int32, (rows, rows), 0)
        < lax.broadcasted_iota(jnp.int32, (rows, rows), 1)
    ).astype(F32)
    ranks = dot(choose.astype(BF16), earlier.astype(BF16))
    rank = jnp.sum(choose * ranks, axis=0, keepdims=True)
    target = ids * slots + rank.astype(jnp.int32)
    place = (lax.broadcasted_iota(jnp.int32, (total, rows), 0) == target).astype(F32)
    return choose, place


def attend(query_pair, key_pair, scale, bias, side, low_half):
    own = jnp.where(low_half if side == 0 else jnp.logical_not(low_half), query_pair, 0)
    scores = cols_by_cols(own.astype(BF16), key_pair) * scale + bias
    grown = jnp.exp(scores - jnp.max(scores, axis=-1, keepdims=True))
    return grown / jnp.sum(grown, axis=-1, keepdims=True)


def forward_kernel(
    heads,
    wait,
    flush,
    own_ref,
    other_ref,
    gain_first_ref,
    ids_ref,
    ids_other_ref,
    table_ref,
    hot_ref,
    wk,
    wv,
    wq,
    wo,
    gain_second_ref,
    router_ref,
    cot_ref,
    middle_ref,
    gate_ref,
    out_ref,
    mixed_ref,
    win_ref,
    fetch_ref,
    fetch_other_ref,
):
    rows, width = own_ref.shape
    size = width // heads
    scale = 1.0 / math.sqrt(size)
    core = lax.axis_index("ffn")
    total = out_ref.shape[0]
    experts = router_ref.shape[0]
    choose, place = placement(ids_ref[...], experts, total)
    _, place_other = placement(ids_other_ref[...], experts, total)
    fetch_ref[...] = place.T.astype(BF16)
    fetch_other_ref[...] = place_other.T.astype(BF16)
    choose = choose.T
    lane = lax.broadcasted_iota(jnp.int32, (total, LANES), 1)
    out_ref[:, 2 * width :] = jnp.where(
        lane == 0,
        jnp.sum(place, axis=1, keepdims=True),
        jnp.sum(place_other, axis=1, keepdims=True),
    ).astype(BF16)
    place = place.astype(BF16)
    windows = jnp.dot(
        table_ref[...], hot_ref[...], precision=TOP_PRECISION, preferred_element_type=F32
    )
    win_ref[...] = windows
    for i in (4, 5, 6):
        flush(i)
    x = own_ref[...].astype(F32)
    y = other_ref[...].astype(F32)
    gain = gain_first_ref[...].reshape(1, width)
    act_own = (x * root_mean(x) * gain).astype(BF16)
    act_other = (y * root_mean(y) * gain).astype(BF16)
    act = jnp.concatenate([act_own, act_other], axis=0)
    wait(7)
    keys = dot(act, wk[...]).astype(BF16)
    wait(8)
    values = dot(act, wv[...]).astype(BF16)
    wait(9)
    queries = dot(act_own, wq[...]).astype(BF16)
    low_half = lax.broadcasted_iota(jnp.int32, (rows, 2 * size), 1) < size
    same = windows[:, : 2 * rows]
    apart = jnp.where(core == 1, windows[:, 2 * rows : 4 * rows], windows[:, 4 * rows :])
    mixed = []
    for pair in range(heads // 2):
        lanes = slice(pair * 2 * size, (pair + 1) * 2 * size)
        outs = []
        for side in range(2):
            head = 2 * pair + side
            bias = jnp.concatenate(
                [
                    toeplitz(same[head : head + 1], rows),
                    toeplitz(apart[head : head + 1], rows),
                ],
                axis=1,
            )
            probs = attend(queries[:, lanes], keys[:, lanes], scale, bias, side, low_half)
            outs.append(dot(probs.astype(BF16), values[:, lanes]))
        mixed.append(jnp.where(low_half, outs[0], outs[1]).astype(BF16))
    mixed = jnp.concatenate(mixed, axis=1)
    mixed_ref[...] = mixed
    flush(3)
    for i in (10, 11, 12, 13):
        wait(i)
    out_ref[:, width : 2 * width] = dot(place, cot_ref[...]).astype(BF16)
    middle = x + dot(mixed, wo[...])
    middle_ref[...] = middle
    flush(0)
    gain_second = gain_second_ref[...].reshape(1, width)
    act_second = (middle * root_mean(middle) * gain_second).astype(BF16)
    logits = cols_by_cols(act_second, router_ref[...])
    grown = jnp.exp(logits - jnp.max(logits, axis=-1, keepdims=True))
    gate = jnp.sum(grown * choose, axis=-1, keepdims=True) / jnp.sum(
        grown, axis=-1, keepdims=True
    )
    gate_ref[...] = jnp.broadcast_to(gate, gate_ref.shape)
    out_ref[:, :width] = dot(place, act_second).astype(BF16)


def halves_kernel(
    heads,
    wait,
    flush,
    own_ref,
    other_ref,
    gain_first_ref,
    wq_ref,
    wk_ref,
    wv_ref,
    win_ref,
    after_ref,
    act_ref,
    query_ref,
    key_ref,
    value_ref,
    probs_ref,
    wq_half,
    wk_half,
    wv_half,
    sems,
):
    rows, width = own_ref.shape
    size = width // heads
    part = width // 2
    scale = 1.0 / math.sqrt(size)
    core = lax.axis_index("ffn")
    columns = pl.ds(pl.multiple_of(core * part, LANES), part)
    copies = [
        pltpu.make_async_copy(ref.at[:, columns], half, sems.at[i])
        for i, (ref, half) in enumerate(((wq_ref, wq_half), (wk_ref, wk_half), (wv_ref, wv_half)))
    ]
    for copy in copies:
        copy.start()
    x = own_ref[...].astype(F32)
    y = other_ref[...].astype(F32)
    gain = gain_first_ref[...].reshape(1, width)
    act = jnp.concatenate(
        [(x * root_mean(x) * gain).astype(BF16), (y * root_mean(y) * gain).astype(BF16)], axis=0
    )
    act_ref[...] = act
    for copy in copies:
        copy.wait()
    queries = dot(act, wq_half[...]).astype(BF16)
    keys = dot(act, wk_half[...]).astype(BF16)
    values = dot(act, wv_half[...]).astype(BF16)
    query_ref[...] = queries
    key_ref[...] = keys
    value_ref[...] = values
    for i in range(4):
        flush(i)
    low_half = lax.broadcasted_iota(jnp.int32, (2 * rows, 2 * size), 1) < size
    for pair in range(heads // 4):
        lanes = slice(pair * 2 * size, (pair + 1) * 2 * size)
        for side in range(2):
            head = 2 * pair + side
            window = win_ref[pl.ds(core * (heads // 2) + head, 1), :]
            same = toeplitz(window[:, : 2 * rows], rows)
            ahead = toeplitz(window[:, 2 * rows : 4 * rows], rows)
            behind = toeplitz(window[:, 4 * rows :], rows)
            first = jnp.where(core == 1, ahead, behind)
            second = jnp.where(core == 1, behind, ahead)
            bias = jnp.concatenate(
                [
                    jnp.concatenate([same, first], axis=1),
                    jnp.concatenate([second, same], axis=1),
                ],
                axis=0,
            )
            probs_ref[head] = attend(
                queries[:, lanes], keys[:, lanes], scale, bias, side, low_half
            )


def expert_kernel(
    capacity,
    chunk,
    wait,
    flush,
    arrived_ref,
    router_ref,
    in_own_ref,
    in_other_ref,
    down_own_ref,
    down_other_ref,
    after_ref,
    hid_own_ref,
    pre_own_ref,
    sent_ref,
    bundle_ref,
    grad_ref,
    produced_ref,
    router_grad_ref,
    in_vmem,
    down_vmem,
    sems,
):
    total = arrived_ref.shape[0]
    experts, width = router_ref.shape
    slots = total // experts
    hidden = in_own_ref.shape[1]
    steps = hidden // chunk
    mine = lax.axis_index("expert")
    core = lax.axis_index("ffn")
    copies = []
    for side, (win, wdown) in enumerate(
        ((in_own_ref, down_own_ref), (in_other_ref, down_other_ref))
    ):
        for step in range(steps):
            i = side * steps + step
            span = pl.ds(step * chunk, chunk)
            copies.append(
                (
                    pltpu.make_async_copy(win.at[:, span], in_vmem.at[i], sems.at[0, i]),
                    pltpu.make_async_copy(wdown.at[span, :], down_vmem.at[i], sems.at[1, i]),
                )
            )
    for pair in copies:
        for copy in pair:
            copy.start()
    flat = arrived_ref[:, :width]
    cot = arrived_ref[:, width : 2 * width]
    filled = arrived_ref[:, 2 * width :]
    row = lax.broadcasted_iota(jnp.int32, (total, total), 0)
    col = lax.broadcasted_iota(jnp.int32, (total, total), 1)
    shift = slots.bit_length() - 1
    row_block = jnp.right_shift(row, shift)
    col_block = jnp.right_shift(col, shift)
    before = (col_block < row_block).astype(F32).astype(BF16)
    ahead = (col_block < row_block + core).astype(F32).astype(BF16)
    slot = jnp.bitwise_and(lax.broadcasted_iota(jnp.int32, (total, 1), 0), slots - 1)
    position = dot(before, filled)[:, 0:1] + dot(ahead, filled)[:, 1:2] + slot.astype(F32)
    keep = jnp.where(position < capacity, 1.0, 0.0)
    logits = cols_by_cols(flat, router_ref[...])
    grown = jnp.exp(logits - jnp.max(logits, axis=-1, keepdims=True))
    router_probs = grown / jnp.sum(grown, axis=-1, keepdims=True)
    onehot = (lax.broadcasted_iota(jnp.int32, (total, experts), 1) == mine).astype(F32)
    gate = jnp.sum(router_probs * onehot, axis=-1, keepdims=True)
    sent = (cot.astype(F32) * (gate * keep)).astype(BF16)
    sent_ref[...] = sent
    bundle_ref[:, :width] = flat
    bundle_ref[:, width : 2 * width] = sent
    produced = jnp.zeros((total, width), F32)
    grad = jnp.zeros((total, width), F32)
    inner = math.sqrt(2.0 / math.pi)
    for i, pair in enumerate(copies):
        own_side = i < steps
        first = (i % steps) * chunk
        for copy in pair:
            copy.wait()
        win, wdown = in_vmem[i], down_vmem[i]
        pre = dot(flat, win)
        square = pre * pre
        curve = jnp.tanh(inner * pre * (1.0 + 0.044715 * square))
        half_up = 0.5 + 0.5 * curve
        act = (pre * half_up).astype(BF16)
        slope = half_up + (0.5 * inner) * pre * (1.0 - curve * curve) * (
            1.0 + (3 * 0.044715) * square
        )
        grad_pre = (slope * cols_by_cols(sent, wdown)).astype(BF16)
        if own_side:
            hid_own_ref[:, first : first + chunk] = act
            pre_own_ref[:, first : first + chunk] = grad_pre
        else:
            first += 2 * width
            bundle_ref[:, first : first + chunk] = act
            bundle_ref[:, first + hidden : first + hidden + chunk] = grad_pre
        produced = produced + dot(act, wdown)
        grad = grad + cols_by_cols(grad_pre, win)
    for i in range(4):
        flush(i)
    produced_low = produced.astype(BF16)
    kept = produced_low.astype(F32) * keep
    produced_ref[...] = kept.astype(BF16)
    grad_gate = jnp.sum(cot.astype(F32) * kept, axis=-1, keepdims=True)
    grad_logits = ((grad_gate * gate) * (onehot - router_probs)).astype(BF16)
    grad_ref[...] = (grad * keep + dot(grad_logits, router_ref[...])).astype(BF16)
    router_grad_ref[...] = rows_by_rows(grad_logits, flat)


def expert_weights_kernel(
    flat_own, sent_own, hid_own, pre_own, flat_other, sent_other, hid_other, pre_other, in_ref, down_ref
):
    in_ref[0] = rows_by_rows(flat_own[...], pre_own[...]) + rows_by_rows(
        flat_other[...], pre_other[...]
    )
    down_ref[0] = rows_by_rows(hid_own[...], sent_own[...]) + rows_by_rows(
        hid_other[...], sent_other[...]
    )


def expert_weights(flat, sent, hid, pre, bundle, chunk):
    total, width = sent.shape
    hidden = hid.shape[1]
    steps = hidden // chunk
    skip = 2 * width // chunk
    whole = pl.BlockSpec((total, width), lambda i: (0, 0))
    second = pl.BlockSpec((total, width), lambda i: (0, 1))
    part = pl.BlockSpec((total, chunk), lambda i: (0, i))
    return pl.pallas_call(
        expert_weights_kernel,
        grid=(steps,),
        out_shape=[
            jax.ShapeDtypeStruct((1, width, hidden), F32),
            jax.ShapeDtypeStruct((1, hidden, width), F32),
        ],
        in_specs=[
            whole,
            whole,
            part,
            part,
            whole,
            second,
            pl.BlockSpec((total, chunk), lambda i: (0, i + skip)),
            pl.BlockSpec((total, chunk), lambda i: (0, i + skip + steps)),
        ],
        out_specs=[
            pl.BlockSpec((1, width, chunk), lambda i: (0, 0, i)),
            pl.BlockSpec((1, chunk, width), lambda i: (0, i, 0)),
        ],
        compiler_params=pltpu.CompilerParams(vmem_limit_bytes=64 * 2**20),
        cost_estimate=pl.CostEstimate(
            flops=8 * total * width * hidden, bytes_accessed=14000000, transcendentals=0
        ),
    )(flat, sent, hid, pre, bundle, bundle, bundle, bundle)


def middle_back(returned, fetch, middle, gain, cot):
    grad = dot(fetch, returned)
    root = root_mean(middle)
    scaled = middle * root
    up = gain * grad
    grad_middle = cot.astype(F32) + root * (
        up - scaled * jnp.mean(up * scaled, axis=-1, keepdims=True)
    )
    return grad_middle, grad * scaled


def place_of(target, order):
    relative = jnp.bitwise_xor(target, lax.axis_index("expert"))
    place = 0
    for bit in order:
        place = place * 2 + jnp.bitwise_and(jnp.right_shift(relative, bit), 1)
    return place


def chunk_place(chunk, order, levels):
    target = sum((((chunk >> (levels - 1 - k)) & 1) << bit) for k, bit in enumerate(order[:levels]))
    return place_of(target, order[:levels])


def small_rows(experts):
    return [0, 2, 4, 16, 16 + experts, 16 + 2 * experts]


def small_height(experts, levels):
    return -(-(16 + 2 * experts) // (16 << levels)) * 16


def backward_kernel(
    heads,
    orders,
    levels,
    wait,
    flush,
    returned_ref,
    returned_other_ref,
    fetch_ref,
    fetch_other_ref,
    middle_ref,
    middle_other_ref,
    cot_ref,
    cot_other_ref,
    gain_second_ref,
    own_ref,
    other_ref,
    act_ref,
    query_ref,
    key_ref,
    value_ref,
    probs_ref,
    mixed_own_ref,
    mixed_other_ref,
    hot_ref,
    router_ref,
    after_ref,
    wq_ref,
    wk_ref,
    wv_ref,
    wo_ref,
    keep_0_ref,
    send_0_ref,
    keep_1_ref,
    send_1_ref,
    keep_2_ref,
    send_2_ref,
    input_own_ref,
    input_other_ref,
    grad_middle_ref,
    wq_half,
    wk_half,
    wv_half,
    wo_half,
    part_0,
    part_1,
    part_2,
    natural,
    sems,
):
    rows, width = own_ref.shape
    size = width // heads
    part = width // 2
    experts = router_ref.shape[0]
    scale = 1.0 / math.sqrt(size)
    core = lax.axis_index("ffn")
    span = pl.ds(pl.multiple_of(core * part, LANES), part)
    copies = [
        pltpu.make_async_copy(src, half, sems.at[i])
        for i, (src, half) in enumerate(
            (
                (wo_ref.at[span, :], wo_half),
                (wq_ref.at[:, span], wq_half),
                (wk_ref.at[:, span], wk_half),
                (wv_ref.at[:, span], wv_half),
            )
        )
    ]
    for copy in copies:
        copy.start()
    parts = (part_0, part_1, part_2)
    halves = ((keep_0_ref, send_0_ref), (keep_1_ref, send_1_ref), (keep_2_ref, send_2_ref))
    third = width // 3
    height = third >> levels
    writes = []
    for p, pair in enumerate(halves):
        rows_half = pair[0].shape[0]
        for i, ref in enumerate(pair):
            writes.append(
                pltpu.make_async_copy(
                    parts[p].at[pl.ds(i * rows_half, rows_half), :], ref, sems.at[4 + 2 * p + i]
                )
            )

    def pack(matrix, value):
        for p, ref in enumerate(parts):
            for chunk in range(2**levels):
                place = chunk_place(chunk, orders[p], levels)
                first = p * third + chunk * height
                step = ref.shape[0] >> levels
                at = pl.multiple_of(place * step + matrix * height, 16)
                ref[pl.ds(at, height), :] = value[first : first + height]

    gain = gain_second_ref[...].reshape(1, width)
    grad_own, gain_terms = middle_back(
        returned_ref[...], fetch_ref[...], middle_ref[...], gain, cot_ref[...]
    )
    grad_other, _ = middle_back(
        returned_other_ref[...], fetch_other_ref[...], middle_other_ref[...], gain, cot_other_ref[...]
    )
    gain_second = jnp.sum(gain_terms, axis=0, keepdims=True)
    grad_middle_ref[...] = grad_own
    flush(8)
    grad_low = jnp.concatenate([grad_own, grad_other], axis=0).astype(BF16)
    mixed = jnp.concatenate([mixed_own_ref[...], mixed_other_ref[...]], axis=0)
    grad_columns = jnp.where(core == 0, grad_low[:, :part], grad_low[:, part:])
    pack(3, rows_by_rows(mixed, grad_columns).astype(BF16))
    copies[0].wait()
    grad_mixed = cols_by_cols(grad_low, wo_half[...]).astype(BF16)
    low_half = lax.broadcasted_iota(jnp.int32, (2 * rows, 2 * size), 1) < size
    grad_q, grad_k, grad_v = [], [], []
    same, ahead, behind = [], [], []
    for pair in range(heads // 4):
        lanes = slice(pair * 2 * size, (pair + 1) * 2 * size)
        query, key, value = query_ref[:, lanes], key_ref[:, lanes], value_ref[:, lanes]
        grad_pair = grad_mixed[:, lanes]
        got_q, got_k, got_v = [], [], []
        for side in range(2):
            probs = probs_ref[2 * pair + side]
            keep_lanes = low_half if side == 0 else jnp.logical_not(low_half)
            own_grad = jnp.where(keep_lanes, grad_pair, 0).astype(BF16)
            grad_probs = cols_by_cols(own_grad, value)
            got_v.append(rows_by_rows(probs.astype(BF16), grad_pair))
            inner = jnp.sum(probs * grad_probs, axis=-1, keepdims=True)
            grad_scores = probs * (grad_probs - inner)
            same.append(
                diagonal_sums(grad_scores[:rows, :rows] + grad_scores[rows:, rows:], rows)
            )
            first = diagonal_sums(grad_scores[:rows, rows:], rows)
            second = diagonal_sums(grad_scores[rows:, :rows], rows)
            ahead.append(jnp.where(core == 1, first, second))
            behind.append(jnp.where(core == 1, second, first))
            grad_raw = (grad_scores * scale).astype(BF16)
            got_q.append(dot(grad_raw, key))
            got_k.append(rows_by_rows(grad_raw, query))
        grad_q.append(jnp.where(low_half, got_q[0], got_q[1]).astype(BF16))
        grad_k.append(jnp.where(low_half, got_k[0], got_k[1]).astype(BF16))
        grad_v.append(jnp.where(low_half, got_v[0], got_v[1]).astype(BF16))
    grad_q = jnp.concatenate(grad_q, axis=1)
    grad_k = jnp.concatenate(grad_k, axis=1)
    grad_v = jnp.concatenate(grad_v, axis=1)
    act = act_ref[...]
    pack(0, rows_by_rows(act, grad_q).astype(BF16))
    pack(1, rows_by_rows(act, grad_k).astype(BF16))
    pack(2, rows_by_rows(act, grad_v).astype(BF16))
    for write in writes[:4]:
        write.start()
    sums = jnp.concatenate(
        [jnp.concatenate(part_sums, axis=0) for part_sums in (same, ahead, behind)], axis=1
    )
    table = lax.dot_general(
        sums,
        hot_ref[...],
        (((1,), (1,)), ((), ())),
        precision=TOP_PRECISION,
        preferred_element_type=F32,
    )
    for copy in copies[1:]:
        copy.wait()
    grad_act = (
        cols_by_cols(grad_q, wq_half[...])
        + cols_by_cols(grad_k, wk_half[...])
        + cols_by_cols(grad_v, wv_half[...])
    )
    x = own_ref[...].astype(F32)
    y = other_ref[...].astype(F32)
    gain_first = jnp.sum(
        grad_act[:rows] * (x * root_mean(x)) + grad_act[rows:] * (y * root_mean(y)),
        axis=0,
        keepdims=True,
    )
    input_own_ref[...] = grad_act[:rows]
    input_other_ref[...] = grad_act[rows:].astype(BF16)
    at = small_rows(experts)
    natural[...] = jnp.zeros_like(natural)
    for i, value in enumerate((gain_first, gain_second)):
        natural[at[i] : at[i] + 1] = value[:, :part]
        natural[at[i] + 1 : at[i] + 2] = value[:, part:]
    natural[at[2] : at[2] + heads // 2, : table.shape[1]] = table
    natural[at[3] : at[4]] = router_ref[:, :part]
    natural[at[4] : at[5]] = router_ref[:, part:]
    step = part_2.shape[0] >> levels
    extra = step - 4 * height
    for chunk in range(2**levels):
        place = chunk_place(chunk, orders[2], levels)
        at = pl.multiple_of(place * step + 4 * height, 16)
        part_2[pl.ds(at, extra), :] = natural[chunk * extra : (chunk + 1) * extra].astype(BF16)
    for write in writes[4:]:
        write.start()
    for write in writes:
        write.wait()


def assemble_kernel(orders, levels, chosen, upper, last, wait, flush, *refs):
    arrays, refs = refs[: 2 * len(chosen)], refs[2 * len(chosen) :]
    if last is not None:
        experts, heads = last
        near_refs, refs = refs[:2], refs[2:]
    if upper:
        refs = refs[4:]
    outs, (wide, sems) = refs[:4], refs[-2:]
    if last is not None:
        gain_first_ref, gain_second_ref, table_ref, router_ref = refs[4:8]
    width = outs[0].shape[1]
    part = width // 2
    third = width // 3
    side = third // 2
    height = third >> levels
    half = 2 ** (levels - 1)
    core = lax.axis_index("ffn")
    mine = lax.axis_index("expert")
    own = pl.ds(pl.multiple_of(core * part, LANES), part)
    theirs = pl.ds(pl.multiple_of((1 - core) * part, LANES), part)
    writes = []
    for n, p in enumerate(chosen):
        order = orders[p]
        for i in (2 * n, 2 * n + 1):
            wait(i)
        for low in range(half):
            place = chunk_place(low, order, levels)
            place = jnp.bitwise_and(place, half - 1)
            step = arrays[2 * n].shape[0] // half
            for matrix in range(4):
                at = pl.ds(pl.multiple_of(place * step + matrix * height, 16), height)
                to = pl.ds(low * height, height)
                wide[n, matrix, to, own] = arrays[2 * n][at, :].astype(F32)
                wide[n, matrix, to, theirs] = arrays[2 * n + 1][at, :].astype(F32)
        bit = jnp.bitwise_and(jnp.right_shift(mine, order[0]), 1)
        if upper:
            bit = 1 - bit
        first = pl.multiple_of(p * third + bit * side, side)
        for matrix in range(4):
            write = pltpu.make_async_copy(
                wide.at[n, matrix], outs[matrix].at[pl.ds(first, side), :], sems.at[4 * n + matrix]
            )
            write.start()
            writes.append(write)
    if last is not None:
        at = small_rows(experts)
        extra = small_height(experts, levels)
        step = arrays[-1].shape[0] // half
        found = []
        for chunk in range(-(-at[5] // extra)):
            place = chunk_place(chunk, orders[2], levels)
            away = place >= half
            first = jnp.bitwise_and(place, half - 1) * step + 4 * height
            rows = pl.ds(pl.multiple_of(first, 16), extra)
            found.append(
                [
                    jnp.where(away, arrays[i - 2][rows, :].astype(F32), near_refs[i][rows, :].astype(F32))
                    for i in range(2)
                ]
            )
        mine = jnp.concatenate([a for a, _ in found], axis=0)
        other = jnp.concatenate([b for _, b in found], axis=0)
        both = mine + other
        gain_first_ref[...] = jnp.concatenate([both[0:1], both[1:2]], axis=1).reshape(width)
        gain_second_ref[...] = jnp.concatenate([both[2:3], both[3:4]], axis=1).reshape(width)
        buckets = table_ref.shape[1]
        low = mine[at[2] : at[2] + heads // 2, :buckets]
        high = other[at[2] : at[2] + heads // 2, :buckets]
        table_ref[...] = jnp.where(
            core == 0,
            jnp.concatenate([low, high], axis=0),
            jnp.concatenate([high, low], axis=0),
        )
        router_ref[...] = jnp.concatenate([both[at[3] : at[4]], both[at[4] : at[5]]], axis=1)
    for write in writes:
        write.wait()


def assemble(orders, levels, chosen, arrays, width, earlier=(), near=(), last=None):
    tail = []
    modes = "l" * len(arrays)
    if last is not None:
        experts, heads, buckets = last
        tail = [((width,), F32), ((width,), F32), ((heads, buckets), F32), ((experts, width), F32)]
        modes += "hh"
        last = (experts, heads)
    first = len(modes)
    modes += "r" * len(earlier)
    return call(
        functools.partial(assemble_kernel, orders, levels, chosen, bool(earlier), last),
        [((width, width), F32)] * 4 + tail,
        (*arrays, *near, *earlier),
        modes + "rrrr" + "h" * len(tail),
        vmem=64,
        aliases={first + i: i for i in range(len(earlier))},
        scratch=[
            pltpu.VMEM((len(chosen), 4, width // 6, width), F32),
            pltpu.SemaphoreType.DMA((4 * len(chosen),)),
        ],
        nbytes=8000000,
    )


def swap(x):
    return lax.ppermute(x, "ffn", [(0, 1), (1, 0)])


def flip(x, bit):
    peers = lax.axis_size("expert")
    return lax.ppermute(x, "expert", [(i, i ^ (1 << bit)) for i in range(peers)])


def add_low(left, right):
    return (left.astype(F32) + right.astype(F32)).astype(BF16)


def scatter_sum(keep, send, order, levels):
    for k, bit in enumerate(order):
        got = flip(send, bit)
        half = keep.shape[0] // 2
        if k + 2 == len(order):
            both = add_low(keep, got)
            send = both
            if k + 1 < levels:
                send = jnp.concatenate([both[half:], both[:half]])
            return add_low(both, flip(send, order[-1]))
        if k + 1 < levels:
            keep, send = add_low(keep[:half], got[:half]), add_low(keep[half:], got[half:])
        else:
            both = add_low(keep, got)
            upper = (lax.axis_index("expert") >> order[k + 1]) & 1
            keep = lax.dynamic_slice_in_dim(both, upper * half, half, 0)
            send = lax.dynamic_slice_in_dim(both, (1 - upper) * half, half, 0)


def gather_back(x, order, levels):
    for k, bit in reversed(list(enumerate(order[:-1]))):
        got = flip(x, bit)
        if k == 0:
            return x, got
        if k < levels:
            x = jnp.concatenate([x, got])
        else:
            upper = (lax.axis_index("expert") >> bit) & 1
            x = jnp.where(upper == 1, jnp.concatenate([got, x]), jnp.concatenate([x, got]))


def shards(
    tokens,
    norm_first,
    w_query,
    w_key,
    w_value,
    w_out,
    bucket_bias_table,
    norm_second,
    w_router,
    w_in,
    w_down,
    expert_ids,
    cotangent,
):
    rows, width = tokens.shape
    buckets, heads = bucket_bias_table.shape
    pair = lax.axis_size("ffn")
    experts = w_router.shape[1]
    total = 2 * rows
    capacity = 5 * rows * pair // 4
    hidden = w_in.shape[2]
    part = width // 2
    hot = jnp.asarray(bucket_windows(rows, buckets, REACH))
    router = w_router.T

    other = swap(tokens)
    ids = expert_ids.reshape(1, rows)
    ids_other = swap(ids)
    other, ids_other, w_in, w_down, cotangent = lax.optimization_barrier(
        (other, ids_other, w_in, w_down, cotangent)
    )
    in_own, down_own = w_in[0], w_down[0]
    in_other, down_other = swap(in_own), swap(down_own)
    cot_other = swap(cotangent)
    middle, gate, outgoing, mixed, windows, fetch, fetch_other = call(
        functools.partial(forward_kernel, heads),
        [
            ((rows, width), F32),
            ((rows, LANES), F32),
            ((total, 2 * width + LANES), BF16),
            ((rows, width), BF16),
            ((heads, 6 * rows), F32),
            ((rows, total), BF16),
            ((rows, total), BF16),
        ],
        (
            tokens,
            other,
            norm_first,
            ids,
            ids_other,
            bucket_bias_table.T,
            hot,
            w_key,
            w_value,
            w_query,
            w_out,
            norm_second,
            router,
            cotangent,
        ),
        "hhhhhhhlllllll" + "hhhhhhh",
        vmem=64,
        flops=3000000000,
    )
    arrived = lax.all_to_all(outgoing, "expert", 0, 0, tiled=True)
    mixed_other, middle_other = swap(mixed), swap(middle)
    act, queries, keys, values, probs = call(
        functools.partial(halves_kernel, heads),
        [
            ((2 * rows, width), BF16),
            ((2 * rows, part), BF16),
            ((2 * rows, part), BF16),
            ((2 * rows, part), BF16),
            ((heads // 2, 2 * rows, 2 * rows), F32),
        ],
        (tokens, other, norm_first, w_query, w_key, w_value, windows, gate),
        "hhhrrrhr" + "hhhhh",
        vmem=64,
        flops=3000000000,
        scratch=[pltpu.VMEM((width, part), BF16)] * 3 + [pltpu.SemaphoreType.DMA((3,))],
    )
    chunk = 512
    steps = 2 * hidden // chunk
    hid_own, pre_own, sent, bundle, grad_slots, produced, router_part = call(
        functools.partial(expert_kernel, capacity, chunk),
        [
            ((total, hidden), BF16),
            ((total, hidden), BF16),
            ((total, width), BF16),
            ((total, 2 * width + 2 * hidden), BF16),
            ((total, width), BF16),
            ((total, width), BF16),
            ((experts, width), F32),
        ],
        (arrived, router, in_own, in_other, down_own, down_other, act),
        "hhrrrrr" + "hhhhhhh",
        vmem=64,
        flops=6000000000,
        scratch=[
            pltpu.VMEM((steps, width, chunk), BF16),
            pltpu.VMEM((steps, chunk, width), BF16),
            pltpu.SemaphoreType.DMA((2, steps)),
        ],
    )
    bundle_other = swap(bundle)
    grad_returned = lax.all_to_all(grad_slots, "expert", 0, 0, tiled=True)
    grad_w_in, grad_w_down = expert_weights(arrived, sent, hid_own, pre_own, bundle_other, 256)
    produced, grad_returned, grad_w_in = lax.optimization_barrier(
        (produced, grad_returned, grad_w_in)
    )
    produced_returned = lax.all_to_all(produced, "expert", 0, 0, tiled=True)
    bits = experts.bit_length() - 1
    levels = min(bits, 4)
    rest = list(range(3, bits))
    orders = [[0, 1, 2] + rest, [1, 2, 0] + rest, [2, 0, 1] + rest]
    third = 4 * width // 3
    extra = small_height(experts, levels) << levels
    heights = [third, third, third + extra]
    *halves, input_own, input_other, grad_middle = call(
        functools.partial(backward_kernel, heads, orders, levels),
        [((height // 2, part), BF16) for height in heights for _ in range(2)]
        + [((rows, width), F32), ((rows, width), BF16), ((rows, width), F32)],
        (
            grad_returned,
            swap(grad_returned),
            fetch,
            fetch_other,
            middle,
            middle_other,
            cotangent,
            cot_other,
            norm_second,
            tokens,
            other,
            act,
            queries,
            keys,
            values,
            probs,
            mixed,
            mixed_other,
            hot,
            router_part,
            grad_w_in,
            w_query,
            w_key,
            w_value,
            w_out,
        ),
        "hhhhhhhhh" + "hhhhhhhhhhh" + "rrrrr" + "rrrrrrhhh",
        vmem=64,
        flops=4000000000,
        scratch=[pltpu.VMEM((width, part), BF16)] * 3
        + [
            pltpu.VMEM((part, width), BF16),
            *[pltpu.VMEM((height, part), BF16) for height in heights],
            pltpu.VMEM((extra, part), F32),
            pltpu.SemaphoreType.DMA((10,)),
        ],
    )
    halves, input_own, input_other, grad_middle, produced_returned = lax.optimization_barrier(
        (halves, input_own, input_other, grad_middle, produced_returned)
    )
    scattered = [
        scatter_sum(halves[2 * p], halves[2 * p + 1], order, levels)
        for p, order in enumerate(orders)
    ]
    inputs = tokens.astype(F32)
    root = root_mean(inputs)
    up = norm_first * (input_own + swap(input_other).astype(F32))
    grad_input = grad_middle + root * up - inputs * root**3 * jnp.mean(
        up * inputs, axis=-1, keepdims=True
    )
    expert_branch = gate[:, :1] * dot(fetch, produced_returned)
    output = (middle + expert_branch).astype(BF16)
    gathered = [gather_back(piece, order, levels) for piece, order in zip(scattered, orders)]
    near = []
    for kept, _ in gathered:
        near += [kept, swap(kept)]
    matrices = assemble(orders, levels, (0, 1, 2), near, width)
    got = [pair[1] for pair in gathered]
    got, matrices, output, expert_branch, grad_input = lax.optimization_barrier(
        (got, matrices, output, expert_branch, grad_input)
    )
    far = []
    for rows_got in got:
        far += [rows_got, swap(rows_got)]
    results = assemble(
        orders,
        levels,
        (0, 1, 2),
        far,
        width,
        matrices,
        near[4:],
        (experts, heads, buckets),
    )
    return (
        output,
        grad_input,
        results[4],
        results[0],
        results[1],
        results[2],
        results[3],
        results[6].T,
        results[5],
        results[7].T,
        grad_w_in,
        grad_w_down,
        expert_branch,
    )


def solution(mesh):
    placed = (
        P(("expert", "ffn"), None),
        P(),
        P(),
        P(),
        P(),
        P(),
        P(),
        P(),
        P(),
        P("expert", None, "ffn"),
        P("expert", "ffn", None),
        P(("expert", "ffn")),
        P(("expert", "ffn"), None),
    )
    return jax.shard_map(
        shards,
        mesh=mesh,
        in_specs=placed,
        out_specs=(
            P(("expert", "ffn"), None),
            P(("expert", "ffn"), None),
            P(),
            P(),
            P(),
            P(),
            P(),
            P(),
            P(),
            P(),
            P("expert", None, "ffn"),
            P("expert", "ffn", None),
            P(("expert", "ffn"), None),
        ),
        check_vma=False,
    )
```

```python
import functools
import math

import jax
import jax.numpy as jnp
import numpy as np
from jax import lax
from jax.experimental import pallas as pl
from jax.experimental.pallas import tpu as pltpu
from jax.sharding import PartitionSpec as P

REACH = 128
EPS = 1e-06
TOP_PRECISION = lax.Precision.HIGHEST
LANES = 128
F32 = jnp.float32
BF16 = jnp.bfloat16


def bucket_of(distance, buckets, reach):
    half = buckets // 2
    exact = half // 2
    result = np.where(distance < 0, half, 0)
    magnitude = np.abs(distance)
    spread = exact + np.floor(
        np.log(np.maximum(magnitude, 1) / exact) / np.log(reach / exact) * (half - exact)
    )
    spread = np.minimum(spread, half - 1)
    return result + np.where(magnitude < exact, magnitude, spread)


def bucket_windows(rows, buckets, reach):
    lane = np.arange(2 * rows)
    offset = np.where(lane < rows, -lane, 2 * rows - lane)
    windows = []
    for shift in (0, rows, -rows):
        hot = bucket_of(offset + shift, buckets, reach)[None, :] == np.arange(buckets)[:, None]
        hot[:, rows] = False
        windows.append(hot)
    return np.concatenate(windows, axis=1).astype(np.float32)


def rows_by_rows(left, right):
    return lax.dot_general(left, right, (((0,), (0,)), ((), ())), preferred_element_type=F32)


def cols_by_cols(left, right):
    return lax.dot_general(left, right, (((1,), (1,)), ((), ())), preferred_element_type=F32)


def dot(left, right):
    return jnp.dot(left, right, preferred_element_type=F32)


def root_mean(x):
    return lax.rsqrt(jnp.mean(x * x, axis=-1, keepdims=True) + EPS)


def call(body, outs, args, modes, vmem=16, flops=0, scratch=(), aliases=None, nbytes=1000000):
    count, total = len(args), len(args) + len(outs)
    shapes = [(a.shape, a.dtype) for a in args] + list(outs)
    moved = [i for i in range(total) if modes[i] in "hls"]
    buffers = [pltpu.VMEM(*shapes[i]) for i in moved]

    def kernel(*refs):
        bodies = list(refs[:total])
        for i, ref in zip(moved, refs[total : total + len(moved)]):
            bodies[i] = ref
        extra = refs[total + len(moved) : -1]
        sems = refs[-1]
        copies = {}
        for i in moved:
            ends = (refs[i], bodies[i]) if i < count else (bodies[i], refs[i])
            copies[i] = pltpu.make_async_copy(*ends, sems.at[i])
        for i in moved:
            if i < count and modes[i] != "s":
                copies[i].start()
        flushed = set()

        def wait(i):
            copies[i].wait()

        wait.start = lambda i: copies[i].start()

        def flush(i):
            flushed.add(i)
            copies[count + i].start()

        for i in moved:
            if i < count and modes[i] == "h":
                wait(i)
        body(wait, flush, *bodies, *extra)
        for i in moved:
            if i >= count and i - count not in flushed:
                copies[i].start()
        for i in moved:
            if i >= count:
                copies[i].wait()

    specs = [pl.BlockSpec(memory_space=pltpu.HBM)] * total
    return pl.pallas_call(
        kernel,
        out_shape=[jax.ShapeDtypeStruct(s, d) for s, d in outs],
        in_specs=specs[:count],
        out_specs=specs[count:],
        scratch_shapes=buffers + list(scratch) + [pltpu.SemaphoreType.DMA((total,))],
        input_output_aliases=aliases or {},
        compiler_params=pltpu.CompilerParams(vmem_limit_bytes=vmem * 2**20),
        cost_estimate=pl.CostEstimate(flops=flops, bytes_accessed=nbytes, transcendentals=0),
    )(*args)


def toeplitz(window, rows):
    wide = jnp.broadcast_to(window, (rows, 2 * rows))
    return pltpu.roll(wide, 0, 1, stride=1, stride_axis=0)[:, :rows]


def diagonal_sums(square, rows):
    wide = jnp.concatenate([square, jnp.zeros_like(square)], axis=1)
    height = rows
    while height > 1:
        height //= 2
        wide = wide[:height] + pltpu.roll(wide[height:], 2 * rows - height, 1)
    return wide


def placement(ids, experts, total):
    rows = ids.shape[1]
    slots = total // experts
    choose = (lax.broadcasted_iota(jnp.int32, (experts, rows), 0) == ids).astype(F32)
    earlier = (
        lax.broadcasted_iota(jnp.int32, (rows, rows), 0)
        < lax.broadcasted_iota(jnp.int32, (rows, rows), 1)
    ).astype(F32)
    ranks = dot(choose.astype(BF16), earlier.astype(BF16))
    rank = jnp.sum(choose * ranks, axis=0, keepdims=True)
    target = ids * slots + rank.astype(jnp.int32)
    place = (lax.broadcasted_iota(jnp.int32, (total, rows), 0) == target).astype(F32)
    return choose, place


def attend(query_pair, key_pair, scale, bias, side, low_half):
    own = jnp.where(low_half if side == 0 else jnp.logical_not(low_half), query_pair, 0)
    scores = cols_by_cols(own.astype(BF16), key_pair) * scale + bias
    grown = jnp.exp(scores - jnp.max(scores, axis=-1, keepdims=True))
    return grown * (1.0 / jnp.sum(grown, axis=-1, keepdims=True))


def forward_kernel(
    heads,
    wait,
    flush,
    own_ref,
    other_ref,
    gain_first_ref,
    ids_ref,
    ids_other_ref,
    table_ref,
    hot_ref,
    wk,
    wv,
    wq,
    wo,
    gain_second_ref,
    router_ref,
    cot_ref,
    middle_ref,
    gate_ref,
    out_ref,
    mixed_ref,
    win_ref,
    fetch_ref,
    fetch_other_ref,
    root_ref,
    bias,
):
    rows, width = own_ref.shape
    size = width // heads
    scale = 1.0 / math.sqrt(size)
    core = lax.axis_index("ffn")
    total = out_ref.shape[0]
    experts = router_ref.shape[0]
    choose, place = placement(ids_ref[...], experts, total)
    _, place_other = placement(ids_other_ref[...], experts, total)
    fetch_ref[...] = place.T.astype(BF16)
    fetch_other_ref[...] = place_other.T.astype(BF16)
    choose = choose.T
    lane = lax.broadcasted_iota(jnp.int32, (total, LANES), 1)
    out_ref[:, 2 * width :] = jnp.where(
        lane == 0,
        jnp.sum(place, axis=1, keepdims=True),
        jnp.sum(place_other, axis=1, keepdims=True),
    ).astype(BF16)
    place = place.astype(BF16)
    windows = jnp.dot(
        table_ref[...], hot_ref[...], precision=TOP_PRECISION, preferred_element_type=F32
    )
    win_ref[...] = windows
    for i in (4, 5, 6):
        flush(i)
    same = windows[:, : 2 * rows]
    apart = jnp.where(core == 1, windows[:, 2 * rows : 4 * rows], windows[:, 4 * rows :])
    for head in range(heads):
        bias[head, :, :rows] = toeplitz(same[head : head + 1], rows)
        bias[head, :, rows:] = toeplitz(apart[head : head + 1], rows)
    x = own_ref[...].astype(F32)
    y = other_ref[...].astype(F32)
    gain = gain_first_ref[...].reshape(1, width)
    root = root_mean(x)
    root_ref[...] = jnp.broadcast_to(root, root_ref.shape)
    flush(7)
    act_own = (x * root * gain).astype(BF16)
    act_other = (y * root_mean(y) * gain).astype(BF16)
    act = jnp.concatenate([act_own, act_other], axis=0)
    wait(7)
    keys = dot(act, wk[...]).astype(BF16)
    wait(8)
    values = dot(act, wv[...]).astype(BF16)
    wait(9)
    queries = dot(act_own, wq[...]).astype(BF16)
    low_half = lax.broadcasted_iota(jnp.int32, (rows, 2 * size), 1) < size
    mixed = []
    for pair in range(heads // 2):
        lanes = slice(pair * 2 * size, (pair + 1) * 2 * size)
        outs = []
        for side in range(2):
            probs = attend(
                queries[:, lanes], keys[:, lanes], scale, bias[2 * pair + side], side, low_half
            )
            outs.append(dot(probs.astype(BF16), values[:, lanes]))
        mixed.append(jnp.where(low_half, outs[0], outs[1]).astype(BF16))
    mixed = jnp.concatenate(mixed, axis=1)
    mixed_ref[...] = mixed
    flush(3)
    for i in (10, 11, 12, 13):
        wait(i)
    out_ref[:, width : 2 * width] = dot(place, cot_ref[...]).astype(BF16)
    middle = x + dot(mixed, wo[...])
    middle_ref[...] = middle
    flush(0)
    gain_second = gain_second_ref[...].reshape(1, width)
    act_second = (middle * root_mean(middle) * gain_second).astype(BF16)
    logits = cols_by_cols(act_second, router_ref[...])
    grown = jnp.exp(logits - jnp.max(logits, axis=-1, keepdims=True))
    gate = jnp.sum(grown * choose, axis=-1, keepdims=True) / jnp.sum(
        grown, axis=-1, keepdims=True
    )
    gate_ref[...] = jnp.broadcast_to(gate, gate_ref.shape)
    out_ref[:, :width] = dot(place, act_second).astype(BF16)


def halves_kernel(
    heads,
    wait,
    flush,
    own_ref,
    other_ref,
    gain_first_ref,
    wq_ref,
    wk_ref,
    wv_ref,
    win_ref,
    after_ref,
    act_ref,
    query_ref,
    key_ref,
    value_ref,
    probs_ref,
    wq_half,
    wk_half,
    wv_half,
    sems,
):
    rows, width = own_ref.shape
    size = width // heads
    part = width // 2
    scale = 1.0 / math.sqrt(size)
    core = lax.axis_index("ffn")
    columns = pl.ds(pl.multiple_of(core * part, LANES), part)
    copies = [
        pltpu.make_async_copy(ref.at[:, columns], half, sems.at[i])
        for i, (ref, half) in enumerate(((wq_ref, wq_half), (wk_ref, wk_half), (wv_ref, wv_half)))
    ]
    for copy in copies:
        copy.start()
    x = own_ref[...].astype(F32)
    y = other_ref[...].astype(F32)
    gain = gain_first_ref[...].reshape(1, width)
    act = jnp.concatenate(
        [(x * root_mean(x) * gain).astype(BF16), (y * root_mean(y) * gain).astype(BF16)], axis=0
    )
    act_ref[...] = act
    for copy in copies:
        copy.wait()
    queries = dot(act, wq_half[...]).astype(BF16)
    keys = dot(act, wk_half[...]).astype(BF16)
    values = dot(act, wv_half[...]).astype(BF16)
    query_ref[...] = queries
    key_ref[...] = keys
    value_ref[...] = values
    for i in range(4):
        flush(i)
    low_half = lax.broadcasted_iota(jnp.int32, (2 * rows, 2 * size), 1) < size
    for pair in range(heads // 4):
        lanes = slice(pair * 2 * size, (pair + 1) * 2 * size)
        for side in range(2):
            head = 2 * pair + side
            window = win_ref[pl.ds(core * (heads // 2) + head, 1), :]
            same = toeplitz(window[:, : 2 * rows], rows)
            ahead = toeplitz(window[:, 2 * rows : 4 * rows], rows)
            behind = toeplitz(window[:, 4 * rows :], rows)
            first = jnp.where(core == 1, ahead, behind)
            second = jnp.where(core == 1, behind, ahead)
            bias = jnp.concatenate(
                [
                    jnp.concatenate([same, first], axis=1),
                    jnp.concatenate([second, same], axis=1),
                ],
                axis=0,
            )
            probs_ref[head] = attend(
                queries[:, lanes], keys[:, lanes], scale, bias, side, low_half
            )


def expert_kernel(
    capacity,
    chunk,
    wait,
    flush,
    arrived_ref,
    router_ref,
    in_own_ref,
    in_other_ref,
    down_own_ref,
    down_other_ref,
    after_ref,
    hid_own_ref,
    pre_own_ref,
    sent_ref,
    bundle_ref,
    grad_ref,
    produced_ref,
    router_grad_ref,
    in_vmem,
    down_vmem,
    bundle,
    sems,
):
    total = arrived_ref.shape[0]
    experts, width = router_ref.shape
    slots = total // experts
    hidden = in_own_ref.shape[1]
    steps = hidden // chunk
    mine = lax.axis_index("expert")
    core = lax.axis_index("ffn")
    copies = []
    for side, (win, wdown) in enumerate(
        ((in_own_ref, down_own_ref), (in_other_ref, down_other_ref))
    ):
        for step in range(steps):
            i = side * steps + step
            span = pl.ds(step * chunk, chunk)
            copies.append(
                (
                    pltpu.make_async_copy(win.at[:, span], in_vmem.at[i], sems.at[0, i]),
                    pltpu.make_async_copy(wdown.at[span, :], down_vmem.at[i], sems.at[1, i]),
                )
            )
    for copy in copies[0]:
        copy.start()
    for i in (0, 1):
        wait(i)
    for pair in copies[1:]:
        for copy in pair:
            copy.start()
    flat = arrived_ref[:, :width]
    cot = arrived_ref[:, width : 2 * width]
    filled = arrived_ref[:, 2 * width :]
    row = lax.broadcasted_iota(jnp.int32, (total, total), 0)
    col = lax.broadcasted_iota(jnp.int32, (total, total), 1)
    shift = slots.bit_length() - 1
    row_block = jnp.right_shift(row, shift)
    col_block = jnp.right_shift(col, shift)
    before = (col_block < row_block).astype(F32).astype(BF16)
    ahead = (col_block < row_block + core).astype(F32).astype(BF16)
    slot = jnp.bitwise_and(lax.broadcasted_iota(jnp.int32, (total, 1), 0), slots - 1)
    position = dot(before, filled)[:, 0:1] + dot(ahead, filled)[:, 1:2] + slot.astype(F32)
    keep = jnp.where(position < capacity, 1.0, 0.0)
    logits = cols_by_cols(flat, router_ref[...])
    grown = jnp.exp(logits - jnp.max(logits, axis=-1, keepdims=True))
    router_probs = grown / jnp.sum(grown, axis=-1, keepdims=True)
    onehot = (lax.broadcasted_iota(jnp.int32, (total, experts), 1) == mine).astype(F32)
    gate = jnp.sum(router_probs * onehot, axis=-1, keepdims=True)
    sent = (cot.astype(F32) * (gate * keep)).astype(BF16)
    sent_ref[...] = sent
    flush(2)
    bundle[:, :width] = flat
    bundle[:, width : 2 * width] = sent
    writes = []

    def forward(first, size):
        span = pl.ds(first, size)
        write = pltpu.make_async_copy(
            bundle.at[:, span], bundle_ref.at[:, span], sems.at[2, len(writes)]
        )
        write.start()
        writes.append(write)

    forward(0, 2 * width)
    produced = jnp.zeros((total, width), F32)
    grad = jnp.zeros((total, width), F32)
    inner = math.sqrt(2.0 / math.pi)
    for i, pair in enumerate(copies):
        own_side = i < steps
        first = (i % steps) * chunk
        for copy in pair:
            copy.wait()
        win, wdown = in_vmem[i], down_vmem[i]
        pre = dot(flat, win)
        square = pre * pre
        curve = jnp.tanh(inner * pre * (1.0 + 0.044715 * square))
        half_up = 0.5 + 0.5 * curve
        act = (pre * half_up).astype(BF16)
        slope = half_up + (0.5 * inner) * pre * (1.0 - curve * curve) * (
            1.0 + (3 * 0.044715) * square
        )
        grad_pre = (slope * cols_by_cols(sent, wdown)).astype(BF16)
        if own_side:
            hid_own_ref[:, first : first + chunk] = act
            pre_own_ref[:, first : first + chunk] = grad_pre
        else:
            first += 2 * width
            bundle[:, first : first + chunk] = act
            bundle[:, first + hidden : first + hidden + chunk] = grad_pre
            forward(first, chunk)
            forward(first + hidden, chunk)
        if i + 1 == steps:
            flush(0)
            flush(1)
        produced = produced + dot(act, wdown)
        grad = grad + cols_by_cols(grad_pre, win)
    produced_low = produced.astype(BF16)
    kept = produced_low.astype(F32) * keep
    produced_ref[...] = kept.astype(BF16)
    flush(5)
    grad_gate = jnp.sum(cot.astype(F32) * kept, axis=-1, keepdims=True)
    grad_logits = ((grad_gate * gate) * (onehot - router_probs)).astype(BF16)
    grad_ref[...] = (grad * keep + dot(grad_logits, router_ref[...])).astype(BF16)
    flush(4)
    router_grad_ref[...] = rows_by_rows(grad_logits, flat)
    for write in writes:
        write.wait()


def expert_weights_kernel(
    flat_own, sent_own, hid_own, pre_own, flat_other, sent_other, hid_other, pre_other, in_ref, down_ref
):
    in_ref[0] = rows_by_rows(flat_own[...], pre_own[...]) + rows_by_rows(
        flat_other[...], pre_other[...]
    )
    down_ref[0] = rows_by_rows(hid_own[...], sent_own[...]) + rows_by_rows(
        hid_other[...], sent_other[...]
    )


def expert_weights(flat, sent, hid, pre, bundle, chunk):
    total, width = sent.shape
    hidden = hid.shape[1]
    steps = hidden // chunk
    skip = 2 * width // chunk
    whole = pl.BlockSpec((total, width), lambda i: (0, 0))
    second = pl.BlockSpec((total, width), lambda i: (0, 1))
    part = pl.BlockSpec((total, chunk), lambda i: (0, i))
    return pl.pallas_call(
        expert_weights_kernel,
        grid=(steps,),
        out_shape=[
            jax.ShapeDtypeStruct((1, width, hidden), F32),
            jax.ShapeDtypeStruct((1, hidden, width), F32),
        ],
        in_specs=[
            whole,
            whole,
            part,
            part,
            whole,
            second,
            pl.BlockSpec((total, chunk), lambda i: (0, i + skip)),
            pl.BlockSpec((total, chunk), lambda i: (0, i + skip + steps)),
        ],
        out_specs=[
            pl.BlockSpec((1, width, chunk), lambda i: (0, 0, i)),
            pl.BlockSpec((1, chunk, width), lambda i: (0, i, 0)),
        ],
        compiler_params=pltpu.CompilerParams(vmem_limit_bytes=64 * 2**20),
        cost_estimate=pl.CostEstimate(
            flops=8 * total * width * hidden, bytes_accessed=14000000, transcendentals=0
        ),
    )(flat, sent, hid, pre, bundle, bundle, bundle, bundle)


def middle_back(returned, fetch, middle, gain, cot):
    grad = dot(fetch, returned)
    root = root_mean(middle)
    scaled = middle * root
    up = gain * grad
    grad_middle = cot.astype(F32) + root * (
        up - scaled * jnp.mean(up * scaled, axis=-1, keepdims=True)
    )
    return grad_middle, grad * scaled


def place_of(target, order):
    relative = jnp.bitwise_xor(target, lax.axis_index("expert"))
    place = 0
    for bit in order:
        place = place * 2 + jnp.bitwise_and(jnp.right_shift(relative, bit), 1)
    return place


def chunk_place(chunk, order, levels):
    target = sum((((chunk >> (levels - 1 - k)) & 1) << bit) for k, bit in enumerate(order[:levels]))
    return place_of(target, order[:levels])


def small_rows(experts):
    return [0, 2, 4, 16, 16 + experts, 16 + 2 * experts]


def backward_kernel(
    heads,
    orders,
    levels,
    wait,
    flush,
    returned_ref,
    returned_other_ref,
    fetch_ref,
    fetch_other_ref,
    middle_ref,
    middle_other_ref,
    cot_ref,
    cot_other_ref,
    gain_second_ref,
    mixed_own_ref,
    mixed_other_ref,
    value_ref,
    probs_ref,
    key_ref,
    query_ref,
    act_ref,
    hot_ref,
    own_ref,
    other_ref,
    router_ref,
    after_ref,
    wo_ref,
    wq_ref,
    wk_ref,
    wv_ref,
    keep_0_ref,
    send_0_ref,
    keep_1_ref,
    send_1_ref,
    keep_2_ref,
    send_2_ref,
    grad_middle_ref,
    small_ref,
    input_own_ref,
    input_other_ref,
    wo_half,
    wq_half,
    wk_half,
    wv_half,
    part_0,
    part_1,
    part_2,
    small,
    sems,
):
    rows, width = middle_ref.shape
    size = width // heads
    part = width // 2
    experts = router_ref.shape[0]
    scale = 1.0 / math.sqrt(size)
    core = lax.axis_index("ffn")
    span = pl.ds(pl.multiple_of(core * part, LANES), part)
    copies = [
        pltpu.make_async_copy(src, half, sems.at[6 + i])
        for i, (src, half) in enumerate(
            (
                (wo_ref.at[span, :], wo_half),
                (wq_ref.at[:, span], wq_half),
                (wk_ref.at[:, span], wk_half),
                (wv_ref.at[:, span], wv_half),
            )
        )
    ]
    for copy in copies:
        copy.start()
    parts = (part_0, part_1, part_2)
    halves = ((keep_0_ref, send_0_ref), (keep_1_ref, send_1_ref), (keep_2_ref, send_2_ref))
    third = width // 3
    height = third >> levels
    writes = []
    for p, pair in enumerate(halves):
        rows_half = pair[0].shape[0]
        for i, ref in enumerate(pair):
            writes.append(
                pltpu.make_async_copy(
                    parts[p].at[pl.ds(i * rows_half, rows_half), :], ref, sems.at[2 * p + i]
                )
            )
    places = [
        [chunk_place(chunk, order, levels) * (4 * height) for chunk in range(2**levels)]
        for order in orders
    ]

    def pack(matrix, value):
        for p, ref in enumerate(parts):
            for chunk in range(2**levels):
                first = p * third + chunk * height
                at = pl.multiple_of(places[p][chunk] + matrix * height, 16)
                ref[pl.ds(at, height), :] = value[first : first + height]

    for i in range(9):
        wait(i)
    copies[0].wait()
    gain = gain_second_ref[...].reshape(1, width)
    grad_own, gain_terms = middle_back(
        returned_ref[...], fetch_ref[...], middle_ref[...], gain, cot_ref[...]
    )
    grad_other, _ = middle_back(
        returned_other_ref[...], fetch_other_ref[...], middle_other_ref[...], gain, cot_other_ref[...]
    )
    gain_second = jnp.sum(gain_terms, axis=0, keepdims=True)
    grad_middle_ref[...] = grad_own
    flush(6)
    grad_low = jnp.concatenate([grad_own, grad_other], axis=0).astype(BF16)
    grad_mixed = cols_by_cols(grad_low, wo_half[...]).astype(BF16)
    for i in range(9, 20):
        wait(i)
    for copy in copies[1:]:
        copy.wait()
    mixed = jnp.concatenate([mixed_own_ref[...], mixed_other_ref[...]], axis=0)
    grad_columns = jnp.where(core == 0, grad_low[:, :part], grad_low[:, part:])
    pack(3, rows_by_rows(mixed, grad_columns).astype(BF16))
    low_half = lax.broadcasted_iota(jnp.int32, (2 * rows, 2 * size), 1) < size
    grad_q, grad_k, grad_v = [], [], []
    same, ahead, behind = [], [], []
    for pair in range(heads // 4):
        lanes = slice(pair * 2 * size, (pair + 1) * 2 * size)
        query, key, value = query_ref[:, lanes], key_ref[:, lanes], value_ref[:, lanes]
        grad_pair = grad_mixed[:, lanes]
        got_q, got_k, got_v = [], [], []
        for side in range(2):
            probs = probs_ref[2 * pair + side]
            keep_lanes = low_half if side == 0 else jnp.logical_not(low_half)
            own_grad = jnp.where(keep_lanes, grad_pair, 0).astype(BF16)
            grad_probs = cols_by_cols(own_grad, value)
            got_v.append(rows_by_rows(probs.astype(BF16), grad_pair))
            inner = jnp.sum(probs * grad_probs, axis=-1, keepdims=True)
            grad_scores = probs * (grad_probs - inner)
            same.append(
                diagonal_sums(grad_scores[:rows, :rows] + grad_scores[rows:, rows:], rows)
            )
            first = diagonal_sums(grad_scores[:rows, rows:], rows)
            second = diagonal_sums(grad_scores[rows:, :rows], rows)
            ahead.append(jnp.where(core == 1, first, second))
            behind.append(jnp.where(core == 1, second, first))
            grad_raw = (grad_scores * scale).astype(BF16)
            got_q.append(dot(grad_raw, key))
            got_k.append(rows_by_rows(grad_raw, query))
        grad_q.append(jnp.where(low_half, got_q[0], got_q[1]).astype(BF16))
        grad_k.append(jnp.where(low_half, got_k[0], got_k[1]).astype(BF16))
        grad_v.append(jnp.where(low_half, got_v[0], got_v[1]).astype(BF16))
    grad_q = jnp.concatenate(grad_q, axis=1)
    grad_k = jnp.concatenate(grad_k, axis=1)
    grad_v = jnp.concatenate(grad_v, axis=1)
    act = act_ref[...]
    pack(0, rows_by_rows(act, grad_q).astype(BF16))
    pack(1, rows_by_rows(act, grad_k).astype(BF16))
    pack(2, rows_by_rows(act, grad_v).astype(BF16))
    for write in writes:
        write.start()
    grad_act = (
        cols_by_cols(grad_q, wq_half[...])
        + cols_by_cols(grad_k, wk_half[...])
        + cols_by_cols(grad_v, wv_half[...])
    )
    input_other_ref[...] = grad_act[rows:].astype(BF16)
    flush(9)
    input_own_ref[...] = grad_act[:rows]
    flush(8)
    x = own_ref[...].astype(F32)
    y = other_ref[...].astype(F32)
    gain_first = jnp.sum(
        grad_act[:rows] * (x * root_mean(x)) + grad_act[rows:] * (y * root_mean(y)),
        axis=0,
        keepdims=True,
    )
    sums = jnp.concatenate(
        [jnp.concatenate(part_sums, axis=0) for part_sums in (same, ahead, behind)], axis=1
    )
    table = lax.dot_general(
        sums,
        hot_ref[...],
        (((1,), (1,)), ((), ())),
        precision=TOP_PRECISION,
        preferred_element_type=F32,
    )
    at = small_rows(experts)
    small[: at[3]] = jnp.zeros((at[3], part), F32)
    for i, value in enumerate((gain_first, gain_second)):
        small[at[i] : at[i] + 1] = value[:, :part]
        small[at[i] + 1 : at[i] + 2] = value[:, part:]
    small[at[2] : at[2] + heads // 2, : table.shape[1]] = table
    small[at[3] : at[4]] = router_ref[:, :part]
    small[at[4] : at[5]] = router_ref[:, part:]
    small_ref[...] = small[...].astype(BF16)
    flush(7)
    for write in writes:
        write.wait()


def assemble_kernel(orders, levels, chosen, upper, last, wait, flush, *refs):
    arrays, refs = refs[: 2 * len(chosen)], refs[2 * len(chosen) :]
    if last is not None:
        experts, heads = last
        (small_own_ref, small_other_ref), refs = refs[:2], refs[2:]
    if upper:
        refs = refs[4:]
    outs, (wide, sems) = refs[:4], refs[-2:]
    if last is not None:
        gain_first_ref, gain_second_ref, table_ref, router_ref = refs[4:8]
    width = outs[0].shape[1]
    part = width // 2
    third = width // 3
    side = third // 2
    height = third >> levels
    half = 2 ** (levels - 1)
    core = lax.axis_index("ffn")
    mine = lax.axis_index("expert")
    own = pl.ds(pl.multiple_of(core * part, LANES), part)
    theirs = pl.ds(pl.multiple_of((1 - core) * part, LANES), part)
    writes = []
    for n, p in enumerate(chosen):
        order = orders[p]
        for i in (2 * n, 2 * n + 1):
            wait(i)
        for low in range(half):
            place = chunk_place(low, order, levels)
            place = jnp.bitwise_and(place, half - 1)
            for matrix in range(4):
                at = pl.ds(pl.multiple_of((place * 4 + matrix) * height, 16), height)
                to = pl.ds(low * height, height)
                wide[n, matrix, to, own] = arrays[2 * n][at, :].astype(F32)
                wide[n, matrix, to, theirs] = arrays[2 * n + 1][at, :].astype(F32)
        bit = jnp.bitwise_and(jnp.right_shift(mine, order[0]), 1)
        if upper:
            bit = 1 - bit
        first = pl.multiple_of(p * third + bit * side, side)
        for matrix in range(4):
            write = pltpu.make_async_copy(
                wide.at[n, matrix], outs[matrix].at[pl.ds(first, side), :], sems.at[4 * n + matrix]
            )
            write.start()
            writes.append(write)
    if last is not None:
        at = small_rows(experts)
        mine, other = small_own_ref[...], small_other_ref[...]
        both = mine + other
        gain_first_ref[...] = jnp.concatenate([both[0:1], both[1:2]], axis=1).reshape(width)
        gain_second_ref[...] = jnp.concatenate([both[2:3], both[3:4]], axis=1).reshape(width)
        buckets = table_ref.shape[1]
        low = mine[at[2] : at[2] + heads // 2, :buckets]
        high = other[at[2] : at[2] + heads // 2, :buckets]
        table_ref[...] = jnp.where(
            core == 0,
            jnp.concatenate([low, high], axis=0),
            jnp.concatenate([high, low], axis=0),
        )
        router_ref[...] = jnp.concatenate([both[at[3] : at[4]], both[at[4] : at[5]]], axis=1)
    for write in writes:
        write.wait()


def assemble(orders, levels, chosen, arrays, width, earlier=(), smalls=(), last=None):
    tail = []
    modes = "l" * len(arrays)
    if last is not None:
        experts, heads, buckets = last
        tail = [((width,), F32), ((width,), F32), ((heads, buckets), F32), ((experts, width), F32)]
        modes += "hh"
        last = (experts, heads)
    first = len(modes)
    modes += "r" * len(earlier)
    return call(
        functools.partial(assemble_kernel, orders, levels, chosen, bool(earlier), last),
        [((width, width), F32)] * 4 + tail,
        (*arrays, *smalls, *earlier),
        modes + "rrrr" + "h" * len(tail),
        vmem=16,
        aliases={first + i: i for i in range(len(earlier))},
        scratch=[
            pltpu.VMEM((len(chosen), 4, width // 6, width), F32),
            pltpu.SemaphoreType.DMA((4 * len(chosen),)),
        ],
        nbytes=8000000,
    )


def swap(x):
    return lax.ppermute(x, "ffn", [(0, 1), (1, 0)])


def flip(x, bit):
    peers = lax.axis_size("expert")
    return lax.ppermute(x, "expert", [(i, i ^ (1 << bit)) for i in range(peers)])


def add_low(left, right):
    return (left.astype(F32) + right.astype(F32)).astype(BF16)


def sum_over_chips(keeps, sends, orders, levels, small, beside):
    count = len(orders[0])
    todo = set(orders[0])
    ridden = set()

    def exchange(phase, x, bit):
        nonlocal small
        if bit not in todo or phase in ridden or phase < 2 or phase > 2 * count - 3:
            return flip(x, bit)
        todo.discard(bit)
        ridden.add(phase)
        got = flip(jnp.concatenate([x, small.astype(BF16)]), bit)
        rows = x.shape[0]
        small = small.astype(F32) + got[rows:].astype(F32)
        return got[:rows]

    def mine(bit):
        return (lax.axis_index("expert") >> bit) & 1

    whole = [None] * len(orders)
    for k in range(count - 1):
        for p, order in enumerate(orders):
            keep, got = keeps[p], exchange(k, sends[p], order[k])
            half = keep.shape[0] // 2
            if k + 2 == count:
                whole[p] = add_low(keep, got)
            elif k + 1 < levels:
                keeps[p] = add_low(keep[:half], got[:half])
                sends[p] = add_low(keep[half:], got[half:])
            else:
                both = add_low(keep, got)
                upper = mine(order[k + 1])
                keeps[p] = lax.dynamic_slice_in_dim(both, upper * half, half, 0)
                sends[p] = lax.dynamic_slice_in_dim(both, (1 - upper) * half, half, 0)
    whole, beside = lax.optimization_barrier((whole, beside))
    for p, order in enumerate(orders):
        x = whole[p]
        whole[p] = add_low(x, exchange(count - 1, x, order[-1]))
    got = [None] * len(orders)
    for k in reversed(range(count - 1)):
        for p, order in enumerate(orders):
            x = whole[p]
            got[p] = exchange(2 * count - 2 - k, x, order[k])
            if k == 0:
                continue
            if k < levels:
                whole[p] = jnp.concatenate([x, got[p]])
            else:
                whole[p] = jnp.where(
                    mine(order[k]) == 1,
                    jnp.concatenate([got[p], x]),
                    jnp.concatenate([x, got[p]]),
                )
    for bit in sorted(todo):
        small = small.astype(F32) + flip(small, bit).astype(F32)
    return whole, got, small, beside


def shards(
    tokens,
    norm_first,
    w_query,
    w_key,
    w_value,
    w_out,
    bucket_bias_table,
    norm_second,
    w_router,
    w_in,
    w_down,
    expert_ids,
    cotangent,
):
    rows, width = tokens.shape
    buckets, heads = bucket_bias_table.shape
    pair = lax.axis_size("ffn")
    experts = w_router.shape[1]
    total = 2 * rows
    capacity = 5 * rows * pair // 4
    hidden = w_in.shape[2]
    part = width // 2
    hot = jnp.asarray(bucket_windows(rows, buckets, REACH))
    router = w_router.T

    other = swap(tokens)
    ids = expert_ids.reshape(1, rows)
    ids_other = swap(ids)
    other, ids_other, w_in, w_down, cotangent = lax.optimization_barrier(
        (other, ids_other, w_in, w_down, cotangent)
    )
    in_own, down_own = w_in[0], w_down[0]
    in_other, down_other = swap(in_own), swap(down_own)
    cot_other = swap(cotangent)
    middle, gate, outgoing, mixed, windows, fetch, fetch_other, root = call(
        functools.partial(forward_kernel, heads),
        [
            ((rows, width), F32),
            ((rows, LANES), F32),
            ((total, 2 * width + LANES), BF16),
            ((rows, width), BF16),
            ((heads, 6 * rows), F32),
            ((rows, total), BF16),
            ((rows, total), BF16),
            ((rows, LANES), F32),
        ],
        (
            tokens,
            other,
            norm_first,
            ids,
            ids_other,
            bucket_bias_table.T,
            hot,
            w_key,
            w_value,
            w_query,
            w_out,
            norm_second,
            router,
            cotangent,
        ),
        "hhhhhhhlllllll" + "hhhhhhhh",
        vmem=64,
        flops=3000000000,
        scratch=[pltpu.VMEM((heads, rows, 2 * rows), F32)],
    )
    arrived = lax.all_to_all(outgoing, "expert", 0, 0, tiled=True)
    mixed_other, middle_other = swap(mixed), swap(middle)
    act, queries, keys, values, probs = call(
        functools.partial(halves_kernel, heads),
        [
            ((2 * rows, width), BF16),
            ((2 * rows, part), BF16),
            ((2 * rows, part), BF16),
            ((2 * rows, part), BF16),
            ((heads // 2, 2 * rows, 2 * rows), F32),
        ],
        (tokens, other, norm_first, w_query, w_key, w_value, windows, gate),
        "hhhrrrhr" + "hhhhh",
        vmem=64,
        flops=3000000000,
        scratch=[pltpu.VMEM((width, part), BF16)] * 3 + [pltpu.SemaphoreType.DMA((3,))],
    )
    chunk = hidden // 2
    steps = 2 * hidden // chunk
    hid_own, pre_own, sent, bundle, grad_slots, produced, router_part = call(
        functools.partial(expert_kernel, capacity, chunk),
        [
            ((total, hidden), BF16),
            ((total, hidden), BF16),
            ((total, width), BF16),
            ((total, 2 * width + 2 * hidden), BF16),
            ((total, width), BF16),
            ((total, width), BF16),
            ((experts, width), F32),
        ],
        (arrived, router, in_own, in_other, down_own, down_other, act),
        "llrrrrr" + "hhhrhhh",
        vmem=64,
        flops=6000000000,
        scratch=[
            pltpu.VMEM((steps, width, chunk), BF16),
            pltpu.VMEM((steps, chunk, width), BF16),
            pltpu.VMEM((total, 2 * width + 2 * hidden), BF16),
            pltpu.SemaphoreType.DMA((3, steps + 1)),
        ],
    )
    bundle_other = swap(bundle)
    grad_returned = lax.all_to_all(grad_slots, "expert", 0, 0, tiled=True)
    grad_w_in, grad_w_down = expert_weights(arrived, sent, hid_own, pre_own, bundle_other, 256)
    produced, grad_returned, grad_w_in = lax.optimization_barrier(
        (produced, grad_returned, grad_w_in)
    )
    produced_returned = lax.all_to_all(produced, "expert", 0, 0, tiled=True)
    bits = experts.bit_length() - 1
    levels = min(bits - 1, 3)
    rest = list(range(3, bits))
    orders = [[0, 1, 2] + rest, [1, 2, 0] + rest, [2, 0, 1] + rest]
    third = 4 * width // 3
    *halves, grad_middle, small, input_own, input_other = call(
        functools.partial(backward_kernel, heads, orders, levels),
        [((third // 2, part), BF16)] * 6
        + [
            ((rows, width), F32),
            ((16 + 2 * experts, part), BF16),
            ((rows, width), F32),
            ((rows, width), BF16),
        ],
        (
            grad_returned,
            swap(grad_returned),
            fetch,
            fetch_other,
            middle,
            middle_other,
            cotangent,
            cot_other,
            norm_second,
            mixed,
            mixed_other,
            values,
            probs,
            keys,
            queries,
            act,
            hot,
            tokens,
            other,
            router_part,
            grad_w_in,
            w_out,
            w_query,
            w_key,
            w_value,
        ),
        "l" * 20 + "rrrrr" + "rrrrrr" + "hhhh",
        vmem=56,
        flops=4000000000,
        scratch=[
            pltpu.VMEM((part, width), BF16),
            *[pltpu.VMEM((width, part), BF16)] * 3,
            *[pltpu.VMEM((third, part), BF16)] * 3,
            pltpu.VMEM((16 + 2 * experts, part), F32),
            pltpu.SemaphoreType.DMA((10,)),
        ],
    )
    halves, grad_middle, small, input_own, input_other, produced_returned = (
        lax.optimization_barrier(
            (halves, grad_middle, small, input_own, input_other, produced_returned)
        )
    )
    beside = (grad_middle, input_own, swap(input_other), produced_returned)
    kept, got, small, beside = sum_over_chips(
        list(halves[0::2]), list(halves[1::2]), orders, levels, small, beside
    )
    grad_middle, input_own, input_swapped, produced_returned = beside
    root = root[:, :1]
    scaled = tokens.astype(F32) * root
    up = norm_first * (input_own + input_swapped.astype(F32))
    grad_input = grad_middle + root * (
        up - scaled * jnp.mean(up * scaled, axis=-1, keepdims=True)
    )
    expert_branch = gate[:, :1] * dot(fetch, produced_returned)
    output = (middle + expert_branch).astype(BF16)
    near = []
    for rows_kept in kept:
        near += [rows_kept, swap(rows_kept)]
    matrices = assemble(orders, levels, (0, 1, 2), near, width)
    small_other = swap(small)
    got, matrices, small, small_other, output, expert_branch, grad_input = (
        lax.optimization_barrier(
            (got, matrices, small, small_other, output, expert_branch, grad_input)
        )
    )
    far = []
    for rows_got in got:
        far += [rows_got, swap(rows_got)]
    results = assemble(
        orders,
        levels,
        (0, 1, 2),
        far,
        width,
        matrices,
        (small, small_other),
        (experts, heads, buckets),
    )
    return (
        output,
        grad_input,
        results[4],
        results[0],
        results[1],
        results[2],
        results[3],
        results[6].T,
        results[5],
        results[7].T,
        grad_w_in,
        grad_w_down,
        expert_branch,
    )


def solution(mesh):
    placed = (
        P(("expert", "ffn"), None),
        P(),
        P(),
        P(),
        P(),
        P(),
        P(),
        P(),
        P(),
        P("expert", None, "ffn"),
        P("expert", "ffn", None),
        P(("expert", "ffn")),
        P(("expert", "ffn"), None),
    )
    return jax.shard_map(
        shards,
        mesh=mesh,
        in_specs=placed,
        out_specs=(
            P(("expert", "ffn"), None),
            P(("expert", "ffn"), None),
            P(),
            P(),
            P(),
            P(),
            P(),
            P(),
            P(),
            P(),
            P("expert", None, "ffn"),
            P("expert", "ffn", None),
            P(("expert", "ffn"), None),
        ),
        check_vma=False,
    )
```

```python
import functools
import math

import jax
import jax.numpy as jnp
import numpy as np
from jax import lax
from jax.experimental import pallas as pl
from jax.experimental.pallas import tpu as pltpu
from jax.sharding import PartitionSpec as P

REACH = 128
EPS = 1e-06
TOP_PRECISION = lax.Precision.HIGHEST
LANES = 128
F32 = jnp.float32
BF16 = jnp.bfloat16


def bucket_of(distance, buckets, reach):
    half = buckets // 2
    exact = half // 2
    result = np.where(distance < 0, half, 0)
    magnitude = np.abs(distance)
    spread = exact + np.floor(
        np.log(np.maximum(magnitude, 1) / exact) / np.log(reach / exact) * (half - exact)
    )
    spread = np.minimum(spread, half - 1)
    return result + np.where(magnitude < exact, magnitude, spread)


def bucket_windows(rows, buckets, reach):
    lane = np.arange(2 * rows)
    offset = np.where(lane < rows, -lane, 2 * rows - lane)
    windows = []
    for shift in (0, rows, -rows):
        hot = bucket_of(offset + shift, buckets, reach)[None, :] == np.arange(buckets)[:, None]
        hot[:, rows] = False
        windows.append(hot)
    return np.concatenate(windows, axis=1).astype(np.float32)


def rows_by_rows(left, right):
    return lax.dot_general(left, right, (((0,), (0,)), ((), ())), preferred_element_type=F32)


def cols_by_cols(left, right):
    return lax.dot_general(left, right, (((1,), (1,)), ((), ())), preferred_element_type=F32)


def dot(left, right):
    return jnp.dot(left, right, preferred_element_type=F32)


def root_mean(x):
    return lax.rsqrt(jnp.mean(x * x, axis=-1, keepdims=True) + EPS)


def call(body, outs, args, modes, vmem=16, flops=0, scratch=(), aliases=None, nbytes=1000000):
    count, total = len(args), len(args) + len(outs)
    shapes = [(a.shape, a.dtype) for a in args] + list(outs)
    moved = [i for i in range(total) if modes[i] in "hls"]
    buffers = [pltpu.VMEM(*shapes[i]) for i in moved]

    def kernel(*refs):
        bodies = list(refs[:total])
        for i, ref in zip(moved, refs[total : total + len(moved)]):
            bodies[i] = ref
        extra = refs[total + len(moved) : -1]
        sems = refs[-1]
        copies = {}
        for i in moved:
            ends = (refs[i], bodies[i]) if i < count else (bodies[i], refs[i])
            copies[i] = pltpu.make_async_copy(*ends, sems.at[i])
        for i in moved:
            if i < count and modes[i] != "s":
                copies[i].start()
        flushed = set()

        def wait(i):
            copies[i].wait()

        wait.start = lambda i: copies[i].start()

        def flush(i):
            flushed.add(i)
            copies[count + i].start()

        for i in moved:
            if i < count and modes[i] == "h":
                wait(i)
        body(wait, flush, *bodies, *extra)
        for i in moved:
            if i >= count and i - count not in flushed:
                copies[i].start()
        for i in moved:
            if i >= count:
                copies[i].wait()

    specs = [pl.BlockSpec(memory_space=pltpu.HBM)] * total
    return pl.pallas_call(
        kernel,
        out_shape=[jax.ShapeDtypeStruct(s, d) for s, d in outs],
        in_specs=specs[:count],
        out_specs=specs[count:],
        scratch_shapes=buffers + list(scratch) + [pltpu.SemaphoreType.DMA((total,))],
        input_output_aliases=aliases or {},
        compiler_params=pltpu.CompilerParams(vmem_limit_bytes=vmem * 2**20),
        cost_estimate=pl.CostEstimate(flops=flops, bytes_accessed=nbytes, transcendentals=0),
    )(*args)


def toeplitz(window, rows):
    wide = jnp.broadcast_to(window, (rows, 2 * rows))
    return pltpu.roll(wide, 0, 1, stride=1, stride_axis=0)[:, :rows]


def diagonal_sums(square, rows):
    wide = jnp.concatenate([square, jnp.zeros_like(square)], axis=1)
    height = rows
    while height > 1:
        height //= 2
        wide = wide[:height] + pltpu.roll(wide[height:], 2 * rows - height, 1)
    return wide


def placement(ids, experts, total):
    rows = ids.shape[1]
    slots = total // experts
    choose = (lax.broadcasted_iota(jnp.int32, (experts, rows), 0) == ids).astype(F32)
    earlier = (
        lax.broadcasted_iota(jnp.int32, (rows, rows), 0)
        < lax.broadcasted_iota(jnp.int32, (rows, rows), 1)
    ).astype(F32)
    ranks = dot(choose.astype(BF16), earlier.astype(BF16))
    rank = jnp.sum(choose * ranks, axis=0, keepdims=True)
    target = ids * slots + rank.astype(jnp.int32)
    place = (lax.broadcasted_iota(jnp.int32, (total, rows), 0) == target).astype(F32)
    return choose, place


def attend(query_pair, key_pair, scale, bias, side, low_half):
    own = jnp.where(low_half if side == 0 else jnp.logical_not(low_half), query_pair, 0)
    scores = cols_by_cols(own.astype(BF16), key_pair) * scale + bias
    grown = jnp.exp(scores - jnp.max(scores, axis=-1, keepdims=True))
    return grown * (1.0 / jnp.sum(grown, axis=-1, keepdims=True))


def forward_kernel(
    heads,
    wait,
    flush,
    own_ref,
    other_ref,
    gain_first_ref,
    ids_ref,
    ids_other_ref,
    table_ref,
    hot_ref,
    wk,
    wv,
    wq,
    wo,
    gain_second_ref,
    router_ref,
    cot_ref,
    middle_ref,
    gate_ref,
    out_ref,
    mixed_ref,
    win_ref,
    fetch_ref,
    fetch_other_ref,
    root_ref,
    bias,
):
    rows, width = own_ref.shape
    size = width // heads
    scale = 1.0 / math.sqrt(size)
    core = lax.axis_index("ffn")
    total = out_ref.shape[0]
    experts = router_ref.shape[0]
    choose, place = placement(ids_ref[...], experts, total)
    _, place_other = placement(ids_other_ref[...], experts, total)
    fetch_ref[...] = place.T.astype(BF16)
    fetch_other_ref[...] = place_other.T.astype(BF16)
    choose = choose.T
    lane = lax.broadcasted_iota(jnp.int32, (total, LANES), 1)
    out_ref[:, 2 * width :] = jnp.where(
        lane == 0,
        jnp.sum(place, axis=1, keepdims=True),
        jnp.sum(place_other, axis=1, keepdims=True),
    ).astype(BF16)
    place = place.astype(BF16)
    windows = jnp.dot(
        table_ref[...], hot_ref[...], precision=TOP_PRECISION, preferred_element_type=F32
    )
    win_ref[...] = windows
    for i in (4, 5, 6):
        flush(i)
    same = windows[:, : 2 * rows]
    apart = jnp.where(core == 1, windows[:, 2 * rows : 4 * rows], windows[:, 4 * rows :])
    for head in range(heads):
        bias[head, :, :rows] = toeplitz(same[head : head + 1], rows)
        bias[head, :, rows:] = toeplitz(apart[head : head + 1], rows)
    x = own_ref[...].astype(F32)
    y = other_ref[...].astype(F32)
    gain = gain_first_ref[...].reshape(1, width)
    root = root_mean(x)
    root_ref[...] = jnp.broadcast_to(root, root_ref.shape)
    flush(7)
    act_own = (x * root * gain).astype(BF16)
    act_other = (y * root_mean(y) * gain).astype(BF16)
    act = jnp.concatenate([act_own, act_other], axis=0)
    wait(7)
    keys = dot(act, wk[...]).astype(BF16)
    wait(8)
    values = dot(act, wv[...]).astype(BF16)
    wait(9)
    queries = dot(act_own, wq[...]).astype(BF16)
    low_half = lax.broadcasted_iota(jnp.int32, (rows, 2 * size), 1) < size
    mixed = []
    for pair in range(heads // 2):
        lanes = slice(pair * 2 * size, (pair + 1) * 2 * size)
        outs = []
        for side in range(2):
            probs = attend(
                queries[:, lanes], keys[:, lanes], scale, bias[2 * pair + side], side, low_half
            )
            outs.append(dot(probs.astype(BF16), values[:, lanes]))
        mixed.append(jnp.where(low_half, outs[0], outs[1]).astype(BF16))
    mixed = jnp.concatenate(mixed, axis=1)
    mixed_ref[...] = mixed
    flush(3)
    for i in (10, 11, 12, 13):
        wait(i)
    out_ref[:, width : 2 * width] = dot(place, cot_ref[...]).astype(BF16)
    middle = x + dot(mixed, wo[...])
    middle_ref[...] = middle
    flush(0)
    gain_second = gain_second_ref[...].reshape(1, width)
    act_second = (middle * root_mean(middle) * gain_second).astype(BF16)
    logits = cols_by_cols(act_second, router_ref[...])
    grown = jnp.exp(logits - jnp.max(logits, axis=-1, keepdims=True))
    gate = jnp.sum(grown * choose, axis=-1, keepdims=True) / jnp.sum(
        grown, axis=-1, keepdims=True
    )
    gate_ref[...] = jnp.broadcast_to(gate, gate_ref.shape)
    out_ref[:, :width] = dot(place, act_second).astype(BF16)


def halves_kernel(
    heads,
    wait,
    flush,
    own_ref,
    other_ref,
    gain_first_ref,
    wq_ref,
    wk_ref,
    wv_ref,
    win_ref,
    after_ref,
    act_ref,
    query_ref,
    key_ref,
    value_ref,
    probs_ref,
    wq_half,
    wk_half,
    wv_half,
    sems,
):
    rows, width = own_ref.shape
    size = width // heads
    part = width // 2
    scale = 1.0 / math.sqrt(size)
    core = lax.axis_index("ffn")
    columns = pl.ds(pl.multiple_of(core * part, LANES), part)
    copies = [
        pltpu.make_async_copy(ref.at[:, columns], half, sems.at[i])
        for i, (ref, half) in enumerate(((wq_ref, wq_half), (wk_ref, wk_half), (wv_ref, wv_half)))
    ]
    for copy in copies:
        copy.start()
    x = own_ref[...].astype(F32)
    y = other_ref[...].astype(F32)
    gain = gain_first_ref[...].reshape(1, width)
    act = jnp.concatenate(
        [(x * root_mean(x) * gain).astype(BF16), (y * root_mean(y) * gain).astype(BF16)], axis=0
    )
    act_ref[...] = act
    for copy in copies:
        copy.wait()
    queries = dot(act, wq_half[...]).astype(BF16)
    keys = dot(act, wk_half[...]).astype(BF16)
    values = dot(act, wv_half[...]).astype(BF16)
    query_ref[...] = queries
    key_ref[...] = keys
    value_ref[...] = values
    for i in range(4):
        flush(i)
    low_half = lax.broadcasted_iota(jnp.int32, (2 * rows, 2 * size), 1) < size
    for pair in range(heads // 4):
        lanes = slice(pair * 2 * size, (pair + 1) * 2 * size)
        for side in range(2):
            head = 2 * pair + side
            window = win_ref[pl.ds(core * (heads // 2) + head, 1), :]
            same = toeplitz(window[:, : 2 * rows], rows)
            ahead = toeplitz(window[:, 2 * rows : 4 * rows], rows)
            behind = toeplitz(window[:, 4 * rows :], rows)
            first = jnp.where(core == 1, ahead, behind)
            second = jnp.where(core == 1, behind, ahead)
            bias = jnp.concatenate(
                [
                    jnp.concatenate([same, first], axis=1),
                    jnp.concatenate([second, same], axis=1),
                ],
                axis=0,
            )
            probs_ref[head] = attend(
                queries[:, lanes], keys[:, lanes], scale, bias, side, low_half
            )


def expert_kernel(
    capacity,
    chunk,
    wait,
    flush,
    arrived_ref,
    router_ref,
    in_own_ref,
    in_other_ref,
    down_own_ref,
    down_other_ref,
    after_ref,
    hid_own_ref,
    pre_own_ref,
    sent_ref,
    bundle_ref,
    grad_ref,
    produced_ref,
    router_grad_ref,
    in_vmem,
    down_vmem,
    bundle,
    sems,
):
    total = arrived_ref.shape[0]
    experts, width = router_ref.shape
    slots = total // experts
    hidden = in_own_ref.shape[1]
    steps = hidden // chunk
    mine = lax.axis_index("expert")
    core = lax.axis_index("ffn")
    copies = []
    for side, (win, wdown) in enumerate(
        ((in_own_ref, down_own_ref), (in_other_ref, down_other_ref))
    ):
        for step in range(steps):
            i = side * steps + step
            span = pl.ds(step * chunk, chunk)
            copies.append(
                (
                    pltpu.make_async_copy(win.at[:, span], in_vmem.at[i], sems.at[0, i]),
                    pltpu.make_async_copy(wdown.at[span, :], down_vmem.at[i], sems.at[1, i]),
                )
            )
    for copy in copies[0]:
        copy.start()
    for i in (0, 1):
        wait(i)
    for pair in copies[1:]:
        for copy in pair:
            copy.start()
    flat = arrived_ref[:, :width]
    cot = arrived_ref[:, width : 2 * width]
    filled = arrived_ref[:, 2 * width :]
    row = lax.broadcasted_iota(jnp.int32, (total, total), 0)
    col = lax.broadcasted_iota(jnp.int32, (total, total), 1)
    shift = slots.bit_length() - 1
    row_block = jnp.right_shift(row, shift)
    col_block = jnp.right_shift(col, shift)
    before = (col_block < row_block).astype(F32).astype(BF16)
    ahead = (col_block < row_block + core).astype(F32).astype(BF16)
    slot = jnp.bitwise_and(lax.broadcasted_iota(jnp.int32, (total, 1), 0), slots - 1)
    position = dot(before, filled)[:, 0:1] + dot(ahead, filled)[:, 1:2] + slot.astype(F32)
    keep = jnp.where(position < capacity, 1.0, 0.0)
    logits = cols_by_cols(flat, router_ref[...])
    grown = jnp.exp(logits - jnp.max(logits, axis=-1, keepdims=True))
    router_probs = grown / jnp.sum(grown, axis=-1, keepdims=True)
    onehot = (lax.broadcasted_iota(jnp.int32, (total, experts), 1) == mine).astype(F32)
    gate = jnp.sum(router_probs * onehot, axis=-1, keepdims=True)
    sent = (cot.astype(F32) * (gate * keep)).astype(BF16)
    sent_ref[...] = sent
    flush(2)
    bundle[:, :width] = flat
    bundle[:, width : 2 * width] = sent
    writes = []

    def forward(first, size):
        span = pl.ds(first, size)
        write = pltpu.make_async_copy(
            bundle.at[:, span], bundle_ref.at[:, span], sems.at[2, len(writes)]
        )
        write.start()
        writes.append(write)

    forward(0, 2 * width)
    produced = jnp.zeros((total, width), F32)
    grad = jnp.zeros((total, width), F32)
    inner = math.sqrt(2.0 / math.pi)
    for i, pair in enumerate(copies):
        own_side = i < steps
        first = (i % steps) * chunk
        for copy in pair:
            copy.wait()
        win, wdown = in_vmem[i], down_vmem[i]
        pre = dot(flat, win)
        square = pre * pre
        curve = jnp.tanh(inner * pre * (1.0 + 0.044715 * square))
        half_up = 0.5 + 0.5 * curve
        act = (pre * half_up).astype(BF16)
        slope = half_up + (0.5 * inner) * pre * (1.0 - curve * curve) * (
            1.0 + (3 * 0.044715) * square
        )
        grad_pre = (slope * cols_by_cols(sent, wdown)).astype(BF16)
        if own_side:
            hid_own_ref[:, first : first + chunk] = act
            pre_own_ref[:, first : first + chunk] = grad_pre
        else:
            first += 2 * width
            bundle[:, first : first + chunk] = act
            bundle[:, first + hidden : first + hidden + chunk] = grad_pre
            forward(first, chunk)
            forward(first + hidden, chunk)
        if i + 1 == steps:
            flush(0)
            flush(1)
        produced = produced + dot(act, wdown)
        grad = grad + cols_by_cols(grad_pre, win)
    produced_low = produced.astype(BF16)
    kept = produced_low.astype(F32) * keep
    produced_ref[...] = kept.astype(BF16)
    flush(5)
    grad_gate = jnp.sum(cot.astype(F32) * kept, axis=-1, keepdims=True)
    grad_logits = ((grad_gate * gate) * (onehot - router_probs)).astype(BF16)
    grad_ref[...] = (grad * keep + dot(grad_logits, router_ref[...])).astype(BF16)
    flush(4)
    router_grad_ref[...] = rows_by_rows(grad_logits, flat)
    for write in writes:
        write.wait()


def expert_weights_kernel(
    flat_own, sent_own, hid_own, pre_own, flat_other, sent_other, hid_other, pre_other, in_ref, down_ref
):
    in_ref[0] = rows_by_rows(flat_own[...], pre_own[...]) + rows_by_rows(
        flat_other[...], pre_other[...]
    )
    down_ref[0] = rows_by_rows(hid_own[...], sent_own[...]) + rows_by_rows(
        hid_other[...], sent_other[...]
    )


def expert_weights(flat, sent, hid, pre, bundle, chunk):
    total, width = sent.shape
    hidden = hid.shape[1]
    steps = hidden // chunk
    skip = 2 * width // chunk
    whole = pl.BlockSpec((total, width), lambda i: (0, 0))
    second = pl.BlockSpec((total, width), lambda i: (0, 1))
    part = pl.BlockSpec((total, chunk), lambda i: (0, i))
    return pl.pallas_call(
        expert_weights_kernel,
        grid=(steps,),
        out_shape=[
            jax.ShapeDtypeStruct((1, width, hidden), F32),
            jax.ShapeDtypeStruct((1, hidden, width), F32),
        ],
        in_specs=[
            whole,
            whole,
            part,
            part,
            whole,
            second,
            pl.BlockSpec((total, chunk), lambda i: (0, i + skip)),
            pl.BlockSpec((total, chunk), lambda i: (0, i + skip + steps)),
        ],
        out_specs=[
            pl.BlockSpec((1, width, chunk), lambda i: (0, 0, i)),
            pl.BlockSpec((1, chunk, width), lambda i: (0, i, 0)),
        ],
        compiler_params=pltpu.CompilerParams(vmem_limit_bytes=64 * 2**20),
        cost_estimate=pl.CostEstimate(
            flops=8 * total * width * hidden, bytes_accessed=14000000, transcendentals=0
        ),
    )(flat, sent, hid, pre, bundle, bundle, bundle, bundle)


def middle_back(returned, fetch, middle, gain, cot):
    grad = dot(fetch, returned)
    root = root_mean(middle)
    scaled = middle * root
    up = gain * grad
    grad_middle = cot.astype(F32) + root * (
        up - scaled * jnp.mean(up * scaled, axis=-1, keepdims=True)
    )
    return grad_middle, grad * scaled


def place_of(target, order):
    relative = jnp.bitwise_xor(target, lax.axis_index("expert"))
    place = 0
    for bit in order:
        place = place * 2 + jnp.bitwise_and(jnp.right_shift(relative, bit), 1)
    return place


def chunk_place(chunk, order, levels):
    target = sum((((chunk >> (levels - 1 - k)) & 1) << bit) for k, bit in enumerate(order[:levels]))
    return place_of(target, order[:levels])


def small_rows(experts):
    return [0, 2, 4, 16, 16 + experts, 16 + 2 * experts]


def backward_kernel(
    heads,
    orders,
    levels,
    wait,
    flush,
    returned_ref,
    returned_other_ref,
    fetch_ref,
    fetch_other_ref,
    middle_ref,
    middle_other_ref,
    cot_ref,
    cot_other_ref,
    gain_second_ref,
    mixed_own_ref,
    mixed_other_ref,
    value_ref,
    probs_ref,
    key_ref,
    query_ref,
    act_ref,
    hot_ref,
    own_ref,
    other_ref,
    router_ref,
    after_ref,
    wo_ref,
    wq_ref,
    wk_ref,
    wv_ref,
    keep_0_ref,
    send_0_ref,
    keep_1_ref,
    send_1_ref,
    keep_2_ref,
    send_2_ref,
    grad_middle_ref,
    small_ref,
    input_own_ref,
    input_other_ref,
    wo_half,
    wq_half,
    wk_half,
    wv_half,
    part_0,
    part_1,
    part_2,
    small,
    sems,
):
    rows, width = middle_ref.shape
    size = width // heads
    part = width // 2
    experts = router_ref.shape[0]
    scale = 1.0 / math.sqrt(size)
    core = lax.axis_index("ffn")
    span = pl.ds(pl.multiple_of(core * part, LANES), part)
    copies = [
        pltpu.make_async_copy(src, half, sems.at[6 + i])
        for i, (src, half) in enumerate(
            (
                (wo_ref.at[span, :], wo_half),
                (wq_ref.at[:, span], wq_half),
                (wk_ref.at[:, span], wk_half),
                (wv_ref.at[:, span], wv_half),
            )
        )
    ]
    for copy in copies:
        copy.start()
    parts = (part_0, part_1, part_2)
    halves = ((keep_0_ref, send_0_ref), (keep_1_ref, send_1_ref), (keep_2_ref, send_2_ref))
    third = width // 3
    height = third >> levels
    writes = []
    for p, pair in enumerate(halves):
        rows_half = pair[0].shape[0]
        for i, ref in enumerate(pair):
            writes.append(
                pltpu.make_async_copy(
                    parts[p].at[pl.ds(i * rows_half, rows_half), :], ref, sems.at[2 * p + i]
                )
            )
    places = [
        [chunk_place(chunk, order, levels) * (4 * height) for chunk in range(2**levels)]
        for order in orders
    ]

    def pack(matrix, value):
        for p, ref in enumerate(parts):
            for chunk in range(2**levels):
                first = p * third + chunk * height
                at = pl.multiple_of(places[p][chunk] + matrix * height, 16)
                ref[pl.ds(at, height), :] = value[first : first + height]

    for i in range(9):
        wait(i)
    copies[0].wait()
    gain = gain_second_ref[...].reshape(1, width)
    grad_own, gain_terms = middle_back(
        returned_ref[...], fetch_ref[...], middle_ref[...], gain, cot_ref[...]
    )
    grad_other, _ = middle_back(
        returned_other_ref[...], fetch_other_ref[...], middle_other_ref[...], gain, cot_other_ref[...]
    )
    gain_second = jnp.sum(gain_terms, axis=0, keepdims=True)
    grad_middle_ref[...] = grad_own
    flush(6)
    grad_low = jnp.concatenate([grad_own, grad_other], axis=0).astype(BF16)
    grad_mixed = cols_by_cols(grad_low, wo_half[...]).astype(BF16)
    for i in range(9, 20):
        wait(i)
    for copy in copies[1:]:
        copy.wait()
    mixed = jnp.concatenate([mixed_own_ref[...], mixed_other_ref[...]], axis=0)
    grad_columns = jnp.where(core == 0, grad_low[:, :part], grad_low[:, part:])
    pack(3, rows_by_rows(mixed, grad_columns).astype(BF16))
    low_half = lax.broadcasted_iota(jnp.int32, (2 * rows, 2 * size), 1) < size
    grad_q, grad_k, grad_v = [], [], []
    same, ahead, behind = [], [], []
    for pair in range(heads // 4):
        lanes = slice(pair * 2 * size, (pair + 1) * 2 * size)
        query, key, value = query_ref[:, lanes], key_ref[:, lanes], value_ref[:, lanes]
        grad_pair = grad_mixed[:, lanes]
        got_q, got_k, got_v = [], [], []
        for side in range(2):
            probs = probs_ref[2 * pair + side]
            keep_lanes = low_half if side == 0 else jnp.logical_not(low_half)
            own_grad = jnp.where(keep_lanes, grad_pair, 0).astype(BF16)
            grad_probs = cols_by_cols(own_grad, value)
            got_v.append(rows_by_rows(probs.astype(BF16), grad_pair))
            inner = jnp.sum(probs * grad_probs, axis=-1, keepdims=True)
            grad_scores = probs * (grad_probs - inner)
            same.append(
                diagonal_sums(grad_scores[:rows, :rows] + grad_scores[rows:, rows:], rows)
            )
            first = diagonal_sums(grad_scores[:rows, rows:], rows)
            second = diagonal_sums(grad_scores[rows:, :rows], rows)
            ahead.append(jnp.where(core == 1, first, second))
            behind.append(jnp.where(core == 1, second, first))
            grad_raw = (grad_scores * scale).astype(BF16)
            got_q.append(dot(grad_raw, key))
            got_k.append(rows_by_rows(grad_raw, query))
        grad_q.append(jnp.where(low_half, got_q[0], got_q[1]).astype(BF16))
        grad_k.append(jnp.where(low_half, got_k[0], got_k[1]).astype(BF16))
        grad_v.append(jnp.where(low_half, got_v[0], got_v[1]).astype(BF16))
    grad_q = jnp.concatenate(grad_q, axis=1)
    grad_k = jnp.concatenate(grad_k, axis=1)
    grad_v = jnp.concatenate(grad_v, axis=1)
    act = act_ref[...]
    pack(0, rows_by_rows(act, grad_q).astype(BF16))
    pack(1, rows_by_rows(act, grad_k).astype(BF16))
    pack(2, rows_by_rows(act, grad_v).astype(BF16))
    for write in writes:
        write.start()
    grad_act = (
        cols_by_cols(grad_q, wq_half[...])
        + cols_by_cols(grad_k, wk_half[...])
        + cols_by_cols(grad_v, wv_half[...])
    )
    input_other_ref[...] = grad_act[rows:].astype(BF16)
    flush(9)
    input_own_ref[...] = grad_act[:rows]
    flush(8)
    x = own_ref[...].astype(F32)
    y = other_ref[...].astype(F32)
    gain_first = jnp.sum(
        grad_act[:rows] * (x * root_mean(x)) + grad_act[rows:] * (y * root_mean(y)),
        axis=0,
        keepdims=True,
    )
    sums = jnp.concatenate(
        [jnp.concatenate(part_sums, axis=0) for part_sums in (same, ahead, behind)], axis=1
    )
    table = lax.dot_general(
        sums,
        hot_ref[...],
        (((1,), (1,)), ((), ())),
        precision=TOP_PRECISION,
        preferred_element_type=F32,
    )
    at = small_rows(experts)
    small[: at[3]] = jnp.zeros((at[3], part), F32)
    for i, value in enumerate((gain_first, gain_second)):
        small[at[i] : at[i] + 1] = value[:, :part]
        small[at[i] + 1 : at[i] + 2] = value[:, part:]
    small[at[2] : at[2] + heads // 2, : table.shape[1]] = table
    small[at[3] : at[4]] = router_ref[:, :part]
    small[at[4] : at[5]] = router_ref[:, part:]
    small_ref[...] = small[...].astype(BF16)
    flush(7)
    for write in writes:
        write.wait()


def assemble_kernel(orders, levels, sides, upper, last, wait, flush, *refs):
    count = len(orders) * len(sides)
    arrays, refs = refs[:count], refs[count:]
    if last is not None:
        experts, heads = last
        (small_own_ref, small_other_ref), refs = refs[:2], refs[2:]
    if upper:
        refs = refs[4:]
    outs, (wide, sems) = refs[:4], refs[-2:]
    if last is not None:
        gain_first_ref, gain_second_ref, table_ref, router_ref = refs[4:8]
    width = outs[0].shape[1]
    part = width // 2
    third = width // 3
    span = third // 2
    height = third >> levels
    half = 2 ** (levels - 1)
    core = lax.axis_index("ffn")
    mine = lax.axis_index("expert")
    columns = [
        pl.ds(pl.multiple_of((1 - core if side else core) * part, LANES), part) for side in sides
    ]
    writes = []
    for p, order in enumerate(orders):
        for i in range(len(sides)):
            wait(len(sides) * p + i)
        for low in range(half):
            place = jnp.bitwise_and(chunk_place(low, order, levels), half - 1)
            for matrix in range(4):
                at = pl.ds(pl.multiple_of((place * 4 + matrix) * height, height), height)
                to = pl.ds(low * height, height)
                for i in range(len(sides)):
                    lanes = columns[i] if len(sides) == 2 else slice(None)
                    wide[p, matrix, to, lanes] = arrays[len(sides) * p + i][at, :].astype(F32)
        bit = jnp.bitwise_and(jnp.right_shift(mine, order[0]), 1)
        if upper:
            bit = 1 - bit
        first = pl.multiple_of(p * third + bit * span, span)
        for matrix in range(4):
            target = outs[matrix].at[pl.ds(first, span), :]
            if len(sides) == 1:
                target = outs[matrix].at[pl.ds(first, span), columns[0]]
            write = pltpu.make_async_copy(wide.at[p, matrix], target, sems.at[4 * p + matrix])
            write.start()
            writes.append(write)
    if last is not None:
        at = small_rows(experts)
        mine, other = small_own_ref[...], small_other_ref[...]
        both = mine + other
        gain_first_ref[...] = jnp.concatenate([both[0:1], both[1:2]], axis=1).reshape(width)
        gain_second_ref[...] = jnp.concatenate([both[2:3], both[3:4]], axis=1).reshape(width)
        buckets = table_ref.shape[1]
        low = mine[at[2] : at[2] + heads // 2, :buckets]
        high = other[at[2] : at[2] + heads // 2, :buckets]
        table_ref[...] = jnp.where(
            core == 0,
            jnp.concatenate([low, high], axis=0),
            jnp.concatenate([high, low], axis=0),
        )
        router_ref[...] = jnp.concatenate([both[at[3] : at[4]], both[at[4] : at[5]]], axis=1)
    for write in writes:
        write.wait()


def assemble(orders, levels, sides, arrays, width, earlier=(), smalls=(), last=None):
    tail = []
    modes = "l" * len(arrays)
    if last is not None:
        experts, heads, buckets = last
        tail = [((width,), F32), ((width,), F32), ((heads, buckets), F32), ((experts, width), F32)]
        modes += "hh"
        last = (experts, heads)
    first = len(modes)
    modes += "r" * len(earlier)
    columns = width * len(sides) // 2
    return call(
        functools.partial(assemble_kernel, orders, levels, sides, bool(earlier), last),
        [((width, width), F32)] * 4 + tail,
        (*arrays, *smalls, *earlier),
        modes + "rrrr" + "h" * len(tail),
        vmem=16,
        aliases={first + i: i for i in range(len(earlier))},
        scratch=[
            pltpu.VMEM((len(orders), 4, width // 6, columns), F32),
            pltpu.SemaphoreType.DMA((4 * len(orders),)),
        ],
        nbytes=8000000,
    )


def swap(x):
    return lax.ppermute(x, "ffn", [(0, 1), (1, 0)])


def flip(x, bit):
    peers = lax.axis_size("expert")
    return lax.ppermute(x, "expert", [(i, i ^ (1 << bit)) for i in range(peers)])


def add_low(left, right):
    return (left.astype(F32) + right.astype(F32)).astype(BF16)


def sum_over_chips(keeps, sends, orders, levels, small, beside):
    count = len(orders[0])
    todo = set(orders[0])
    ridden = set()

    def exchange(phase, x, bit):
        nonlocal small
        if bit not in todo or phase in ridden or phase < 2 or phase > 2 * count - 3:
            return flip(x, bit)
        todo.discard(bit)
        ridden.add(phase)
        got = flip(jnp.concatenate([x, small.astype(BF16)]), bit)
        rows = x.shape[0]
        small = small.astype(F32) + got[rows:].astype(F32)
        return got[:rows]

    def mine(bit):
        return (lax.axis_index("expert") >> bit) & 1

    whole = [None] * len(orders)
    for k in range(count - 1):
        for p, order in enumerate(orders):
            keep, got = keeps[p], exchange(k, sends[p], order[k])
            half = keep.shape[0] // 2
            if k + 2 == count:
                whole[p] = add_low(keep, got)
            elif k + 1 < levels:
                keeps[p] = add_low(keep[:half], got[:half])
                sends[p] = add_low(keep[half:], got[half:])
            else:
                both = add_low(keep, got)
                upper = mine(order[k + 1])
                keeps[p] = lax.dynamic_slice_in_dim(both, upper * half, half, 0)
                sends[p] = lax.dynamic_slice_in_dim(both, (1 - upper) * half, half, 0)
    for p, order in enumerate(orders):
        x = whole[p]
        whole[p] = add_low(x, exchange(count - 1, x, order[-1]))
    got = [None] * len(orders)
    for k in reversed(range(count - 1)):
        for p, order in enumerate(orders):
            x = whole[p]
            got[p] = exchange(2 * count - 2 - k, x, order[k])
            if k == 0:
                continue
            if k < levels:
                whole[p] = jnp.concatenate([x, got[p]])
            else:
                whole[p] = jnp.where(
                    mine(order[k]) == 1,
                    jnp.concatenate([got[p], x]),
                    jnp.concatenate([x, got[p]]),
                )
    for bit in sorted(todo):
        small = small.astype(F32) + flip(small, bit).astype(F32)
    return whole, got, small, beside


def shards(
    tokens,
    norm_first,
    w_query,
    w_key,
    w_value,
    w_out,
    bucket_bias_table,
    norm_second,
    w_router,
    w_in,
    w_down,
    expert_ids,
    cotangent,
):
    rows, width = tokens.shape
    buckets, heads = bucket_bias_table.shape
    pair = lax.axis_size("ffn")
    experts = w_router.shape[1]
    total = 2 * rows
    capacity = 5 * rows * pair // 4
    hidden = w_in.shape[2]
    part = width // 2
    hot = jnp.asarray(bucket_windows(rows, buckets, REACH))
    router = w_router.T

    other = swap(tokens)
    ids = expert_ids.reshape(1, rows)
    ids_other = swap(ids)
    other, ids_other, w_in, w_down, cotangent = lax.optimization_barrier(
        (other, ids_other, w_in, w_down, cotangent)
    )
    in_own, down_own = w_in[0], w_down[0]
    in_other, down_other = swap(in_own), swap(down_own)
    cot_other = swap(cotangent)
    middle, gate, outgoing, mixed, windows, fetch, fetch_other, root = call(
        functools.partial(forward_kernel, heads),
        [
            ((rows, width), F32),
            ((rows, LANES), F32),
            ((total, 2 * width + LANES), BF16),
            ((rows, width), BF16),
            ((heads, 6 * rows), F32),
            ((rows, total), BF16),
            ((rows, total), BF16),
            ((rows, LANES), F32),
        ],
        (
            tokens,
            other,
            norm_first,
            ids,
            ids_other,
            bucket_bias_table.T,
            hot,
            w_key,
            w_value,
            w_query,
            w_out,
            norm_second,
            router,
            cotangent,
        ),
        "hhhhhhhlllllll" + "hhhhhhhh",
        vmem=64,
        flops=3000000000,
        scratch=[pltpu.VMEM((heads, rows, 2 * rows), F32)],
    )
    arrived = lax.all_to_all(outgoing, "expert", 0, 0, tiled=True)
    mixed_other, middle_other = swap(mixed), swap(middle)
    act, queries, keys, values, probs = call(
        functools.partial(halves_kernel, heads),
        [
            ((2 * rows, width), BF16),
            ((2 * rows, part), BF16),
            ((2 * rows, part), BF16),
            ((2 * rows, part), BF16),
            ((heads // 2, 2 * rows, 2 * rows), F32),
        ],
        (tokens, other, norm_first, w_query, w_key, w_value, windows, gate),
        "hhhrrrhr" + "hhhhh",
        vmem=64,
        flops=3000000000,
        scratch=[pltpu.VMEM((width, part), BF16)] * 3 + [pltpu.SemaphoreType.DMA((3,))],
    )
    chunk = hidden // 2
    steps = 2 * hidden // chunk
    hid_own, pre_own, sent, bundle, grad_slots, produced, router_part = call(
        functools.partial(expert_kernel, capacity, chunk),
        [
            ((total, hidden), BF16),
            ((total, hidden), BF16),
            ((total, width), BF16),
            ((total, 2 * width + 2 * hidden), BF16),
            ((total, width), BF16),
            ((total, width), BF16),
            ((experts, width), F32),
        ],
        (arrived, router, in_own, in_other, down_own, down_other, act),
        "llrrrrr" + "hhhrhhh",
        vmem=64,
        flops=6000000000,
        scratch=[
            pltpu.VMEM((steps, width, chunk), BF16),
            pltpu.VMEM((steps, chunk, width), BF16),
            pltpu.VMEM((total, 2 * width + 2 * hidden), BF16),
            pltpu.SemaphoreType.DMA((3, steps + 1)),
        ],
    )
    bundle_other = swap(bundle)
    grad_returned = lax.all_to_all(grad_slots, "expert", 0, 0, tiled=True)
    grad_w_in, grad_w_down = expert_weights(arrived, sent, hid_own, pre_own, bundle_other, 256)
    produced, grad_returned, grad_w_in = lax.optimization_barrier(
        (produced, grad_returned, grad_w_in)
    )
    produced_returned = lax.all_to_all(produced, "expert", 0, 0, tiled=True)
    bits = experts.bit_length() - 1
    levels = min(bits - 1, 3)
    rest = list(range(3, bits))
    orders = [[0, 1, 2] + rest, [1, 2, 0] + rest, [2, 0, 1] + rest]
    third = 4 * width // 3
    *halves, grad_middle, small, input_own, input_other = call(
        functools.partial(backward_kernel, heads, orders, levels),
        [((third // 2, part), BF16)] * 6
        + [
            ((rows, width), F32),
            ((16 + 2 * experts, part), BF16),
            ((rows, width), F32),
            ((rows, width), BF16),
        ],
        (
            grad_returned,
            swap(grad_returned),
            fetch,
            fetch_other,
            middle,
            middle_other,
            cotangent,
            cot_other,
            norm_second,
            mixed,
            mixed_other,
            values,
            probs,
            keys,
            queries,
            act,
            hot,
            tokens,
            other,
            router_part,
            grad_w_in,
            w_out,
            w_query,
            w_key,
            w_value,
        ),
        "l" * 20 + "rrrrr" + "rrrrrr" + "hhhh",
        vmem=56,
        flops=4000000000,
        scratch=[
            pltpu.VMEM((part, width), BF16),
            *[pltpu.VMEM((width, part), BF16)] * 3,
            *[pltpu.VMEM((third, part), BF16)] * 3,
            pltpu.VMEM((16 + 2 * experts, part), F32),
            pltpu.SemaphoreType.DMA((10,)),
        ],
    )
    keeps, grad_middle, small, input_own, input_other, produced_returned = (
        lax.optimization_barrier(
            (halves[0::2], grad_middle, small, input_own, input_other, produced_returned)
        )
    )
    beside = (grad_middle, input_own, swap(input_other), produced_returned)
    kept, got, small, beside = sum_over_chips(
        list(keeps), list(halves[1::2]), orders, levels, small, beside
    )
    grad_middle, input_own, input_swapped, produced_returned = beside
    root = root[:, :1]
    scaled = tokens.astype(F32) * root
    up = norm_first * (input_own + input_swapped.astype(F32))
    grad_input = grad_middle + root * (
        up - scaled * jnp.mean(up * scaled, axis=-1, keepdims=True)
    )
    expert_branch = gate[:, :1] * dot(fetch, produced_returned)
    output = (middle + expert_branch).astype(BF16)
    near = []
    for rows_kept in kept:
        near += [rows_kept, swap(rows_kept)]
    matrices = assemble(orders, levels, (0, 1), near, width)
    small_other = swap(small)
    got, matrices, small, small_other, output, expert_branch, grad_input = (
        lax.optimization_barrier(
            (got, matrices, small, small_other, output, expert_branch, grad_input)
        )
    )
    far = [swap(rows_got) for rows_got in got]
    matrices = assemble(orders, levels, (0,), got, width, matrices)
    results = assemble(
        orders,
        levels,
        (1,),
        far,
        width,
        matrices,
        (small, small_other),
        (experts, heads, buckets),
    )
    return (
        output,
        grad_input,
        results[4],
        results[0],
        results[1],
        results[2],
        results[3],
        results[6].T,
        results[5],
        results[7].T,
        grad_w_in,
        grad_w_down,
        expert_branch,
    )


def solution(mesh):
    placed = (
        P(("expert", "ffn"), None),
        P(),
        P(),
        P(),
        P(),
        P(),
        P(),
        P(),
        P(),
        P("expert", None, "ffn"),
        P("expert", "ffn", None),
        P(("expert", "ffn")),
        P(("expert", "ffn"), None),
    )
    return jax.shard_map(
        shards,
        mesh=mesh,
        in_specs=placed,
        out_specs=(
            P(("expert", "ffn"), None),
            P(("expert", "ffn"), None),
            P(),
            P(),
            P(),
            P(),
            P(),
            P(),
            P(),
            P(),
            P("expert", None, "ffn"),
            P("expert", "ffn", None),
            P(("expert", "ffn"), None),
        ),
        check_vma=False,
    )
```

```python
import functools
import math

import jax
import jax.numpy as jnp
import numpy as np
from jax import lax
from jax.experimental import pallas as pl
from jax.experimental.pallas import tpu as pltpu
from jax.sharding import PartitionSpec as P

REACH = 128
EPS = 1e-06
TOP_PRECISION = lax.Precision.HIGHEST
LANES = 128
F32 = jnp.float32
BF16 = jnp.bfloat16


def bucket_of(distance, buckets, reach):
    half = buckets // 2
    exact = half // 2
    result = np.where(distance < 0, half, 0)
    magnitude = np.abs(distance)
    spread = exact + np.floor(
        np.log(np.maximum(magnitude, 1) / exact) / np.log(reach / exact) * (half - exact)
    )
    spread = np.minimum(spread, half - 1)
    return result + np.where(magnitude < exact, magnitude, spread)


def bucket_windows(rows, buckets, reach):
    lane = np.arange(2 * rows)
    offset = np.where(lane < rows, -lane, 2 * rows - lane)
    windows = []
    for shift in (0, rows, -rows):
        hot = bucket_of(offset + shift, buckets, reach)[None, :] == np.arange(buckets)[:, None]
        hot[:, rows] = False
        windows.append(hot)
    return np.concatenate(windows, axis=1).astype(np.float32)


def rows_by_rows(left, right):
    return lax.dot_general(left, right, (((0,), (0,)), ((), ())), preferred_element_type=F32)


def cols_by_cols(left, right):
    return lax.dot_general(left, right, (((1,), (1,)), ((), ())), preferred_element_type=F32)


def dot(left, right):
    return jnp.dot(left, right, preferred_element_type=F32)


def root_mean(x):
    return lax.rsqrt(jnp.mean(x * x, axis=-1, keepdims=True) + EPS)


def call(body, outs, args, modes, vmem=16, flops=0, scratch=(), aliases=None, nbytes=1000000):
    count, total = len(args), len(args) + len(outs)
    shapes = [(a.shape, a.dtype) for a in args] + list(outs)
    moved = [i for i in range(total) if modes[i] in "hls"]
    buffers = [pltpu.VMEM(*shapes[i]) for i in moved]

    def kernel(*refs):
        bodies = list(refs[:total])
        for i, ref in zip(moved, refs[total : total + len(moved)]):
            bodies[i] = ref
        extra = refs[total + len(moved) : -1]
        sems = refs[-1]
        copies = {}
        for i in moved:
            ends = (refs[i], bodies[i]) if i < count else (bodies[i], refs[i])
            copies[i] = pltpu.make_async_copy(*ends, sems.at[i])
        for i in moved:
            if i < count and modes[i] != "s":
                copies[i].start()
        flushed = set()

        def wait(i):
            copies[i].wait()

        wait.start = lambda i: copies[i].start()

        def flush(i):
            flushed.add(i)
            copies[count + i].start()

        for i in moved:
            if i < count and modes[i] == "h":
                wait(i)
        body(wait, flush, *bodies, *extra)
        for i in moved:
            if i >= count and i - count not in flushed:
                copies[i].start()
        for i in moved:
            if i >= count:
                copies[i].wait()

    specs = [pl.BlockSpec(memory_space=pltpu.HBM)] * total
    return pl.pallas_call(
        kernel,
        out_shape=[jax.ShapeDtypeStruct(s, d) for s, d in outs],
        in_specs=specs[:count],
        out_specs=specs[count:],
        scratch_shapes=buffers + list(scratch) + [pltpu.SemaphoreType.DMA((total,))],
        input_output_aliases=aliases or {},
        compiler_params=pltpu.CompilerParams(vmem_limit_bytes=vmem * 2**20),
        cost_estimate=pl.CostEstimate(flops=flops, bytes_accessed=nbytes, transcendentals=0),
    )(*args)


def toeplitz(window, rows):
    wide = jnp.broadcast_to(window, (rows, 2 * rows))
    return pltpu.roll(wide, 0, 1, stride=1, stride_axis=0)[:, :rows]


def diagonal_sums(square, rows):
    wide = jnp.concatenate([square, jnp.zeros_like(square)], axis=1)
    height = rows
    while height > 1:
        height //= 2
        wide = wide[:height] + pltpu.roll(wide[height:], 2 * rows - height, 1)
    return wide


def placement(ids, experts, total):
    rows = ids.shape[1]
    slots = total // experts
    choose = (lax.broadcasted_iota(jnp.int32, (experts, rows), 0) == ids).astype(F32)
    earlier = (
        lax.broadcasted_iota(jnp.int32, (rows, rows), 0)
        < lax.broadcasted_iota(jnp.int32, (rows, rows), 1)
    ).astype(F32)
    ranks = dot(choose.astype(BF16), earlier.astype(BF16))
    rank = jnp.sum(choose * ranks, axis=0, keepdims=True)
    target = ids * slots + rank.astype(jnp.int32)
    place = (lax.broadcasted_iota(jnp.int32, (total, rows), 0) == target).astype(F32)
    return choose, place


def attend(query_pair, key_pair, scale, bias, side, low_half):
    own = jnp.where(low_half if side == 0 else jnp.logical_not(low_half), query_pair, 0)
    scores = cols_by_cols(own.astype(BF16), key_pair) * scale + bias
    grown = jnp.exp(scores - jnp.max(scores, axis=-1, keepdims=True))
    return grown * (1.0 / jnp.sum(grown, axis=-1, keepdims=True))


def forward_kernel(
    heads,
    wait,
    flush,
    own_ref,
    other_ref,
    gain_first_ref,
    ids_ref,
    ids_other_ref,
    table_ref,
    hot_ref,
    wk,
    wv,
    wq,
    wo,
    gain_second_ref,
    router_ref,
    cot_ref,
    middle_ref,
    gate_ref,
    out_ref,
    mixed_ref,
    win_ref,
    fetch_ref,
    fetch_other_ref,
    root_ref,
    bias,
):
    rows, width = own_ref.shape
    size = width // heads
    scale = 1.0 / math.sqrt(size)
    core = lax.axis_index("ffn")
    total = out_ref.shape[0]
    experts = router_ref.shape[0]
    choose, place = placement(ids_ref[...], experts, total)
    _, place_other = placement(ids_other_ref[...], experts, total)
    fetch_ref[...] = place.T.astype(BF16)
    fetch_other_ref[...] = place_other.T.astype(BF16)
    choose = choose.T
    lane = lax.broadcasted_iota(jnp.int32, (total, LANES), 1)
    out_ref[:, 2 * width :] = jnp.where(
        lane == 0,
        jnp.sum(place, axis=1, keepdims=True),
        jnp.sum(place_other, axis=1, keepdims=True),
    ).astype(BF16)
    place = place.astype(BF16)
    windows = jnp.dot(
        table_ref[...], hot_ref[...], precision=TOP_PRECISION, preferred_element_type=F32
    )
    win_ref[...] = windows
    for i in (4, 5, 6):
        flush(i)
    same = windows[:, : 2 * rows]
    apart = jnp.where(core == 1, windows[:, 2 * rows : 4 * rows], windows[:, 4 * rows :])
    for head in range(heads):
        bias[head, :, :rows] = toeplitz(same[head : head + 1], rows)
        bias[head, :, rows:] = toeplitz(apart[head : head + 1], rows)
    x = own_ref[...].astype(F32)
    y = other_ref[...].astype(F32)
    gain = gain_first_ref[...].reshape(1, width)
    root = root_mean(x)
    root_ref[...] = jnp.broadcast_to(root, root_ref.shape)
    flush(7)
    act_own = (x * root * gain).astype(BF16)
    act_other = (y * root_mean(y) * gain).astype(BF16)
    act = jnp.concatenate([act_own, act_other], axis=0)
    wait(7)
    keys = dot(act, wk[...]).astype(BF16)
    wait(8)
    values = dot(act, wv[...]).astype(BF16)
    wait(9)
    queries = dot(act_own, wq[...]).astype(BF16)
    low_half = lax.broadcasted_iota(jnp.int32, (rows, 2 * size), 1) < size
    mixed = []
    for pair in range(heads // 2):
        lanes = slice(pair * 2 * size, (pair + 1) * 2 * size)
        outs = []
        for side in range(2):
            probs = attend(
                queries[:, lanes], keys[:, lanes], scale, bias[2 * pair + side], side, low_half
            )
            outs.append(dot(probs.astype(BF16), values[:, lanes]))
        mixed.append(jnp.where(low_half, outs[0], outs[1]).astype(BF16))
    mixed = jnp.concatenate(mixed, axis=1)
    mixed_ref[...] = mixed
    flush(3)
    for i in (10, 11, 12, 13):
        wait(i)
    out_ref[:, width : 2 * width] = dot(place, cot_ref[...]).astype(BF16)
    middle = x + dot(mixed, wo[...])
    middle_ref[...] = middle
    flush(0)
    gain_second = gain_second_ref[...].reshape(1, width)
    act_second = (middle * root_mean(middle) * gain_second).astype(BF16)
    logits = cols_by_cols(act_second, router_ref[...])
    grown = jnp.exp(logits - jnp.max(logits, axis=-1, keepdims=True))
    gate = jnp.sum(grown * choose, axis=-1, keepdims=True) / jnp.sum(
        grown, axis=-1, keepdims=True
    )
    gate_ref[...] = jnp.broadcast_to(gate, gate_ref.shape)
    out_ref[:, :width] = dot(place, act_second).astype(BF16)


def halves_kernel(
    heads,
    wait,
    flush,
    own_ref,
    other_ref,
    gain_first_ref,
    wq_ref,
    wk_ref,
    wv_ref,
    win_ref,
    after_ref,
    act_ref,
    query_ref,
    key_ref,
    value_ref,
    probs_ref,
    wq_half,
    wk_half,
    wv_half,
    sems,
):
    rows, width = own_ref.shape
    size = width // heads
    part = width // 2
    scale = 1.0 / math.sqrt(size)
    core = lax.axis_index("ffn")
    columns = pl.ds(pl.multiple_of(core * part, LANES), part)
    copies = [
        pltpu.make_async_copy(ref.at[:, columns], half, sems.at[i])
        for i, (ref, half) in enumerate(((wq_ref, wq_half), (wk_ref, wk_half), (wv_ref, wv_half)))
    ]
    for copy in copies:
        copy.start()
    x = own_ref[...].astype(F32)
    y = other_ref[...].astype(F32)
    gain = gain_first_ref[...].reshape(1, width)
    act = jnp.concatenate(
        [(x * root_mean(x) * gain).astype(BF16), (y * root_mean(y) * gain).astype(BF16)], axis=0
    )
    act_ref[...] = act
    for copy in copies:
        copy.wait()
    queries = dot(act, wq_half[...]).astype(BF16)
    keys = dot(act, wk_half[...]).astype(BF16)
    values = dot(act, wv_half[...]).astype(BF16)
    query_ref[...] = queries
    key_ref[...] = keys
    value_ref[...] = values
    for i in range(4):
        flush(i)
    low_half = lax.broadcasted_iota(jnp.int32, (2 * rows, 2 * size), 1) < size
    for pair in range(heads // 4):
        lanes = slice(pair * 2 * size, (pair + 1) * 2 * size)
        for side in range(2):
            head = 2 * pair + side
            window = win_ref[pl.ds(core * (heads // 2) + head, 1), :]
            same = toeplitz(window[:, : 2 * rows], rows)
            ahead = toeplitz(window[:, 2 * rows : 4 * rows], rows)
            behind = toeplitz(window[:, 4 * rows :], rows)
            first = jnp.where(core == 1, ahead, behind)
            second = jnp.where(core == 1, behind, ahead)
            bias = jnp.concatenate(
                [
                    jnp.concatenate([same, first], axis=1),
                    jnp.concatenate([second, same], axis=1),
                ],
                axis=0,
            )
            probs_ref[head] = attend(
                queries[:, lanes], keys[:, lanes], scale, bias, side, low_half
            )


def expert_kernel(
    capacity,
    chunk,
    wait,
    flush,
    arrived_ref,
    router_ref,
    in_own_ref,
    in_other_ref,
    down_own_ref,
    down_other_ref,
    after_ref,
    hid_own_ref,
    pre_own_ref,
    sent_ref,
    bundle_ref,
    grad_ref,
    produced_ref,
    router_grad_ref,
    in_vmem,
    down_vmem,
    bundle,
    sems,
):
    total = arrived_ref.shape[0]
    experts, width = router_ref.shape
    slots = total // experts
    hidden = in_own_ref.shape[1]
    steps = hidden // chunk
    mine = lax.axis_index("expert")
    core = lax.axis_index("ffn")
    copies = []
    for side, (win, wdown) in enumerate(
        ((in_own_ref, down_own_ref), (in_other_ref, down_other_ref))
    ):
        for step in range(steps):
            i = side * steps + step
            span = pl.ds(step * chunk, chunk)
            copies.append(
                (
                    pltpu.make_async_copy(win.at[:, span], in_vmem.at[i], sems.at[0, i]),
                    pltpu.make_async_copy(wdown.at[span, :], down_vmem.at[i], sems.at[1, i]),
                )
            )
    for copy in copies[0]:
        copy.start()
    for i in (0, 1):
        wait(i)
    for pair in copies[1:]:
        for copy in pair:
            copy.start()
    flat = arrived_ref[:, :width]
    cot = arrived_ref[:, width : 2 * width]
    filled = arrived_ref[:, 2 * width :]
    row = lax.broadcasted_iota(jnp.int32, (total, total), 0)
    col = lax.broadcasted_iota(jnp.int32, (total, total), 1)
    shift = slots.bit_length() - 1
    row_block = jnp.right_shift(row, shift)
    col_block = jnp.right_shift(col, shift)
    before = (col_block < row_block).astype(F32).astype(BF16)
    ahead = (col_block < row_block + core).astype(F32).astype(BF16)
    slot = jnp.bitwise_and(lax.broadcasted_iota(jnp.int32, (total, 1), 0), slots - 1)
    position = dot(before, filled)[:, 0:1] + dot(ahead, filled)[:, 1:2] + slot.astype(F32)
    keep = jnp.where(position < capacity, 1.0, 0.0)
    logits = cols_by_cols(flat, router_ref[...])
    grown = jnp.exp(logits - jnp.max(logits, axis=-1, keepdims=True))
    router_probs = grown / jnp.sum(grown, axis=-1, keepdims=True)
    onehot = (lax.broadcasted_iota(jnp.int32, (total, experts), 1) == mine).astype(F32)
    gate = jnp.sum(router_probs * onehot, axis=-1, keepdims=True)
    sent = (cot.astype(F32) * (gate * keep)).astype(BF16)
    sent_ref[...] = sent
    flush(2)
    bundle[:, :width] = flat
    bundle[:, width : 2 * width] = sent
    writes = []

    def forward(first, size):
        span = pl.ds(first, size)
        write = pltpu.make_async_copy(
            bundle.at[:, span], bundle_ref.at[:, span], sems.at[2, len(writes)]
        )
        write.start()
        writes.append(write)

    forward(0, 2 * width)
    produced = jnp.zeros((total, width), F32)
    grad = jnp.zeros((total, width), F32)
    inner = math.sqrt(2.0 / math.pi)
    for i, pair in enumerate(copies):
        own_side = i < steps
        first = (i % steps) * chunk
        for copy in pair:
            copy.wait()
        win, wdown = in_vmem[i], down_vmem[i]
        pre = dot(flat, win)
        square = pre * pre
        curve = jnp.tanh(inner * pre * (1.0 + 0.044715 * square))
        half_up = 0.5 + 0.5 * curve
        act = (pre * half_up).astype(BF16)
        slope = half_up + (0.5 * inner) * pre * (1.0 - curve * curve) * (
            1.0 + (3 * 0.044715) * square
        )
        grad_pre = (slope * cols_by_cols(sent, wdown)).astype(BF16)
        if own_side:
            hid_own_ref[:, first : first + chunk] = act
            pre_own_ref[:, first : first + chunk] = grad_pre
        else:
            first += 2 * width
            bundle[:, first : first + chunk] = act
            bundle[:, first + hidden : first + hidden + chunk] = grad_pre
            forward(first, chunk)
            forward(first + hidden, chunk)
        if i + 1 == steps:
            flush(0)
            flush(1)
        produced = produced + dot(act, wdown)
        grad = grad + cols_by_cols(grad_pre, win)
    produced_low = produced.astype(BF16)
    kept = produced_low.astype(F32) * keep
    produced_ref[...] = kept.astype(BF16)
    flush(5)
    grad_gate = jnp.sum(cot.astype(F32) * kept, axis=-1, keepdims=True)
    grad_logits = ((grad_gate * gate) * (onehot - router_probs)).astype(BF16)
    grad_ref[...] = (grad * keep + dot(grad_logits, router_ref[...])).astype(BF16)
    flush(4)
    router_grad_ref[...] = rows_by_rows(grad_logits, flat)
    for write in writes:
        write.wait()


def expert_weights_kernel(
    flat_own, sent_own, hid_own, pre_own, flat_other, sent_other, hid_other, pre_other, in_ref, down_ref
):
    in_ref[0] = rows_by_rows(flat_own[...], pre_own[...]) + rows_by_rows(
        flat_other[...], pre_other[...]
    )
    down_ref[0] = rows_by_rows(hid_own[...], sent_own[...]) + rows_by_rows(
        hid_other[...], sent_other[...]
    )


def expert_weights(flat, sent, hid, pre, bundle, chunk):
    total, width = sent.shape
    hidden = hid.shape[1]
    steps = hidden // chunk
    skip = 2 * width // chunk
    whole = pl.BlockSpec((total, width), lambda i: (0, 0))
    second = pl.BlockSpec((total, width), lambda i: (0, 1))
    part = pl.BlockSpec((total, chunk), lambda i: (0, i))
    return pl.pallas_call(
        expert_weights_kernel,
        grid=(steps,),
        out_shape=[
            jax.ShapeDtypeStruct((1, width, hidden), F32),
            jax.ShapeDtypeStruct((1, hidden, width), F32),
        ],
        in_specs=[
            whole,
            whole,
            part,
            part,
            whole,
            second,
            pl.BlockSpec((total, chunk), lambda i: (0, i + skip)),
            pl.BlockSpec((total, chunk), lambda i: (0, i + skip + steps)),
        ],
        out_specs=[
            pl.BlockSpec((1, width, chunk), lambda i: (0, 0, i)),
            pl.BlockSpec((1, chunk, width), lambda i: (0, i, 0)),
        ],
        compiler_params=pltpu.CompilerParams(vmem_limit_bytes=64 * 2**20),
        cost_estimate=pl.CostEstimate(
            flops=8 * total * width * hidden, bytes_accessed=14000000, transcendentals=0
        ),
    )(flat, sent, hid, pre, bundle, bundle, bundle, bundle)


def middle_back(returned, fetch, middle, gain, cot):
    grad = dot(fetch, returned)
    root = root_mean(middle)
    scaled = middle * root
    up = gain * grad
    grad_middle = cot.astype(F32) + root * (
        up - scaled * jnp.mean(up * scaled, axis=-1, keepdims=True)
    )
    return grad_middle, grad * scaled


def bit_of(step, other=0):
    return jnp.where(lax.axis_index("ffn") == other, step[0], step[1])


def chunk_place(chunk, order, levels, other=0):
    chip = lax.axis_index("expert")
    mine = 0
    for step in order[:levels]:
        mine = mine * 2 + jnp.bitwise_and(jnp.right_shift(chip, bit_of(step, other)), 1)
    return jnp.bitwise_xor(mine, chunk)


def small_rows(experts):
    return [0, 2, 4, 16, 16 + experts, 16 + 2 * experts]


def backward_kernel(
    heads,
    orders,
    levels,
    wait,
    flush,
    returned_ref,
    returned_other_ref,
    fetch_ref,
    fetch_other_ref,
    middle_ref,
    middle_other_ref,
    cot_ref,
    cot_other_ref,
    gain_second_ref,
    mixed_own_ref,
    mixed_other_ref,
    value_ref,
    probs_ref,
    key_ref,
    query_ref,
    act_ref,
    hot_ref,
    own_ref,
    other_ref,
    router_ref,
    after_ref,
    wo_ref,
    wq_ref,
    wk_ref,
    wv_ref,
    keep_0_ref,
    send_0_ref,
    keep_1_ref,
    send_1_ref,
    keep_2_ref,
    send_2_ref,
    grad_middle_ref,
    small_ref,
    input_own_ref,
    input_other_ref,
    wo_half,
    wq_half,
    wk_half,
    wv_half,
    part_0,
    part_1,
    part_2,
    small,
    sems,
):
    rows, width = middle_ref.shape
    size = width // heads
    part = width // 2
    experts = router_ref.shape[0]
    scale = 1.0 / math.sqrt(size)
    core = lax.axis_index("ffn")
    span = pl.ds(pl.multiple_of(core * part, LANES), part)
    copies = [
        pltpu.make_async_copy(src, half, sems.at[6 + i])
        for i, (src, half) in enumerate(
            (
                (wo_ref.at[span, :], wo_half),
                (wq_ref.at[:, span], wq_half),
                (wk_ref.at[:, span], wk_half),
                (wv_ref.at[:, span], wv_half),
            )
        )
    ]
    for copy in copies:
        copy.start()
    parts = (part_0, part_1, part_2)
    halves = ((keep_0_ref, send_0_ref), (keep_1_ref, send_1_ref), (keep_2_ref, send_2_ref))
    third = width // 3
    height = third >> levels
    writes = []
    for p, pair in enumerate(halves):
        rows_half = pair[0].shape[0]
        for i, ref in enumerate(pair):
            writes.append(
                pltpu.make_async_copy(
                    parts[p].at[pl.ds(i * rows_half, rows_half), :], ref, sems.at[2 * p + i]
                )
            )
    places = [
        [chunk_place(chunk, order, levels) * (4 * height) for chunk in range(2**levels)]
        for order in orders
    ]

    def pack(matrix, value):
        for p, ref in enumerate(parts):
            for chunk in range(2**levels):
                first = p * third + chunk * height
                at = pl.multiple_of(places[p][chunk] + matrix * height, 16)
                ref[pl.ds(at, height), :] = value[first : first + height]

    for i in range(9):
        wait(i)
    copies[0].wait()
    gain = gain_second_ref[...].reshape(1, width)
    grad_own, gain_terms = middle_back(
        returned_ref[...], fetch_ref[...], middle_ref[...], gain, cot_ref[...]
    )
    grad_other, _ = middle_back(
        returned_other_ref[...], fetch_other_ref[...], middle_other_ref[...], gain, cot_other_ref[...]
    )
    gain_second = jnp.sum(gain_terms, axis=0, keepdims=True)
    grad_middle_ref[...] = grad_own
    flush(6)
    grad_low = jnp.concatenate([grad_own, grad_other], axis=0).astype(BF16)
    grad_mixed = cols_by_cols(grad_low, wo_half[...]).astype(BF16)
    for i in range(9, 20):
        wait(i)
    for copy in copies[1:]:
        copy.wait()
    mixed = jnp.concatenate([mixed_own_ref[...], mixed_other_ref[...]], axis=0)
    grad_columns = jnp.where(core == 0, grad_low[:, :part], grad_low[:, part:])
    pack(3, rows_by_rows(mixed, grad_columns).astype(BF16))
    low_half = lax.broadcasted_iota(jnp.int32, (2 * rows, 2 * size), 1) < size
    grad_q, grad_k, grad_v = [], [], []
    same, ahead, behind = [], [], []
    for pair in range(heads // 4):
        lanes = slice(pair * 2 * size, (pair + 1) * 2 * size)
        query, key, value = query_ref[:, lanes], key_ref[:, lanes], value_ref[:, lanes]
        grad_pair = grad_mixed[:, lanes]
        got_q, got_k, got_v = [], [], []
        for side in range(2):
            probs = probs_ref[2 * pair + side]
            keep_lanes = low_half if side == 0 else jnp.logical_not(low_half)
            own_grad = jnp.where(keep_lanes, grad_pair, 0).astype(BF16)
            grad_probs = cols_by_cols(own_grad, value)
            got_v.append(rows_by_rows(probs.astype(BF16), grad_pair))
            inner = jnp.sum(probs * grad_probs, axis=-1, keepdims=True)
            grad_scores = probs * (grad_probs - inner)
            same.append(
                diagonal_sums(grad_scores[:rows, :rows] + grad_scores[rows:, rows:], rows)
            )
            first = diagonal_sums(grad_scores[:rows, rows:], rows)
            second = diagonal_sums(grad_scores[rows:, :rows], rows)
            ahead.append(jnp.where(core == 1, first, second))
            behind.append(jnp.where(core == 1, second, first))
            grad_raw = (grad_scores * scale).astype(BF16)
            got_q.append(dot(grad_raw, key))
            got_k.append(rows_by_rows(grad_raw, query))
        grad_q.append(jnp.where(low_half, got_q[0], got_q[1]).astype(BF16))
        grad_k.append(jnp.where(low_half, got_k[0], got_k[1]).astype(BF16))
        grad_v.append(jnp.where(low_half, got_v[0], got_v[1]).astype(BF16))
    grad_q = jnp.concatenate(grad_q, axis=1)
    grad_k = jnp.concatenate(grad_k, axis=1)
    grad_v = jnp.concatenate(grad_v, axis=1)
    act = act_ref[...]
    pack(0, rows_by_rows(act, grad_q).astype(BF16))
    pack(1, rows_by_rows(act, grad_k).astype(BF16))
    pack(2, rows_by_rows(act, grad_v).astype(BF16))
    for write in writes:
        write.start()
    grad_act = (
        cols_by_cols(grad_q, wq_half[...])
        + cols_by_cols(grad_k, wk_half[...])
        + cols_by_cols(grad_v, wv_half[...])
    )
    input_other_ref[...] = grad_act[rows:].astype(BF16)
    flush(9)
    input_own_ref[...] = grad_act[:rows]
    flush(8)
    x = own_ref[...].astype(F32)
    y = other_ref[...].astype(F32)
    gain_first = jnp.sum(
        grad_act[:rows] * (x * root_mean(x)) + grad_act[rows:] * (y * root_mean(y)),
        axis=0,
        keepdims=True,
    )
    sums = jnp.concatenate(
        [jnp.concatenate(part_sums, axis=0) for part_sums in (same, ahead, behind)], axis=1
    )
    table = lax.dot_general(
        sums,
        hot_ref[...],
        (((1,), (1,)), ((), ())),
        precision=TOP_PRECISION,
        preferred_element_type=F32,
    )
    at = small_rows(experts)
    small[: at[3]] = jnp.zeros((at[3], part), F32)
    for i, value in enumerate((gain_first, gain_second)):
        small[at[i] : at[i] + 1] = value[:, :part]
        small[at[i] + 1 : at[i] + 2] = value[:, part:]
    small[at[2] : at[2] + heads // 2, : table.shape[1]] = table
    small[at[3] : at[4]] = router_ref[:, :part]
    small[at[4] : at[5]] = router_ref[:, part:]
    small_ref[...] = small[...].astype(BF16)
    flush(7)
    for write in writes:
        write.wait()


def assemble_kernel(orders, levels, sides, upper, last, wait, flush, *refs):
    count = len(orders) * len(sides)
    arrays, refs = refs[:count], refs[count:]
    if last is not None:
        experts, heads = last
        (small_own_ref, small_other_ref), refs = refs[:2], refs[2:]
    if upper:
        refs = refs[4:]
    outs, (wide, sems) = refs[:4], refs[-2:]
    if last is not None:
        gain_first_ref, gain_second_ref, table_ref, router_ref = refs[4:8]
    width = outs[0].shape[1]
    part = width // 2
    third = width // 3
    span = third // 2
    height = third >> levels
    half = 2 ** (levels - 1)
    core = lax.axis_index("ffn")
    mine = lax.axis_index("expert")
    columns = [
        pl.ds(pl.multiple_of((1 - core if side else core) * part, LANES), part) for side in sides
    ]
    writes = []
    for p, order in enumerate(orders):
        for i, side in enumerate(sides):
            n = len(sides) * p + i
            wait(n)
            bit = jnp.bitwise_and(jnp.right_shift(mine, bit_of(order[0], side)), 1)
            if upper:
                bit = 1 - bit
            first = pl.multiple_of(p * third + bit * span, span)
            places = [
                jnp.bitwise_and(chunk_place(low, order, levels, side), half - 1)
                for low in range(half)
            ]
            for matrix in range(4):
                for low in range(half):
                    at = pl.multiple_of((places[low] * 4 + matrix) * height, height)
                    wide[n, matrix, pl.ds(low * height, height)] = arrays[n][
                        pl.ds(at, height), :
                    ].astype(F32)
                write = pltpu.make_async_copy(
                    wide.at[n, matrix],
                    outs[matrix].at[pl.ds(first, span), columns[i]],
                    sems.at[4 * n + matrix],
                )
                write.start()
                writes.append(write)
    if last is not None:
        at = small_rows(experts)
        mine, other = small_own_ref[...], small_other_ref[...]
        both = mine + other
        gain_first_ref[...] = jnp.concatenate([both[0:1], both[1:2]], axis=1).reshape(width)
        gain_second_ref[...] = jnp.concatenate([both[2:3], both[3:4]], axis=1).reshape(width)
        buckets = table_ref.shape[1]
        low = mine[at[2] : at[2] + heads // 2, :buckets]
        high = other[at[2] : at[2] + heads // 2, :buckets]
        table_ref[...] = jnp.where(
            core == 0,
            jnp.concatenate([low, high], axis=0),
            jnp.concatenate([high, low], axis=0),
        )
        router_ref[...] = jnp.concatenate([both[at[3] : at[4]], both[at[4] : at[5]]], axis=1)
    for write in writes:
        write.wait()


def assemble(orders, levels, sides, arrays, width, earlier=(), smalls=(), last=None):
    tail = []
    modes = "l" * len(arrays)
    if last is not None:
        experts, heads, buckets = last
        tail = [((width,), F32), ((width,), F32), ((heads, buckets), F32), ((experts, width), F32)]
        modes += "hh"
        last = (experts, heads)
    first = len(modes)
    modes += "r" * len(earlier)
    return call(
        functools.partial(assemble_kernel, orders, levels, sides, bool(earlier), last),
        [((width, width), F32)] * 4 + tail,
        (*arrays, *smalls, *earlier),
        modes + "rrrr" + "h" * len(tail),
        vmem=16,
        aliases={first + i: i for i in range(len(earlier))},
        scratch=[
            pltpu.VMEM((len(arrays), 4, width // 6, width // 2), F32),
            pltpu.SemaphoreType.DMA((4 * len(arrays),)),
        ],
        nbytes=8000000,
    )


def swap(x):
    return lax.ppermute(x, "ffn", [(0, 1), (1, 0)])


def flip(x, step):
    pairs = []
    for chip in range(lax.axis_size("expert")):
        for core in range(2):
            pairs.append((chip * 2 + core, (chip ^ (1 << step[core])) * 2 + core))
    return lax.ppermute(x, ("expert", "ffn"), pairs)


def add_low(left, right):
    return (left.astype(F32) + right.astype(F32)).astype(BF16)


def sum_over_chips(keeps, sends, orders, levels, small, beside):
    count = len(orders[0])
    todo = [set(step[core] for step in orders[0]) for core in range(2)]
    ridden = set()

    def exchange(phase, x, bit):
        nonlocal small
        fresh = all(bit[core] in todo[core] for core in range(2))
        if not fresh or phase in ridden or phase < 2 or phase > 2 * count - 3:
            return flip(x, bit)
        for core in range(2):
            todo[core].discard(bit[core])
        ridden.add(phase)
        sent = small.astype(BF16)
        got = flip(jnp.concatenate([x, sent]), bit)
        rows = x.shape[0]
        small = sent.astype(F32) + got[rows:].astype(F32)
        return got[:rows]

    def mine(bit):
        return (lax.axis_index("expert") >> bit_of(bit)) & 1

    whole = [None] * len(orders)
    for k in range(count - 1):
        for p, order in enumerate(orders):
            keep, got = keeps[p], exchange(k, sends[p], order[k])
            half = keep.shape[0] // 2
            if k + 2 == count:
                whole[p] = add_low(keep, got)
            elif k + 1 < levels:
                keeps[p] = add_low(keep[:half], got[:half])
                sends[p] = add_low(keep[half:], got[half:])
            else:
                both = add_low(keep, got)
                upper = mine(order[k + 1])
                keeps[p] = lax.dynamic_slice_in_dim(both, upper * half, half, 0)
                sends[p] = lax.dynamic_slice_in_dim(both, (1 - upper) * half, half, 0)
    for p, order in enumerate(orders):
        x = whole[p]
        whole[p] = add_low(x, exchange(count - 1, x, order[-1]))
    got = [None] * len(orders)
    for k in reversed(range(count - 1)):
        for p, order in enumerate(orders):
            x = whole[p]
            got[p] = exchange(2 * count - 2 - k, x, order[k])
            if k == 0:
                continue
            if k < levels:
                whole[p] = jnp.concatenate([x, got[p]])
            else:
                whole[p] = jnp.where(
                    mine(order[k]) == 1,
                    jnp.concatenate([got[p], x]),
                    jnp.concatenate([x, got[p]]),
                )
    for bit in zip(sorted(todo[0]), sorted(todo[1])):
        sent = small.astype(BF16)
        small = sent.astype(F32) + flip(sent, bit).astype(F32)
    return whole, got, small, beside


def shards(
    tokens,
    norm_first,
    w_query,
    w_key,
    w_value,
    w_out,
    bucket_bias_table,
    norm_second,
    w_router,
    w_in,
    w_down,
    expert_ids,
    cotangent,
):
    rows, width = tokens.shape
    buckets, heads = bucket_bias_table.shape
    pair = lax.axis_size("ffn")
    experts = w_router.shape[1]
    total = 2 * rows
    capacity = 5 * rows * pair // 4
    hidden = w_in.shape[2]
    part = width // 2
    hot = jnp.asarray(bucket_windows(rows, buckets, REACH))
    router = w_router.T

    other = swap(tokens)
    ids = expert_ids.reshape(1, rows)
    ids_other = swap(ids)
    other, ids_other, w_in, w_down, cotangent = lax.optimization_barrier(
        (other, ids_other, w_in, w_down, cotangent)
    )
    in_own, down_own = w_in[0], w_down[0]
    in_other, down_other = swap(in_own), swap(down_own)
    cot_other = swap(cotangent)
    middle, gate, outgoing, mixed, windows, fetch, fetch_other, root = call(
        functools.partial(forward_kernel, heads),
        [
            ((rows, width), F32),
            ((rows, LANES), F32),
            ((total, 2 * width + LANES), BF16),
            ((rows, width), BF16),
            ((heads, 6 * rows), F32),
            ((rows, total), BF16),
            ((rows, total), BF16),
            ((rows, LANES), F32),
        ],
        (
            tokens,
            other,
            norm_first,
            ids,
            ids_other,
            bucket_bias_table.T,
            hot,
            w_key,
            w_value,
            w_query,
            w_out,
            norm_second,
            router,
            cotangent,
        ),
        "hhhhhhhlllllll" + "hhhhhhhh",
        vmem=64,
        flops=3000000000,
        scratch=[pltpu.VMEM((heads, rows, 2 * rows), F32)],
    )
    arrived = lax.all_to_all(outgoing, "expert", 0, 0, tiled=True)
    mixed_other, middle_other = swap(mixed), swap(middle)
    act, queries, keys, values, probs = call(
        functools.partial(halves_kernel, heads),
        [
            ((2 * rows, width), BF16),
            ((2 * rows, part), BF16),
            ((2 * rows, part), BF16),
            ((2 * rows, part), BF16),
            ((heads // 2, 2 * rows, 2 * rows), F32),
        ],
        (tokens, other, norm_first, w_query, w_key, w_value, windows, gate),
        "hhhrrrhr" + "hhhhh",
        vmem=64,
        flops=3000000000,
        scratch=[pltpu.VMEM((width, part), BF16)] * 3 + [pltpu.SemaphoreType.DMA((3,))],
    )
    chunk = hidden // 2
    steps = 2 * hidden // chunk
    hid_own, pre_own, sent, bundle, grad_slots, produced, router_part = call(
        functools.partial(expert_kernel, capacity, chunk),
        [
            ((total, hidden), BF16),
            ((total, hidden), BF16),
            ((total, width), BF16),
            ((total, 2 * width + 2 * hidden), BF16),
            ((total, width), BF16),
            ((total, width), BF16),
            ((experts, width), F32),
        ],
        (arrived, router, in_own, in_other, down_own, down_other, act),
        "llrrrrr" + "hhhrhhh",
        vmem=64,
        flops=6000000000,
        scratch=[
            pltpu.VMEM((steps, width, chunk), BF16),
            pltpu.VMEM((steps, chunk, width), BF16),
            pltpu.VMEM((total, 2 * width + 2 * hidden), BF16),
            pltpu.SemaphoreType.DMA((3, steps + 1)),
        ],
    )
    bundle_other = swap(bundle)
    grad_returned = lax.all_to_all(grad_slots, "expert", 0, 0, tiled=True)
    grad_w_in, grad_w_down = expert_weights(arrived, sent, hid_own, pre_own, bundle_other, 256)
    produced, grad_returned, grad_w_in = lax.optimization_barrier(
        (produced, grad_returned, grad_w_in)
    )
    produced_returned = lax.all_to_all(produced, "expert", 0, 0, tiled=True)
    bits = experts.bit_length() - 1
    levels = min(bits - 1, 3)
    rest = [(bit, bit) for bit in range(3, bits)]
    orders = [
        [(0, 2), (1, 0), (2, 1)] + rest,
        [(1, 0), (2, 1), (0, 2)] + rest,
        [(2, 1), (0, 2), (1, 0)] + rest,
    ]
    third = 4 * width // 3
    *halves, grad_middle, small, input_own, input_other = call(
        functools.partial(backward_kernel, heads, orders, levels),
        [((third // 2, part), BF16)] * 6
        + [
            ((rows, width), F32),
            ((16 + 2 * experts, part), BF16),
            ((rows, width), F32),
            ((rows, width), BF16),
        ],
        (
            grad_returned,
            swap(grad_returned),
            fetch,
            fetch_other,
            middle,
            middle_other,
            cotangent,
            cot_other,
            norm_second,
            mixed,
            mixed_other,
            values,
            probs,
            keys,
            queries,
            act,
            hot,
            tokens,
            other,
            router_part,
            grad_w_in,
            w_out,
            w_query,
            w_key,
            w_value,
        ),
        "l" * 20 + "rrrrr" + "rrrrrr" + "hhhh",
        vmem=56,
        flops=4000000000,
        scratch=[
            pltpu.VMEM((part, width), BF16),
            *[pltpu.VMEM((width, part), BF16)] * 3,
            *[pltpu.VMEM((third, part), BF16)] * 3,
            pltpu.VMEM((16 + 2 * experts, part), F32),
            pltpu.SemaphoreType.DMA((10,)),
        ],
    )
    keeps, grad_middle, small, input_own, input_other, produced_returned = (
        lax.optimization_barrier(
            (halves[0::2], grad_middle, small, input_own, input_other, produced_returned)
        )
    )
    beside = (grad_middle, input_own, swap(input_other), produced_returned)
    kept, got, small, beside = sum_over_chips(
        list(keeps), list(halves[1::2]), orders, levels, small, beside
    )
    grad_middle, input_own, input_swapped, produced_returned = beside
    root = root[:, :1]
    scaled = tokens.astype(F32) * root
    up = norm_first * (input_own + input_swapped.astype(F32))
    grad_input = grad_middle + root * (
        up - scaled * jnp.mean(up * scaled, axis=-1, keepdims=True)
    )
    expert_branch = gate[:, :1] * dot(fetch, produced_returned)
    output = (middle + expert_branch).astype(BF16)
    near = []
    for rows_kept in kept:
        near += [rows_kept, swap(rows_kept)]
    matrices = assemble(orders, levels, (0, 1), near, width)
    small_other = swap(small)
    got, matrices, small, small_other, output, expert_branch, grad_input = (
        lax.optimization_barrier(
            (got, matrices, small, small_other, output, expert_branch, grad_input)
        )
    )
    far = [swap(rows_got) for rows_got in got]
    matrices = assemble(orders, levels, (0,), got, width, matrices)
    results = assemble(
        orders,
        levels,
        (1,),
        far,
        width,
        matrices,
        (small, small_other),
        (experts, heads, buckets),
    )
    return (
        output,
        grad_input,
        results[4],
        results[0],
        results[1],
        results[2],
        results[3],
        results[6].T,
        results[5],
        results[7].T,
        grad_w_in,
        grad_w_down,
        expert_branch,
    )


def solution(mesh):
    placed = (
        P(("expert", "ffn"), None),
        P(),
        P(),
        P(),
        P(),
        P(),
        P(),
        P(),
        P(),
        P("expert", None, "ffn"),
        P("expert", "ffn", None),
        P(("expert", "ffn")),
        P(("expert", "ffn"), None),
    )
    return jax.shard_map(
        shards,
        mesh=mesh,
        in_specs=placed,
        out_specs=(
            P(("expert", "ffn"), None),
            P(("expert", "ffn"), None),
            P(),
            P(),
            P(),
            P(),
            P(),
            P(),
            P(),
            P(),
            P("expert", None, "ffn"),
            P("expert", "ffn", None),
            P(("expert", "ffn"), None),
        ),
        check_vma=False,
    )
```

```python
import functools
import math

import jax
import jax.numpy as jnp
import numpy as np
from jax import lax
from jax.experimental import pallas as pl
from jax.experimental.pallas import tpu as pltpu
from jax.sharding import PartitionSpec as P

REACH = 128
EPS = 1e-06
TOP_PRECISION = lax.Precision.HIGHEST
LANES = 128
F32 = jnp.float32
BF16 = jnp.bfloat16


def bucket_of(distance, buckets, reach):
    half = buckets // 2
    exact = half // 2
    result = np.where(distance < 0, half, 0)
    magnitude = np.abs(distance)
    spread = exact + np.floor(
        np.log(np.maximum(magnitude, 1) / exact) / np.log(reach / exact) * (half - exact)
    )
    spread = np.minimum(spread, half - 1)
    return result + np.where(magnitude < exact, magnitude, spread)


def bucket_windows(rows, buckets, reach):
    lane = np.arange(2 * rows)
    offset = np.where(lane < rows, -lane, 2 * rows - lane)
    windows = []
    for shift in (0, rows, -rows):
        hot = bucket_of(offset + shift, buckets, reach)[None, :] == np.arange(buckets)[:, None]
        hot[:, rows] = False
        windows.append(hot)
    return np.concatenate(windows, axis=1).astype(np.float32)


def rows_by_rows(left, right):
    return lax.dot_general(left, right, (((0,), (0,)), ((), ())), preferred_element_type=F32)


def cols_by_cols(left, right):
    return lax.dot_general(left, right, (((1,), (1,)), ((), ())), preferred_element_type=F32)


def dot(left, right):
    return jnp.dot(left, right, preferred_element_type=F32)


def root_mean(x):
    return lax.rsqrt(jnp.mean(x * x, axis=-1, keepdims=True) + EPS)


def call(body, outs, args, modes, vmem=16, flops=0, scratch=(), aliases=None, nbytes=1000000):
    count, total = len(args), len(args) + len(outs)
    shapes = [(a.shape, a.dtype) for a in args] + list(outs)
    moved = [i for i in range(total) if modes[i] in "hls"]
    buffers = [pltpu.VMEM(*shapes[i]) for i in moved]

    def kernel(*refs):
        bodies = list(refs[:total])
        for i, ref in zip(moved, refs[total : total + len(moved)]):
            bodies[i] = ref
        extra = refs[total + len(moved) : -1]
        sems = refs[-1]
        copies = {}
        for i in moved:
            ends = (refs[i], bodies[i]) if i < count else (bodies[i], refs[i])
            copies[i] = pltpu.make_async_copy(*ends, sems.at[i])
        for i in moved:
            if i < count and modes[i] != "s":
                copies[i].start()
        flushed = set()

        def wait(i):
            copies[i].wait()

        wait.start = lambda i: copies[i].start()

        def flush(i):
            flushed.add(i)
            copies[count + i].start()

        for i in moved:
            if i < count and modes[i] == "h":
                wait(i)
        body(wait, flush, *bodies, *extra)
        for i in moved:
            if i >= count and i - count not in flushed:
                copies[i].start()
        for i in moved:
            if i >= count:
                copies[i].wait()

    specs = [pl.BlockSpec(memory_space=pltpu.HBM)] * total
    return pl.pallas_call(
        kernel,
        out_shape=[jax.ShapeDtypeStruct(s, d) for s, d in outs],
        in_specs=specs[:count],
        out_specs=specs[count:],
        scratch_shapes=buffers + list(scratch) + [pltpu.SemaphoreType.DMA((total,))],
        input_output_aliases=aliases or {},
        compiler_params=pltpu.CompilerParams(vmem_limit_bytes=vmem * 2**20),
        cost_estimate=pl.CostEstimate(flops=flops, bytes_accessed=nbytes, transcendentals=0),
    )(*args)


def toeplitz(window, rows):
    wide = jnp.broadcast_to(window, (rows, 2 * rows))
    return pltpu.roll(wide, 0, 1, stride=1, stride_axis=0)[:, :rows]


def diagonal_sums(square, rows):
    wide = jnp.concatenate([square, jnp.zeros_like(square)], axis=1)
    height = rows
    while height > 1:
        height //= 2
        wide = wide[:height] + pltpu.roll(wide[height:], 2 * rows - height, 1)
    return wide


def placement(ids, experts, total):
    rows = ids.shape[1]
    slots = total // experts
    choose = (lax.broadcasted_iota(jnp.int32, (experts, rows), 0) == ids).astype(F32)
    earlier = (
        lax.broadcasted_iota(jnp.int32, (rows, rows), 0)
        < lax.broadcasted_iota(jnp.int32, (rows, rows), 1)
    ).astype(F32)
    ranks = dot(choose.astype(BF16), earlier.astype(BF16))
    rank = jnp.sum(choose * ranks, axis=0, keepdims=True)
    target = ids * slots + rank.astype(jnp.int32)
    place = (lax.broadcasted_iota(jnp.int32, (total, rows), 0) == target).astype(F32)
    return choose, place


def attend(query_pair, key_pair, scale, bias, side, low_half):
    own = jnp.where(low_half if side == 0 else jnp.logical_not(low_half), query_pair, 0)
    scores = cols_by_cols(own.astype(BF16), key_pair) * scale + bias
    grown = jnp.exp(scores - jnp.max(scores, axis=-1, keepdims=True))
    return grown * (1.0 / jnp.sum(grown, axis=-1, keepdims=True))


def forward_kernel(
    heads,
    wait,
    flush,
    own_ref,
    other_ref,
    gain_first_ref,
    ids_ref,
    ids_other_ref,
    table_ref,
    hot_ref,
    wk,
    wv,
    wq,
    wo,
    gain_second_ref,
    router_ref,
    cot_ref,
    middle_ref,
    gate_ref,
    out_ref,
    mixed_ref,
    win_ref,
    fetch_ref,
    fetch_other_ref,
    root_ref,
    bias,
    staged,
    sems,
):
    rows, width = own_ref.shape
    size = width // heads
    scale = 1.0 / math.sqrt(size)
    core = lax.axis_index("ffn")
    total = out_ref.shape[0]
    experts = router_ref.shape[0]
    sends = [
        pltpu.make_async_copy(staged.at[:, span], out_ref.at[:, span], sems.at[i])
        for i, span in enumerate((pl.ds(width, width + LANES), pl.ds(0, width)))
    ]
    choose, place = placement(ids_ref[...], experts, total)
    _, place_other = placement(ids_other_ref[...], experts, total)
    fetch_ref[...] = place.T.astype(BF16)
    fetch_other_ref[...] = place_other.T.astype(BF16)
    choose = choose.T
    lane = lax.broadcasted_iota(jnp.int32, (total, LANES), 1)
    staged[:, 2 * width :] = jnp.where(
        lane == 0,
        jnp.sum(place, axis=1, keepdims=True),
        jnp.sum(place_other, axis=1, keepdims=True),
    ).astype(BF16)
    place = place.astype(BF16)
    windows = jnp.dot(
        table_ref[...], hot_ref[...], precision=TOP_PRECISION, preferred_element_type=F32
    )
    win_ref[...] = windows
    for i in (4, 5, 6):
        flush(i)
    same = windows[:, : 2 * rows]
    apart = jnp.where(core == 1, windows[:, 2 * rows : 4 * rows], windows[:, 4 * rows :])
    for head in range(heads):
        bias[head, :, :rows] = toeplitz(same[head : head + 1], rows)
        bias[head, :, rows:] = toeplitz(apart[head : head + 1], rows)
    x = own_ref[...].astype(F32)
    y = other_ref[...].astype(F32)
    gain = gain_first_ref[...].reshape(1, width)
    root = root_mean(x)
    root_ref[...] = jnp.broadcast_to(root, root_ref.shape)
    flush(7)
    act_own = (x * root * gain).astype(BF16)
    act_other = (y * root_mean(y) * gain).astype(BF16)
    act = jnp.concatenate([act_own, act_other], axis=0)
    wait(13)
    staged[:, width : 2 * width] = dot(place, cot_ref[...]).astype(BF16)
    sends[0].start()
    wait(7)
    keys = dot(act, wk[...]).astype(BF16)
    wait(8)
    values = dot(act, wv[...]).astype(BF16)
    wait(9)
    queries = dot(act_own, wq[...]).astype(BF16)
    low_half = lax.broadcasted_iota(jnp.int32, (rows, 2 * size), 1) < size
    mixed = []
    for pair in range(heads // 2):
        lanes = slice(pair * 2 * size, (pair + 1) * 2 * size)
        outs = []
        for side in range(2):
            probs = attend(
                queries[:, lanes], keys[:, lanes], scale, bias[2 * pair + side], side, low_half
            )
            outs.append(dot(probs.astype(BF16), values[:, lanes]))
        mixed.append(jnp.where(low_half, outs[0], outs[1]).astype(BF16))
    mixed = jnp.concatenate(mixed, axis=1)
    mixed_ref[...] = mixed
    flush(3)
    for i in (10, 11, 12):
        wait(i)
    middle = x + dot(mixed, wo[...])
    middle_ref[...] = middle
    flush(0)
    gain_second = gain_second_ref[...].reshape(1, width)
    act_second = (middle * root_mean(middle) * gain_second).astype(BF16)
    logits = cols_by_cols(act_second, router_ref[...])
    grown = jnp.exp(logits - jnp.max(logits, axis=-1, keepdims=True))
    gate = jnp.sum(grown * choose, axis=-1, keepdims=True) / jnp.sum(
        grown, axis=-1, keepdims=True
    )
    gate_ref[...] = jnp.broadcast_to(gate, gate_ref.shape)
    staged[:, :width] = dot(place, act_second).astype(BF16)
    sends[1].start()
    flush(1)
    for send in sends:
        send.wait()


def halves_kernel(
    heads,
    wait,
    flush,
    own_ref,
    other_ref,
    gain_first_ref,
    wq_ref,
    wk_ref,
    wv_ref,
    win_ref,
    after_ref,
    act_ref,
    query_ref,
    key_ref,
    value_ref,
    probs_ref,
    wq_half,
    wk_half,
    wv_half,
    sems,
):
    rows, width = own_ref.shape
    size = width // heads
    part = width // 2
    scale = 1.0 / math.sqrt(size)
    core = lax.axis_index("ffn")
    columns = pl.ds(pl.multiple_of(core * part, LANES), part)
    copies = [
        pltpu.make_async_copy(ref.at[:, columns], half, sems.at[i])
        for i, (ref, half) in enumerate(((wq_ref, wq_half), (wk_ref, wk_half), (wv_ref, wv_half)))
    ]
    for copy in copies:
        copy.start()
    x = own_ref[...].astype(F32)
    y = other_ref[...].astype(F32)
    gain = gain_first_ref[...].reshape(1, width)
    act = jnp.concatenate(
        [(x * root_mean(x) * gain).astype(BF16), (y * root_mean(y) * gain).astype(BF16)], axis=0
    )
    act_ref[...] = act
    for copy in copies:
        copy.wait()
    queries = dot(act, wq_half[...]).astype(BF16)
    keys = dot(act, wk_half[...]).astype(BF16)
    values = dot(act, wv_half[...]).astype(BF16)
    query_ref[...] = queries
    key_ref[...] = keys
    value_ref[...] = values
    for i in range(4):
        flush(i)
    low_half = lax.broadcasted_iota(jnp.int32, (2 * rows, 2 * size), 1) < size
    for pair in range(heads // 4):
        lanes = slice(pair * 2 * size, (pair + 1) * 2 * size)
        for side in range(2):
            head = 2 * pair + side
            window = win_ref[pl.ds(core * (heads // 2) + head, 1), :]
            same = toeplitz(window[:, : 2 * rows], rows)
            ahead = toeplitz(window[:, 2 * rows : 4 * rows], rows)
            behind = toeplitz(window[:, 4 * rows :], rows)
            first = jnp.where(core == 1, ahead, behind)
            second = jnp.where(core == 1, behind, ahead)
            bias = jnp.concatenate(
                [
                    jnp.concatenate([same, first], axis=1),
                    jnp.concatenate([second, same], axis=1),
                ],
                axis=0,
            )
            probs_ref[head] = attend(
                queries[:, lanes], keys[:, lanes], scale, bias, side, low_half
            )


def expert_kernel(
    capacity,
    chunk,
    wait,
    flush,
    arrived_ref,
    router_ref,
    in_own_ref,
    in_other_ref,
    down_own_ref,
    down_other_ref,
    after_ref,
    hid_own_ref,
    pre_own_ref,
    sent_ref,
    bundle_ref,
    grad_ref,
    produced_ref,
    router_grad_ref,
    in_vmem,
    down_vmem,
    bundle,
    sems,
):
    total = arrived_ref.shape[0]
    experts, width = router_ref.shape
    slots = total // experts
    hidden = in_own_ref.shape[1]
    steps = hidden // chunk
    mine = lax.axis_index("expert")
    core = lax.axis_index("ffn")
    copies = []
    for side, (win, wdown) in enumerate(
        ((in_own_ref, down_own_ref), (in_other_ref, down_other_ref))
    ):
        for step in range(steps):
            i = side * steps + step
            span = pl.ds(step * chunk, chunk)
            copies.append(
                (
                    pltpu.make_async_copy(win.at[:, span], in_vmem.at[i], sems.at[0, i]),
                    pltpu.make_async_copy(wdown.at[span, :], down_vmem.at[i], sems.at[1, i]),
                )
            )
    for copy in copies[0]:
        copy.start()
    for i in (0, 1):
        wait(i)
    for pair in copies[1:]:
        for copy in pair:
            copy.start()
    flat = arrived_ref[:, :width]
    cot = arrived_ref[:, width : 2 * width]
    filled = arrived_ref[:, 2 * width :]
    row = lax.broadcasted_iota(jnp.int32, (total, total), 0)
    col = lax.broadcasted_iota(jnp.int32, (total, total), 1)
    shift = slots.bit_length() - 1
    row_block = jnp.right_shift(row, shift)
    col_block = jnp.right_shift(col, shift)
    before = (col_block < row_block).astype(F32).astype(BF16)
    ahead = (col_block < row_block + core).astype(F32).astype(BF16)
    slot = jnp.bitwise_and(lax.broadcasted_iota(jnp.int32, (total, 1), 0), slots - 1)
    position = dot(before, filled)[:, 0:1] + dot(ahead, filled)[:, 1:2] + slot.astype(F32)
    keep = jnp.where(position < capacity, 1.0, 0.0)
    logits = cols_by_cols(flat, router_ref[...])
    grown = jnp.exp(logits - jnp.max(logits, axis=-1, keepdims=True))
    router_probs = grown / jnp.sum(grown, axis=-1, keepdims=True)
    onehot = (lax.broadcasted_iota(jnp.int32, (total, experts), 1) == mine).astype(F32)
    gate = jnp.sum(router_probs * onehot, axis=-1, keepdims=True)
    sent = (cot.astype(F32) * (gate * keep)).astype(BF16)
    sent_ref[...] = sent
    flush(2)
    bundle[:, :width] = flat
    bundle[:, width : 2 * width] = sent
    writes = []

    def forward(first, size):
        span = pl.ds(first, size)
        write = pltpu.make_async_copy(
            bundle.at[:, span], bundle_ref.at[:, span], sems.at[2, len(writes)]
        )
        write.start()
        writes.append(write)

    forward(0, 2 * width)
    produced = jnp.zeros((total, width), F32)
    grad = jnp.zeros((total, width), F32)
    inner = math.sqrt(2.0 / math.pi)
    for i, pair in enumerate(copies):
        own_side = i < steps
        first = (i % steps) * chunk
        for copy in pair:
            copy.wait()
        win, wdown = in_vmem[i], down_vmem[i]
        pre = dot(flat, win)
        square = pre * pre
        curve = jnp.tanh(inner * pre * (1.0 + 0.044715 * square))
        half_up = 0.5 + 0.5 * curve
        act = (pre * half_up).astype(BF16)
        slope = half_up + (0.5 * inner) * pre * (1.0 - curve * curve) * (
            1.0 + (3 * 0.044715) * square
        )
        grad_pre = (slope * cols_by_cols(sent, wdown)).astype(BF16)
        if own_side:
            hid_own_ref[:, first : first + chunk] = act
            pre_own_ref[:, first : first + chunk] = grad_pre
        else:
            first += 2 * width
            bundle[:, first : first + chunk] = act
            bundle[:, first + hidden : first + hidden + chunk] = grad_pre
            forward(first, chunk)
            forward(first + hidden, chunk)
        if i + 1 == steps:
            flush(0)
            flush(1)
        produced = produced + dot(act, wdown)
        grad = grad + cols_by_cols(grad_pre, win)
    produced_low = produced.astype(BF16)
    kept = produced_low.astype(F32) * keep
    produced_ref[...] = kept.astype(BF16)
    flush(5)
    grad_gate = jnp.sum(cot.astype(F32) * kept, axis=-1, keepdims=True)
    grad_logits = ((grad_gate * gate) * (onehot - router_probs)).astype(BF16)
    grad_ref[...] = (grad * keep + dot(grad_logits, router_ref[...])).astype(BF16)
    flush(4)
    router_grad_ref[...] = rows_by_rows(grad_logits, flat)
    for write in writes:
        write.wait()


def expert_weights_kernel(
    flat_own, sent_own, hid_own, pre_own, flat_other, sent_other, hid_other, pre_other, in_ref, down_ref
):
    in_ref[0] = rows_by_rows(flat_own[...], pre_own[...]) + rows_by_rows(
        flat_other[...], pre_other[...]
    )
    down_ref[0] = rows_by_rows(hid_own[...], sent_own[...]) + rows_by_rows(
        hid_other[...], sent_other[...]
    )


def expert_weights(flat, sent, hid, pre, bundle, chunk):
    total, width = sent.shape
    hidden = hid.shape[1]
    steps = hidden // chunk
    skip = 2 * width // chunk
    whole = pl.BlockSpec((total, width), lambda i: (0, 0))
    second = pl.BlockSpec((total, width), lambda i: (0, 1))
    part = pl.BlockSpec((total, chunk), lambda i: (0, i))
    return pl.pallas_call(
        expert_weights_kernel,
        grid=(steps,),
        out_shape=[
            jax.ShapeDtypeStruct((1, width, hidden), F32),
            jax.ShapeDtypeStruct((1, hidden, width), F32),
        ],
        in_specs=[
            whole,
            whole,
            part,
            part,
            whole,
            second,
            pl.BlockSpec((total, chunk), lambda i: (0, i + skip)),
            pl.BlockSpec((total, chunk), lambda i: (0, i + skip + steps)),
        ],
        out_specs=[
            pl.BlockSpec((1, width, chunk), lambda i: (0, 0, i)),
            pl.BlockSpec((1, chunk, width), lambda i: (0, i, 0)),
        ],
        compiler_params=pltpu.CompilerParams(vmem_limit_bytes=64 * 2**20),
        cost_estimate=pl.CostEstimate(
            flops=8 * total * width * hidden, bytes_accessed=14000000, transcendentals=0
        ),
    )(flat, sent, hid, pre, bundle, bundle, bundle, bundle)


def middle_back(returned, fetch, middle, gain, cot):
    grad = dot(fetch, returned)
    root = root_mean(middle)
    scaled = middle * root
    up = gain * grad
    grad_middle = cot.astype(F32) + root * (
        up - scaled * jnp.mean(up * scaled, axis=-1, keepdims=True)
    )
    return grad_middle, grad * scaled


def bit_of(step, other=0):
    return jnp.where(lax.axis_index("ffn") == other, step[0], step[1])


def chunk_place(chunk, order, levels, other=0):
    chip = lax.axis_index("expert")
    mine = 0
    for step in order[:levels]:
        mine = mine * 2 + jnp.bitwise_and(jnp.right_shift(chip, bit_of(step, other)), 1)
    return jnp.bitwise_xor(mine, chunk)


def small_rows(experts):
    return [0, 2, 4, 16, 16 + experts, 16 + 2 * experts]


def backward_kernel(
    heads,
    orders,
    levels,
    wait,
    flush,
    returned_ref,
    returned_other_ref,
    fetch_ref,
    fetch_other_ref,
    middle_ref,
    middle_other_ref,
    cot_ref,
    cot_other_ref,
    gain_second_ref,
    mixed_own_ref,
    mixed_other_ref,
    value_ref,
    probs_ref,
    key_ref,
    query_ref,
    act_ref,
    hot_ref,
    own_ref,
    other_ref,
    router_ref,
    after_ref,
    wo_ref,
    wq_ref,
    wk_ref,
    wv_ref,
    keep_0_ref,
    send_0_ref,
    keep_1_ref,
    send_1_ref,
    keep_2_ref,
    send_2_ref,
    grad_middle_ref,
    small_ref,
    input_own_ref,
    input_other_ref,
    wo_half,
    wq_half,
    wk_half,
    wv_half,
    part_0,
    part_1,
    part_2,
    small,
    sems,
):
    rows, width = middle_ref.shape
    size = width // heads
    part = width // 2
    experts = router_ref.shape[0]
    scale = 1.0 / math.sqrt(size)
    core = lax.axis_index("ffn")
    span = pl.ds(pl.multiple_of(core * part, LANES), part)
    copies = [
        pltpu.make_async_copy(src, half, sems.at[6 + i])
        for i, (src, half) in enumerate(
            (
                (wo_ref.at[span, :], wo_half),
                (wq_ref.at[:, span], wq_half),
                (wk_ref.at[:, span], wk_half),
                (wv_ref.at[:, span], wv_half),
            )
        )
    ]
    for copy in copies:
        copy.start()
    parts = (part_0, part_1, part_2)
    halves = ((keep_0_ref, send_0_ref), (keep_1_ref, send_1_ref), (keep_2_ref, send_2_ref))
    third = width // 3
    height = third >> levels
    writes = []
    for p, pair in enumerate(halves):
        rows_half = pair[0].shape[0]
        for i, ref in enumerate(pair):
            writes.append(
                pltpu.make_async_copy(
                    parts[p].at[pl.ds(i * rows_half, rows_half), :], ref, sems.at[2 * p + i]
                )
            )
    places = [
        [chunk_place(chunk, order, levels) * (4 * height) for chunk in range(2**levels)]
        for order in orders
    ]

    def pack(matrix, value):
        for p, ref in enumerate(parts):
            for chunk in range(2**levels):
                first = p * third + chunk * height
                at = pl.multiple_of(places[p][chunk] + matrix * height, 16)
                ref[pl.ds(at, height), :] = value[first : first + height]

    for i in range(9):
        wait(i)
    copies[0].wait()
    gain = gain_second_ref[...].reshape(1, width)
    grad_own, gain_terms = middle_back(
        returned_ref[...], fetch_ref[...], middle_ref[...], gain, cot_ref[...]
    )
    grad_other, _ = middle_back(
        returned_other_ref[...], fetch_other_ref[...], middle_other_ref[...], gain, cot_other_ref[...]
    )
    gain_second = jnp.sum(gain_terms, axis=0, keepdims=True)
    grad_middle_ref[...] = grad_own
    flush(6)
    grad_low = jnp.concatenate([grad_own, grad_other], axis=0).astype(BF16)
    grad_mixed = cols_by_cols(grad_low, wo_half[...]).astype(BF16)
    for i in range(9, 20):
        wait(i)
    for copy in copies[1:]:
        copy.wait()
    mixed = jnp.concatenate([mixed_own_ref[...], mixed_other_ref[...]], axis=0)
    grad_columns = jnp.where(core == 0, grad_low[:, :part], grad_low[:, part:])
    pack(3, rows_by_rows(mixed, grad_columns).astype(BF16))
    low_half = lax.broadcasted_iota(jnp.int32, (2 * rows, 2 * size), 1) < size
    grad_q, grad_k, grad_v = [], [], []
    same, ahead, behind = [], [], []
    for pair in range(heads // 4):
        lanes = slice(pair * 2 * size, (pair + 1) * 2 * size)
        query, key, value = query_ref[:, lanes], key_ref[:, lanes], value_ref[:, lanes]
        grad_pair = grad_mixed[:, lanes]
        got_q, got_k, got_v = [], [], []
        for side in range(2):
            probs = probs_ref[2 * pair + side]
            keep_lanes = low_half if side == 0 else jnp.logical_not(low_half)
            own_grad = jnp.where(keep_lanes, grad_pair, 0).astype(BF16)
            grad_probs = cols_by_cols(own_grad, value)
            got_v.append(rows_by_rows(probs.astype(BF16), grad_pair))
            inner = jnp.sum(probs * grad_probs, axis=-1, keepdims=True)
            grad_scores = probs * (grad_probs - inner)
            same.append(
                diagonal_sums(grad_scores[:rows, :rows] + grad_scores[rows:, rows:], rows)
            )
            first = diagonal_sums(grad_scores[:rows, rows:], rows)
            second = diagonal_sums(grad_scores[rows:, :rows], rows)
            ahead.append(jnp.where(core == 1, first, second))
            behind.append(jnp.where(core == 1, second, first))
            grad_raw = (grad_scores * scale).astype(BF16)
            got_q.append(dot(grad_raw, key))
            got_k.append(rows_by_rows(grad_raw, query))
        grad_q.append(jnp.where(low_half, got_q[0], got_q[1]).astype(BF16))
        grad_k.append(jnp.where(low_half, got_k[0], got_k[1]).astype(BF16))
        grad_v.append(jnp.where(low_half, got_v[0], got_v[1]).astype(BF16))
    grad_q = jnp.concatenate(grad_q, axis=1)
    grad_k = jnp.concatenate(grad_k, axis=1)
    grad_v = jnp.concatenate(grad_v, axis=1)
    act = act_ref[...]
    pack(0, rows_by_rows(act, grad_q).astype(BF16))
    pack(1, rows_by_rows(act, grad_k).astype(BF16))
    pack(2, rows_by_rows(act, grad_v).astype(BF16))
    for write in writes:
        write.start()
    grad_act = (
        cols_by_cols(grad_q, wq_half[...])
        + cols_by_cols(grad_k, wk_half[...])
        + cols_by_cols(grad_v, wv_half[...])
    )
    input_other_ref[...] = grad_act[rows:].astype(BF16)
    flush(9)
    input_own_ref[...] = grad_act[:rows]
    flush(8)
    x = own_ref[...].astype(F32)
    y = other_ref[...].astype(F32)
    gain_first = jnp.sum(
        grad_act[:rows] * (x * root_mean(x)) + grad_act[rows:] * (y * root_mean(y)),
        axis=0,
        keepdims=True,
    )
    sums = jnp.concatenate(
        [jnp.concatenate(part_sums, axis=0) for part_sums in (same, ahead, behind)], axis=1
    )
    table = lax.dot_general(
        sums,
        hot_ref[...],
        (((1,), (1,)), ((), ())),
        precision=TOP_PRECISION,
        preferred_element_type=F32,
    )
    at = small_rows(experts)
    small[: at[3]] = jnp.zeros((at[3], part), F32)
    for i, value in enumerate((gain_first, gain_second)):
        small[at[i] : at[i] + 1] = value[:, :part]
        small[at[i] + 1 : at[i] + 2] = value[:, part:]
    small[at[2] : at[2] + heads // 2, : table.shape[1]] = table
    small[at[3] : at[4]] = router_ref[:, :part]
    small[at[4] : at[5]] = router_ref[:, part:]
    small_ref[...] = small[...].astype(BF16)
    flush(7)
    for write in writes:
        write.wait()


def assemble_kernel(orders, levels, sides, upper, last, wait, flush, *refs):
    count = len(orders) * len(sides)
    arrays, refs = refs[:count], refs[count:]
    if last is not None:
        experts, heads = last
        (small_own_ref, small_other_ref), refs = refs[:2], refs[2:]
        last_inputs = (count, count + 1)
    if upper:
        refs = refs[4:]
    outs, (wide, sems) = refs[:4], refs[-2:]
    if last is not None:
        gain_first_ref, gain_second_ref, table_ref, router_ref = refs[4:8]
    width = outs[0].shape[1]
    part = width // 2
    third = width // 3
    span = third // 2
    height = third >> levels
    half = 2 ** (levels - 1)
    core = lax.axis_index("ffn")
    mine = lax.axis_index("expert")
    columns = [
        pl.ds(pl.multiple_of((1 - core if side else core) * part, LANES), part) for side in sides
    ]
    writes = []
    for p, order in enumerate(orders):
        for i, side in enumerate(sides):
            n = len(sides) * p + i
            wait(n)
            bit = jnp.bitwise_and(jnp.right_shift(mine, bit_of(order[0], side)), 1)
            if upper:
                bit = 1 - bit
            first = pl.multiple_of(p * third + bit * span, span)
            places = [
                jnp.bitwise_and(chunk_place(low, order, levels, side), half - 1)
                for low in range(half)
            ]
            for matrix in range(4):
                for low in range(half):
                    at = pl.multiple_of((places[low] * 4 + matrix) * height, height)
                    wide[n, matrix, pl.ds(low * height, height)] = arrays[n][
                        pl.ds(at, height), :
                    ].astype(F32)
                write = pltpu.make_async_copy(
                    wide.at[n, matrix],
                    outs[matrix].at[pl.ds(first, span), columns[i]],
                    sems.at[4 * n + matrix],
                )
                write.start()
                writes.append(write)
    if last is not None:
        for i in last_inputs:
            wait(i)
        at = small_rows(experts)
        mine, other = small_own_ref[...], small_other_ref[...]
        both = mine + other
        gain_first_ref[...] = jnp.concatenate([both[0:1], both[1:2]], axis=1).reshape(width)
        gain_second_ref[...] = jnp.concatenate([both[2:3], both[3:4]], axis=1).reshape(width)
        buckets = table_ref.shape[1]
        low = mine[at[2] : at[2] + heads // 2, :buckets]
        high = other[at[2] : at[2] + heads // 2, :buckets]
        table_ref[...] = jnp.where(
            core == 0,
            jnp.concatenate([low, high], axis=0),
            jnp.concatenate([high, low], axis=0),
        )
        router_ref[...] = jnp.concatenate([both[at[3] : at[4]], both[at[4] : at[5]]], axis=1)
    for write in writes:
        write.wait()


def assemble(orders, levels, sides, arrays, width, earlier=(), smalls=(), last=None):
    tail = []
    modes = "l" * len(arrays)
    if last is not None:
        experts, heads, buckets = last
        tail = [((width,), F32), ((width,), F32), ((heads, buckets), F32), ((experts, width), F32)]
        modes += "ll"
        last = (experts, heads)
    first = len(modes)
    modes += "r" * len(earlier)
    return call(
        functools.partial(assemble_kernel, orders, levels, sides, bool(earlier), last),
        [((width, width), F32)] * 4 + tail,
        (*arrays, *smalls, *earlier),
        modes + "rrrr" + "h" * len(tail),
        vmem=16,
        aliases={first + i: i for i in range(len(earlier))},
        scratch=[
            pltpu.VMEM((len(arrays), 4, width // 6, width // 2), F32),
            pltpu.SemaphoreType.DMA((4 * len(arrays),)),
        ],
        nbytes=8000000,
    )


def swap(x):
    return lax.ppermute(x, "ffn", [(0, 1), (1, 0)])


def flip(x, step):
    pairs = []
    for chip in range(lax.axis_size("expert")):
        for core in range(2):
            pairs.append((chip * 2 + core, (chip ^ (1 << step[core])) * 2 + core))
    return lax.ppermute(x, ("expert", "ffn"), pairs)


def add_low(left, right):
    return (left.astype(F32) + right.astype(F32)).astype(BF16)


def sum_over_chips(keeps, sends, orders, levels, small, beside):
    count = len(orders[0])
    todo = [set(step[core] for step in orders[0]) for core in range(2)]
    ridden = set()

    def exchange(phase, x, bit):
        nonlocal small
        fresh = all(bit[core] in todo[core] for core in range(2))
        if not fresh or phase in ridden or phase < 2 or phase > 2 * count - 3:
            return flip(x, bit)
        for core in range(2):
            todo[core].discard(bit[core])
        ridden.add(phase)
        sent = small.astype(BF16)
        got = flip(jnp.concatenate([x, sent]), bit)
        rows = x.shape[0]
        small = sent.astype(F32) + got[rows:].astype(F32)
        return got[:rows]

    def mine(bit):
        return (lax.axis_index("expert") >> bit_of(bit)) & 1

    whole = [None] * len(orders)
    for k in range(count - 1):
        for p, order in enumerate(orders):
            keep, got = keeps[p], exchange(k, sends[p], order[k])
            half = keep.shape[0] // 2
            if k + 2 == count:
                whole[p] = add_low(keep, got)
            elif k + 1 < levels:
                keeps[p] = add_low(keep[:half], got[:half])
                sends[p] = add_low(keep[half:], got[half:])
            else:
                both = add_low(keep, got)
                upper = mine(order[k + 1])
                keeps[p] = lax.dynamic_slice_in_dim(both, upper * half, half, 0)
                sends[p] = lax.dynamic_slice_in_dim(both, (1 - upper) * half, half, 0)
    for p, order in enumerate(orders):
        x = whole[p]
        whole[p] = add_low(x, exchange(count - 1, x, order[-1]))
    got = [None] * len(orders)
    for k in reversed(range(count - 1)):
        for p, order in enumerate(orders):
            x = whole[p]
            got[p] = exchange(2 * count - 2 - k, x, order[k])
            if k == 0:
                continue
            if k < levels:
                whole[p] = jnp.concatenate([x, got[p]])
            else:
                whole[p] = jnp.where(
                    mine(order[k]) == 1,
                    jnp.concatenate([got[p], x]),
                    jnp.concatenate([x, got[p]]),
                )
    for bit in zip(sorted(todo[0]), sorted(todo[1])):
        sent = small.astype(BF16)
        small = sent.astype(F32) + flip(sent, bit).astype(F32)
    return whole, got, small, beside


def shards(
    tokens,
    norm_first,
    w_query,
    w_key,
    w_value,
    w_out,
    bucket_bias_table,
    norm_second,
    w_router,
    w_in,
    w_down,
    expert_ids,
    cotangent,
):
    rows, width = tokens.shape
    buckets, heads = bucket_bias_table.shape
    pair = lax.axis_size("ffn")
    experts = w_router.shape[1]
    total = 2 * rows
    capacity = 5 * rows * pair // 4
    hidden = w_in.shape[2]
    part = width // 2
    hot = jnp.asarray(bucket_windows(rows, buckets, REACH))
    router = w_router.T

    other = swap(tokens)
    ids = expert_ids.reshape(1, rows)
    ids_other = swap(ids)
    middle, gate, outgoing, mixed, windows, fetch, fetch_other, root = call(
        functools.partial(forward_kernel, heads),
        [
            ((rows, width), F32),
            ((rows, LANES), F32),
            ((total, 2 * width + LANES), BF16),
            ((rows, width), BF16),
            ((heads, 6 * rows), F32),
            ((rows, total), BF16),
            ((rows, total), BF16),
            ((rows, LANES), F32),
        ],
        (
            tokens,
            other,
            norm_first,
            ids,
            ids_other,
            bucket_bias_table.T,
            hot,
            w_key,
            w_value,
            w_query,
            w_out,
            norm_second,
            router,
            cotangent,
        ),
        "hhhhhhhlllllll" + "hhrhhhhh",
        vmem=64,
        flops=3000000000,
        scratch=[
            pltpu.VMEM((heads, rows, 2 * rows), F32),
            pltpu.VMEM((total, 2 * width + LANES), BF16),
            pltpu.SemaphoreType.DMA((2,)),
        ],
    )
    arrived = lax.all_to_all(outgoing, "expert", 0, 0, tiled=True)
    gate, w_in, w_down, cot_own = lax.optimization_barrier((gate, w_in, w_down, cotangent))
    in_own, down_own = w_in[0], w_down[0]
    in_other, down_other = swap(in_own), swap(down_own)
    cot_other = swap(cot_own)
    mixed_other, middle_other = swap(mixed), swap(middle)
    act, queries, keys, values, probs = call(
        functools.partial(halves_kernel, heads),
        [
            ((2 * rows, width), BF16),
            ((2 * rows, part), BF16),
            ((2 * rows, part), BF16),
            ((2 * rows, part), BF16),
            ((heads // 2, 2 * rows, 2 * rows), F32),
        ],
        (tokens, other, norm_first, w_query, w_key, w_value, windows, gate),
        "hhhrrrhr" + "hhhhh",
        vmem=64,
        flops=3000000000,
        scratch=[pltpu.VMEM((width, part), BF16)] * 3 + [pltpu.SemaphoreType.DMA((3,))],
    )
    chunk = hidden // 2
    steps = 2 * hidden // chunk
    hid_own, pre_own, sent, bundle, grad_slots, produced, router_part = call(
        functools.partial(expert_kernel, capacity, chunk),
        [
            ((total, hidden), BF16),
            ((total, hidden), BF16),
            ((total, width), BF16),
            ((total, 2 * width + 2 * hidden), BF16),
            ((total, width), BF16),
            ((total, width), BF16),
            ((experts, width), F32),
        ],
        (arrived, router, in_own, in_other, down_own, down_other, act),
        "llrrrrr" + "hhhrhhh",
        vmem=64,
        flops=6000000000,
        scratch=[
            pltpu.VMEM((steps, width, chunk), BF16),
            pltpu.VMEM((steps, chunk, width), BF16),
            pltpu.VMEM((total, 2 * width + 2 * hidden), BF16),
            pltpu.SemaphoreType.DMA((3, steps + 1)),
        ],
    )
    bundle_other = swap(bundle)
    grad_returned = lax.all_to_all(grad_slots, "expert", 0, 0, tiled=True)
    grad_w_in, grad_w_down = expert_weights(arrived, sent, hid_own, pre_own, bundle_other, 256)
    produced, grad_returned, grad_w_in = lax.optimization_barrier(
        (produced, grad_returned, grad_w_in)
    )
    produced_returned = lax.all_to_all(produced, "expert", 0, 0, tiled=True)
    bits = experts.bit_length() - 1
    levels = min(bits - 1, 3)
    rest = [(bit, bit) for bit in range(3, bits)]
    orders = [
        [(0, 2), (1, 0), (2, 1)] + rest,
        [(1, 0), (2, 1), (0, 2)] + rest,
        [(2, 1), (0, 2), (1, 0)] + rest,
    ]
    third = 4 * width // 3
    *halves, grad_middle, small, input_own, input_other = call(
        functools.partial(backward_kernel, heads, orders, levels),
        [((third // 2, part), BF16)] * 6
        + [
            ((rows, width), F32),
            ((16 + 2 * experts, part), BF16),
            ((rows, width), F32),
            ((rows, width), BF16),
        ],
        (
            grad_returned,
            swap(grad_returned),
            fetch,
            fetch_other,
            middle,
            middle_other,
            cotangent,
            cot_other,
            norm_second,
            mixed,
            mixed_other,
            values,
            probs,
            keys,
            queries,
            act,
            hot,
            tokens,
            other,
            router_part,
            grad_w_in,
            w_out,
            w_query,
            w_key,
            w_value,
        ),
        "l" * 20 + "rrrrr" + "rrrrrr" + "hhhh",
        vmem=56,
        flops=4000000000,
        scratch=[
            pltpu.VMEM((part, width), BF16),
            *[pltpu.VMEM((width, part), BF16)] * 3,
            *[pltpu.VMEM((third, part), BF16)] * 3,
            pltpu.VMEM((16 + 2 * experts, part), F32),
            pltpu.SemaphoreType.DMA((10,)),
        ],
    )
    keeps, grad_middle, small, input_own, input_other, produced_returned = (
        lax.optimization_barrier(
            (halves[0::2], grad_middle, small, input_own, input_other, produced_returned)
        )
    )
    beside = (grad_middle, input_own, swap(input_other), produced_returned)
    kept, got, small, beside = sum_over_chips(
        list(keeps), list(halves[1::2]), orders, levels, small, beside
    )
    grad_middle, input_own, input_swapped, produced_returned = beside
    root = root[:, :1]
    scaled = tokens.astype(F32) * root
    up = norm_first * (input_own + input_swapped.astype(F32))
    grad_input = grad_middle + root * (
        up - scaled * jnp.mean(up * scaled, axis=-1, keepdims=True)
    )
    expert_branch = gate[:, :1] * dot(fetch, produced_returned)
    output = (middle + expert_branch).astype(BF16)
    near = []
    for rows_kept in kept:
        near += [rows_kept, swap(rows_kept)]
    small_other = swap(small)
    *matrices, gain_first, gain_second, table, router_sum = assemble(
        orders,
        levels,
        (0, 1),
        near,
        width,
        smalls=(small, small_other),
        last=(experts, heads, buckets),
    )
    got, matrices, output, expert_branch, grad_input = lax.optimization_barrier(
        (got, matrices, output, expert_branch, grad_input)
    )
    far = [swap(rows_got) for rows_got in got]
    matrices = assemble(orders, levels, (0,), got, width, matrices)
    matrices = assemble(orders, levels, (1,), far, width, matrices)
    return (
        output,
        grad_input,
        gain_first,
        *matrices,
        table.T,
        gain_second,
        router_sum.T,
        grad_w_in,
        grad_w_down,
        expert_branch,
    )


def solution(mesh):
    placed = (
        P(("expert", "ffn"), None),
        P(),
        P(),
        P(),
        P(),
        P(),
        P(),
        P(),
        P(),
        P("expert", None, "ffn"),
        P("expert", "ffn", None),
        P(("expert", "ffn")),
        P(("expert", "ffn"), None),
    )
    return jax.shard_map(
        shards,
        mesh=mesh,
        in_specs=placed,
        out_specs=(
            P(("expert", "ffn"), None),
            P(("expert", "ffn"), None),
            P(),
            P(),
            P(),
            P(),
            P(),
            P(),
            P(),
            P(),
            P("expert", None, "ffn"),
            P("expert", "ffn", None),
            P(("expert", "ffn"), None),
        ),
        check_vma=False,
    )
```

```python
import functools
import math

import jax
import jax.numpy as jnp
import numpy as np
from jax import lax
from jax.experimental import pallas as pl
from jax.experimental.pallas import tpu as pltpu
from jax.sharding import PartitionSpec as P

REACH = 128
EPS = 1e-06
TOP_PRECISION = lax.Precision.HIGHEST
LANES = 128
F32 = jnp.float32
BF16 = jnp.bfloat16


def bucket_of(distance, buckets, reach):
    half = buckets // 2
    exact = half // 2
    result = np.where(distance < 0, half, 0)
    magnitude = np.abs(distance)
    spread = exact + np.floor(
        np.log(np.maximum(magnitude, 1) / exact) / np.log(reach / exact) * (half - exact)
    )
    spread = np.minimum(spread, half - 1)
    return result + np.where(magnitude < exact, magnitude, spread)


def bucket_windows(rows, buckets, reach):
    lane = np.arange(2 * rows)
    offset = np.where(lane < rows, -lane, 2 * rows - lane)
    windows = []
    for shift in (0, rows, -rows):
        hot = bucket_of(offset + shift, buckets, reach)[None, :] == np.arange(buckets)[:, None]
        hot[:, rows] = False
        windows.append(hot)
    return np.concatenate(windows, axis=1).astype(np.float32)


def rows_by_rows(left, right):
    return lax.dot_general(left, right, (((0,), (0,)), ((), ())), preferred_element_type=F32)


def cols_by_cols(left, right):
    return lax.dot_general(left, right, (((1,), (1,)), ((), ())), preferred_element_type=F32)


def dot(left, right):
    return jnp.dot(left, right, preferred_element_type=F32)


def root_mean(x):
    return lax.rsqrt(jnp.mean(x * x, axis=-1, keepdims=True) + EPS)


def call(body, outs, args, modes, vmem=16, flops=0, scratch=(), aliases=None, nbytes=1000000):
    count, total = len(args), len(args) + len(outs)
    shapes = [(a.shape, a.dtype) for a in args] + list(outs)
    moved = [i for i in range(total) if modes[i] in "hls"]
    buffers = [pltpu.VMEM(*shapes[i]) for i in moved]

    def kernel(*refs):
        bodies = list(refs[:total])
        for i, ref in zip(moved, refs[total : total + len(moved)]):
            bodies[i] = ref
        extra = refs[total + len(moved) : -1]
        sems = refs[-1]
        copies = {}
        for i in moved:
            ends = (refs[i], bodies[i]) if i < count else (bodies[i], refs[i])
            copies[i] = pltpu.make_async_copy(*ends, sems.at[i])
        for i in moved:
            if i < count and modes[i] != "s":
                copies[i].start()
        flushed = set()

        def wait(i):
            copies[i].wait()

        wait.start = lambda i: copies[i].start()

        def flush(i):
            flushed.add(i)
            copies[count + i].start()

        for i in moved:
            if i < count and modes[i] == "h":
                wait(i)
        body(wait, flush, *bodies, *extra)
        for i in moved:
            if i >= count and i - count not in flushed:
                copies[i].start()
        for i in moved:
            if i >= count:
                copies[i].wait()

    specs = [pl.BlockSpec(memory_space=pltpu.HBM)] * total
    return pl.pallas_call(
        kernel,
        out_shape=[jax.ShapeDtypeStruct(s, d) for s, d in outs],
        in_specs=specs[:count],
        out_specs=specs[count:],
        scratch_shapes=buffers + list(scratch) + [pltpu.SemaphoreType.DMA((total,))],
        input_output_aliases=aliases or {},
        compiler_params=pltpu.CompilerParams(vmem_limit_bytes=vmem * 2**20),
        cost_estimate=pl.CostEstimate(flops=flops, bytes_accessed=nbytes, transcendentals=0),
    )(*args)


def toeplitz(window, rows):
    wide = jnp.broadcast_to(window, (rows, 2 * rows))
    return pltpu.roll(wide, 0, 1, stride=1, stride_axis=0)[:, :rows]


def diagonal_sums(square, rows):
    wide = jnp.concatenate([square, jnp.zeros_like(square)], axis=1)
    height = rows
    while height > 1:
        height //= 2
        wide = wide[:height] + pltpu.roll(wide[height:], 2 * rows - height, 1)
    return wide


def placement(ids, experts, total):
    rows = ids.shape[1]
    slots = total // experts
    choose = (lax.broadcasted_iota(jnp.int32, (experts, rows), 0) == ids).astype(F32)
    earlier = (
        lax.broadcasted_iota(jnp.int32, (rows, rows), 0)
        < lax.broadcasted_iota(jnp.int32, (rows, rows), 1)
    ).astype(F32)
    ranks = dot(choose.astype(BF16), earlier.astype(BF16))
    rank = jnp.sum(choose * ranks, axis=0, keepdims=True)
    target = ids * slots + rank.astype(jnp.int32)
    place = (lax.broadcasted_iota(jnp.int32, (total, rows), 0) == target).astype(F32)
    return choose, place


def attend(query_pair, key_pair, scale, bias, side, low_half):
    own = jnp.where(low_half if side == 0 else jnp.logical_not(low_half), query_pair, 0)
    scores = cols_by_cols(own.astype(BF16), key_pair) * scale + bias
    grown = jnp.exp(scores - jnp.max(scores, axis=-1, keepdims=True))
    return grown * (1.0 / jnp.sum(grown, axis=-1, keepdims=True))


def forward_kernel(
    heads,
    wait,
    flush,
    own_ref,
    other_ref,
    gain_first_ref,
    ids_ref,
    ids_other_ref,
    table_ref,
    hot_ref,
    wk,
    wv,
    wq,
    wo,
    gain_second_ref,
    router_ref,
    cot_ref,
    middle_ref,
    gate_ref,
    out_ref,
    mixed_ref,
    win_ref,
    fetch_ref,
    fetch_other_ref,
    root_ref,
    bias,
    staged,
    sems,
):
    rows, width = own_ref.shape
    size = width // heads
    scale = 1.0 / math.sqrt(size)
    core = lax.axis_index("ffn")
    wait.start(10)
    total = out_ref.shape[0]
    experts = router_ref.shape[0]
    sends = [
        pltpu.make_async_copy(staged.at[:, span], out_ref.at[:, span], sems.at[i])
        for i, span in enumerate((pl.ds(width, width + LANES), pl.ds(0, width)))
    ]
    choose, place = placement(ids_ref[...], experts, total)
    _, place_other = placement(ids_other_ref[...], experts, total)
    fetch_ref[...] = place.T.astype(BF16)
    fetch_other_ref[...] = place_other.T.astype(BF16)
    choose = choose.T
    lane = lax.broadcasted_iota(jnp.int32, (total, LANES), 1)
    staged[:, 2 * width :] = jnp.where(
        lane == 0,
        jnp.sum(place, axis=1, keepdims=True),
        jnp.sum(place_other, axis=1, keepdims=True),
    ).astype(BF16)
    place = place.astype(BF16)
    windows = jnp.dot(
        table_ref[...], hot_ref[...], precision=TOP_PRECISION, preferred_element_type=F32
    )
    win_ref[...] = windows
    for i in (4, 5, 6):
        flush(i)
    same = windows[:, : 2 * rows]
    apart = jnp.where(core == 1, windows[:, 2 * rows : 4 * rows], windows[:, 4 * rows :])
    for head in range(heads):
        bias[head, :, :rows] = toeplitz(same[head : head + 1], rows)
        bias[head, :, rows:] = toeplitz(apart[head : head + 1], rows)
    x = own_ref[...].astype(F32)
    y = other_ref[...].astype(F32)
    gain = gain_first_ref[...].reshape(1, width)
    root = root_mean(x)
    root_ref[...] = jnp.broadcast_to(root, root_ref.shape)
    flush(7)
    act_own = (x * root * gain).astype(BF16)
    act_other = (y * root_mean(y) * gain).astype(BF16)
    act = jnp.concatenate([act_own, act_other], axis=0)
    wait(13)
    staged[:, width : 2 * width] = dot(place, cot_ref[...]).astype(BF16)
    sends[0].start()
    wait(7)
    keys = dot(act, wk[...]).astype(BF16)
    wait(8)
    values = dot(act, wv[...]).astype(BF16)
    wait(9)
    queries = dot(act_own, wq[...]).astype(BF16)
    low_half = lax.broadcasted_iota(jnp.int32, (rows, 2 * size), 1) < size
    mixed = []
    for pair in range(heads // 2):
        lanes = slice(pair * 2 * size, (pair + 1) * 2 * size)
        outs = []
        for side in range(2):
            probs = attend(
                queries[:, lanes], keys[:, lanes], scale, bias[2 * pair + side], side, low_half
            )
            outs.append(dot(probs.astype(BF16), values[:, lanes]))
        mixed.append(jnp.where(low_half, outs[0], outs[1]).astype(BF16))
    mixed = jnp.concatenate(mixed, axis=1)
    mixed_ref[...] = mixed
    flush(3)
    for i in (10, 11, 12):
        wait(i)
    middle = x + dot(mixed, wo[...])
    middle_ref[...] = middle
    flush(0)
    gain_second = gain_second_ref[...].reshape(1, width)
    act_second = (middle * root_mean(middle) * gain_second).astype(BF16)
    staged[:, :width] = dot(place, act_second).astype(BF16)
    sends[1].start()
    logits = cols_by_cols(act_second, router_ref[...])
    grown = jnp.exp(logits - jnp.max(logits, axis=-1, keepdims=True))
    gate = jnp.sum(grown * choose, axis=-1, keepdims=True) / jnp.sum(
        grown, axis=-1, keepdims=True
    )
    gate_ref[...] = jnp.broadcast_to(gate, gate_ref.shape)
    flush(1)
    for send in sends:
        send.wait()


def halves_kernel(
    heads,
    wait,
    flush,
    own_ref,
    other_ref,
    gain_first_ref,
    wq_ref,
    wk_ref,
    wv_ref,
    win_ref,
    after_ref,
    act_ref,
    query_ref,
    key_ref,
    value_ref,
    probs_ref,
    wq_half,
    wk_half,
    wv_half,
    sems,
):
    rows, width = own_ref.shape
    size = width // heads
    part = width // 2
    scale = 1.0 / math.sqrt(size)
    core = lax.axis_index("ffn")
    columns = pl.ds(pl.multiple_of(core * part, LANES), part)
    copies = [
        pltpu.make_async_copy(ref.at[:, columns], half, sems.at[i])
        for i, (ref, half) in enumerate(((wq_ref, wq_half), (wk_ref, wk_half), (wv_ref, wv_half)))
    ]
    for copy in copies:
        copy.start()
    x = own_ref[...].astype(F32)
    y = other_ref[...].astype(F32)
    gain = gain_first_ref[...].reshape(1, width)
    act = jnp.concatenate(
        [(x * root_mean(x) * gain).astype(BF16), (y * root_mean(y) * gain).astype(BF16)], axis=0
    )
    act_ref[...] = act
    for copy in copies:
        copy.wait()
    queries = dot(act, wq_half[...]).astype(BF16)
    keys = dot(act, wk_half[...]).astype(BF16)
    values = dot(act, wv_half[...]).astype(BF16)
    query_ref[...] = queries
    key_ref[...] = keys
    value_ref[...] = values
    for i in range(4):
        flush(i)
    low_half = lax.broadcasted_iota(jnp.int32, (2 * rows, 2 * size), 1) < size
    for pair in range(heads // 4):
        lanes = slice(pair * 2 * size, (pair + 1) * 2 * size)
        for side in range(2):
            head = 2 * pair + side
            window = win_ref[pl.ds(core * (heads // 2) + head, 1), :]
            same = toeplitz(window[:, : 2 * rows], rows)
            ahead = toeplitz(window[:, 2 * rows : 4 * rows], rows)
            behind = toeplitz(window[:, 4 * rows :], rows)
            first = jnp.where(core == 1, ahead, behind)
            second = jnp.where(core == 1, behind, ahead)
            bias = jnp.concatenate(
                [
                    jnp.concatenate([same, first], axis=1),
                    jnp.concatenate([second, same], axis=1),
                ],
                axis=0,
            )
            probs_ref[head] = attend(
                queries[:, lanes], keys[:, lanes], scale, bias, side, low_half
            )


def expert_kernel(
    capacity,
    chunk,
    wait,
    flush,
    arrived_ref,
    router_ref,
    in_own_ref,
    in_other_ref,
    down_own_ref,
    down_other_ref,
    after_ref,
    hid_own_ref,
    pre_own_ref,
    sent_ref,
    bundle_ref,
    grad_ref,
    produced_ref,
    router_grad_ref,
    in_vmem,
    down_vmem,
    bundle,
    sems,
):
    total = arrived_ref.shape[0]
    experts, width = router_ref.shape
    slots = total // experts
    hidden = in_own_ref.shape[1]
    steps = hidden // chunk
    mine = lax.axis_index("expert")
    core = lax.axis_index("ffn")
    copies = []
    for side, (win, wdown) in enumerate(
        ((in_own_ref, down_own_ref), (in_other_ref, down_other_ref))
    ):
        for step in range(steps):
            i = side * steps + step
            span = pl.ds(step * chunk, chunk)
            copies.append(
                (
                    pltpu.make_async_copy(win.at[:, span], in_vmem.at[i], sems.at[0, i]),
                    pltpu.make_async_copy(wdown.at[span, :], down_vmem.at[i], sems.at[1, i]),
                )
            )
    for copy in copies[0]:
        copy.start()
    for i in (0, 1):
        wait(i)
    for pair in copies[1:]:
        for copy in pair:
            copy.start()
    flat = arrived_ref[:, :width]
    cot = arrived_ref[:, width : 2 * width]
    filled = arrived_ref[:, 2 * width :]
    row = lax.broadcasted_iota(jnp.int32, (total, total), 0)
    col = lax.broadcasted_iota(jnp.int32, (total, total), 1)
    shift = slots.bit_length() - 1
    row_block = jnp.right_shift(row, shift)
    col_block = jnp.right_shift(col, shift)
    before = (col_block < row_block).astype(F32).astype(BF16)
    ahead = (col_block < row_block + core).astype(F32).astype(BF16)
    slot = jnp.bitwise_and(lax.broadcasted_iota(jnp.int32, (total, 1), 0), slots - 1)
    position = dot(before, filled)[:, 0:1] + dot(ahead, filled)[:, 1:2] + slot.astype(F32)
    keep = jnp.where(position < capacity, 1.0, 0.0)
    logits = cols_by_cols(flat, router_ref[...])
    grown = jnp.exp(logits - jnp.max(logits, axis=-1, keepdims=True))
    router_probs = grown / jnp.sum(grown, axis=-1, keepdims=True)
    onehot = (lax.broadcasted_iota(jnp.int32, (total, experts), 1) == mine).astype(F32)
    gate = jnp.sum(router_probs * onehot, axis=-1, keepdims=True)
    sent = (cot.astype(F32) * (gate * keep)).astype(BF16)
    sent_ref[...] = sent
    flush(2)
    bundle[:, :width] = flat
    bundle[:, width : 2 * width] = sent
    writes = []

    def forward(first, size):
        span = pl.ds(first, size)
        write = pltpu.make_async_copy(
            bundle.at[:, span], bundle_ref.at[:, span], sems.at[2, len(writes)]
        )
        write.start()
        writes.append(write)

    forward(0, 2 * width)
    produced = jnp.zeros((total, width), F32)
    grad = jnp.zeros((total, width), F32)
    inner = math.sqrt(2.0 / math.pi)
    for i, pair in enumerate(copies):
        own_side = i < steps
        first = (i % steps) * chunk
        for copy in pair:
            copy.wait()
        win, wdown = in_vmem[i], down_vmem[i]
        pre = dot(flat, win)
        square = pre * pre
        curve = jnp.tanh(inner * pre * (1.0 + 0.044715 * square))
        half_up = 0.5 + 0.5 * curve
        act = (pre * half_up).astype(BF16)
        slope = half_up + (0.5 * inner) * pre * (1.0 - curve * curve) * (
            1.0 + (3 * 0.044715) * square
        )
        grad_pre = (slope * cols_by_cols(sent, wdown)).astype(BF16)
        if own_side:
            hid_own_ref[:, first : first + chunk] = act
            pre_own_ref[:, first : first + chunk] = grad_pre
        else:
            first += 2 * width
            bundle[:, first : first + chunk] = act
            bundle[:, first + hidden : first + hidden + chunk] = grad_pre
            forward(first, chunk)
            forward(first + hidden, chunk)
        if i + 1 == steps:
            flush(0)
            flush(1)
        produced = produced + dot(act, wdown)
        grad = grad + cols_by_cols(grad_pre, win)
    produced_low = produced.astype(BF16)
    kept = produced_low.astype(F32) * keep
    produced_ref[...] = kept.astype(BF16)
    flush(5)
    grad_gate = jnp.sum(cot.astype(F32) * kept, axis=-1, keepdims=True)
    grad_logits = ((grad_gate * gate) * (onehot - router_probs)).astype(BF16)
    grad_ref[...] = (grad * keep + dot(grad_logits, router_ref[...])).astype(BF16)
    flush(4)
    router_grad_ref[...] = rows_by_rows(grad_logits, flat)
    for write in writes:
        write.wait()


def expert_weights_kernel(
    flat_own, sent_own, hid_own, pre_own, flat_other, sent_other, hid_other, pre_other, in_ref, down_ref
):
    in_ref[0] = rows_by_rows(flat_own[...], pre_own[...]) + rows_by_rows(
        flat_other[...], pre_other[...]
    )
    down_ref[0] = rows_by_rows(hid_own[...], sent_own[...]) + rows_by_rows(
        hid_other[...], sent_other[...]
    )


def expert_weights(flat, sent, hid, pre, bundle, chunk):
    total, width = sent.shape
    hidden = hid.shape[1]
    steps = hidden // chunk
    skip = 2 * width // chunk
    whole = pl.BlockSpec((total, width), lambda i: (0, 0))
    second = pl.BlockSpec((total, width), lambda i: (0, 1))
    part = pl.BlockSpec((total, chunk), lambda i: (0, i))
    return pl.pallas_call(
        expert_weights_kernel,
        grid=(steps,),
        out_shape=[
            jax.ShapeDtypeStruct((1, width, hidden), F32),
            jax.ShapeDtypeStruct((1, hidden, width), F32),
        ],
        in_specs=[
            whole,
            whole,
            part,
            part,
            whole,
            second,
            pl.BlockSpec((total, chunk), lambda i: (0, i + skip)),
            pl.BlockSpec((total, chunk), lambda i: (0, i + skip + steps)),
        ],
        out_specs=[
            pl.BlockSpec((1, width, chunk), lambda i: (0, 0, i)),
            pl.BlockSpec((1, chunk, width), lambda i: (0, i, 0)),
        ],
        compiler_params=pltpu.CompilerParams(vmem_limit_bytes=64 * 2**20),
        cost_estimate=pl.CostEstimate(
            flops=8 * total * width * hidden, bytes_accessed=14000000, transcendentals=0
        ),
    )(flat, sent, hid, pre, bundle, bundle, bundle, bundle)


def middle_back(returned, fetch, middle, gain, cot):
    grad = dot(fetch, returned)
    root = root_mean(middle)
    scaled = middle * root
    up = gain * grad
    grad_middle = cot.astype(F32) + root * (
        up - scaled * jnp.mean(up * scaled, axis=-1, keepdims=True)
    )
    return grad_middle, grad * scaled


def bit_of(step, other=0):
    return jnp.where(lax.axis_index("ffn") == other, step[0], step[1])


def chunk_place(chunk, order, levels, other=0):
    chip = lax.axis_index("expert")
    mine = 0
    for step in order[:levels]:
        mine = mine * 2 + jnp.bitwise_and(jnp.right_shift(chip, bit_of(step, other)), 1)
    return jnp.bitwise_xor(mine, chunk)


def small_rows(experts):
    return [0, 2, 4, 16, 16 + experts, 16 + 2 * experts]


def backward_kernel(
    heads,
    orders,
    levels,
    wait,
    flush,
    returned_ref,
    returned_other_ref,
    fetch_ref,
    fetch_other_ref,
    middle_ref,
    middle_other_ref,
    cot_ref,
    cot_other_ref,
    gain_second_ref,
    mixed_own_ref,
    mixed_other_ref,
    value_ref,
    probs_ref,
    key_ref,
    query_ref,
    act_ref,
    hot_ref,
    own_ref,
    other_ref,
    router_ref,
    after_ref,
    wo_ref,
    wq_ref,
    wk_ref,
    wv_ref,
    keep_0_ref,
    send_0_ref,
    keep_1_ref,
    send_1_ref,
    keep_2_ref,
    send_2_ref,
    grad_middle_ref,
    small_ref,
    input_own_ref,
    input_other_ref,
    wo_half,
    wq_half,
    wk_half,
    wv_half,
    part_0,
    part_1,
    part_2,
    small,
    sems,
):
    rows, width = middle_ref.shape
    size = width // heads
    part = width // 2
    experts = router_ref.shape[0]
    scale = 1.0 / math.sqrt(size)
    core = lax.axis_index("ffn")
    span = pl.ds(pl.multiple_of(core * part, LANES), part)
    copies = [
        pltpu.make_async_copy(src, half, sems.at[6 + i])
        for i, (src, half) in enumerate(
            (
                (wo_ref.at[span, :], wo_half),
                (wq_ref.at[:, span], wq_half),
                (wk_ref.at[:, span], wk_half),
                (wv_ref.at[:, span], wv_half),
            )
        )
    ]
    for copy in copies:
        copy.start()
    parts = (part_0, part_1, part_2)
    halves = ((keep_0_ref, send_0_ref), (keep_1_ref, send_1_ref), (keep_2_ref, send_2_ref))
    third = width // 3
    height = third >> levels
    writes = []
    for p, pair in enumerate(halves):
        rows_half = pair[0].shape[0]
        for i, ref in enumerate(pair):
            writes.append(
                pltpu.make_async_copy(
                    parts[p].at[pl.ds(i * rows_half, rows_half), :], ref, sems.at[2 * p + i]
                )
            )
    places = [
        [chunk_place(chunk, order, levels) * (4 * height) for chunk in range(2**levels)]
        for order in orders
    ]

    def pack(matrix, value):
        for p, ref in enumerate(parts):
            for chunk in range(2**levels):
                first = p * third + chunk * height
                at = pl.multiple_of(places[p][chunk] + matrix * height, 16)
                ref[pl.ds(at, height), :] = value[first : first + height]

    for i in range(9):
        wait(i)
    copies[0].wait()
    gain = gain_second_ref[...].reshape(1, width)
    grad_own, gain_terms = middle_back(
        returned_ref[...], fetch_ref[...], middle_ref[...], gain, cot_ref[...]
    )
    grad_other, _ = middle_back(
        returned_other_ref[...], fetch_other_ref[...], middle_other_ref[...], gain, cot_other_ref[...]
    )
    gain_second = jnp.sum(gain_terms, axis=0, keepdims=True)
    grad_middle_ref[...] = grad_own
    flush(6)
    grad_low = jnp.concatenate([grad_own, grad_other], axis=0).astype(BF16)
    grad_mixed = cols_by_cols(grad_low, wo_half[...]).astype(BF16)
    for i in range(9, 20):
        wait(i)
    for copy in copies[1:]:
        copy.wait()
    mixed = jnp.concatenate([mixed_own_ref[...], mixed_other_ref[...]], axis=0)
    grad_columns = jnp.where(core == 0, grad_low[:, :part], grad_low[:, part:])
    pack(3, rows_by_rows(mixed, grad_columns).astype(BF16))
    low_half = lax.broadcasted_iota(jnp.int32, (2 * rows, 2 * size), 1) < size
    grad_q, grad_k, grad_v = [], [], []
    same, ahead, behind = [], [], []
    for pair in range(heads // 4):
        lanes = slice(pair * 2 * size, (pair + 1) * 2 * size)
        query, key, value = query_ref[:, lanes], key_ref[:, lanes], value_ref[:, lanes]
        grad_pair = grad_mixed[:, lanes]
        got_q, got_k, got_v = [], [], []
        for side in range(2):
            probs = probs_ref[2 * pair + side]
            keep_lanes = low_half if side == 0 else jnp.logical_not(low_half)
            own_grad = jnp.where(keep_lanes, grad_pair, 0).astype(BF16)
            grad_probs = cols_by_cols(own_grad, value)
            got_v.append(rows_by_rows(probs.astype(BF16), grad_pair))
            inner = jnp.sum(probs * grad_probs, axis=-1, keepdims=True)
            grad_scores = probs * (grad_probs - inner)
            same.append(
                diagonal_sums(grad_scores[:rows, :rows] + grad_scores[rows:, rows:], rows)
            )
            first = diagonal_sums(grad_scores[:rows, rows:], rows)
            second = diagonal_sums(grad_scores[rows:, :rows], rows)
            ahead.append(jnp.where(core == 1, first, second))
            behind.append(jnp.where(core == 1, second, first))
            grad_raw = (grad_scores * scale).astype(BF16)
            got_q.append(dot(grad_raw, key))
            got_k.append(rows_by_rows(grad_raw, query))
        grad_q.append(jnp.where(low_half, got_q[0], got_q[1]).astype(BF16))
        grad_k.append(jnp.where(low_half, got_k[0], got_k[1]).astype(BF16))
        grad_v.append(jnp.where(low_half, got_v[0], got_v[1]).astype(BF16))
    grad_q = jnp.concatenate(grad_q, axis=1)
    grad_k = jnp.concatenate(grad_k, axis=1)
    grad_v = jnp.concatenate(grad_v, axis=1)
    act = act_ref[...]
    pack(0, rows_by_rows(act, grad_q).astype(BF16))
    pack(1, rows_by_rows(act, grad_k).astype(BF16))
    pack(2, rows_by_rows(act, grad_v).astype(BF16))
    for write in writes:
        write.start()
    grad_act = (
        cols_by_cols(grad_q, wq_half[...])
        + cols_by_cols(grad_k, wk_half[...])
        + cols_by_cols(grad_v, wv_half[...])
    )
    input_other_ref[...] = grad_act[rows:].astype(BF16)
    flush(9)
    input_own_ref[...] = grad_act[:rows]
    flush(8)
    x = own_ref[...].astype(F32)
    y = other_ref[...].astype(F32)
    gain_first = jnp.sum(
        grad_act[:rows] * (x * root_mean(x)) + grad_act[rows:] * (y * root_mean(y)),
        axis=0,
        keepdims=True,
    )
    sums = jnp.concatenate(
        [jnp.concatenate(part_sums, axis=0) for part_sums in (same, ahead, behind)], axis=1
    )
    table = lax.dot_general(
        sums,
        hot_ref[...],
        (((1,), (1,)), ((), ())),
        precision=TOP_PRECISION,
        preferred_element_type=F32,
    )
    at = small_rows(experts)
    small[: at[3]] = jnp.zeros((at[3], part), F32)
    for i, value in enumerate((gain_first, gain_second)):
        small[at[i] : at[i] + 1] = value[:, :part]
        small[at[i] + 1 : at[i] + 2] = value[:, part:]
    small[at[2] : at[2] + heads // 2, : table.shape[1]] = table
    small[at[3] : at[4]] = router_ref[:, :part]
    small[at[4] : at[5]] = router_ref[:, part:]
    small_ref[...] = small[...].astype(BF16)
    flush(7)
    for write in writes:
        write.wait()


def assemble_kernel(orders, levels, sides, upper, last, wait, flush, *refs):
    count = len(orders) * len(sides)
    arrays, refs = refs[:count], refs[count:]
    if last is not None:
        experts, heads = last
        (small_own_ref, small_other_ref), refs = refs[:2], refs[2:]
        last_inputs = (count, count + 1)
    if upper:
        refs = refs[4:]
    outs, (wide, sems) = refs[:4], refs[-2:]
    if last is not None:
        gain_first_ref, gain_second_ref, table_ref, router_ref = refs[4:8]
    width = outs[0].shape[1]
    part = width // 2
    third = width // 3
    span = third // 2
    height = third >> levels
    half = 2 ** (levels - 1)
    core = lax.axis_index("ffn")
    mine = lax.axis_index("expert")
    columns = [
        pl.ds(pl.multiple_of((1 - core if side else core) * part, LANES), part) for side in sides
    ]
    writes = []
    for p, order in enumerate(orders):
        for i, side in enumerate(sides):
            n = len(sides) * p + i
            wait(n)
            bit = jnp.bitwise_and(jnp.right_shift(mine, bit_of(order[0], side)), 1)
            if upper:
                bit = 1 - bit
            first = pl.multiple_of(p * third + bit * span, span)
            places = [
                jnp.bitwise_and(chunk_place(low, order, levels, side), half - 1)
                for low in range(half)
            ]
            for matrix in range(4):
                for low in range(half):
                    at = pl.multiple_of((places[low] * 4 + matrix) * height, height)
                    wide[n, matrix, pl.ds(low * height, height)] = arrays[n][
                        pl.ds(at, height), :
                    ].astype(F32)
                write = pltpu.make_async_copy(
                    wide.at[n, matrix],
                    outs[matrix].at[pl.ds(first, span), columns[i]],
                    sems.at[4 * n + matrix],
                )
                write.start()
                writes.append(write)
    if last is not None:
        for i in last_inputs:
            wait(i)
        at = small_rows(experts)
        mine, other = small_own_ref[...], small_other_ref[...]
        both = mine + other
        gain_first_ref[...] = jnp.concatenate([both[0:1], both[1:2]], axis=1).reshape(width)
        gain_second_ref[...] = jnp.concatenate([both[2:3], both[3:4]], axis=1).reshape(width)
        buckets = table_ref.shape[1]
        low = mine[at[2] : at[2] + heads // 2, :buckets]
        high = other[at[2] : at[2] + heads // 2, :buckets]
        table_ref[...] = jnp.where(
            core == 0,
            jnp.concatenate([low, high], axis=0),
            jnp.concatenate([high, low], axis=0),
        )
        router_ref[...] = jnp.concatenate([both[at[3] : at[4]], both[at[4] : at[5]]], axis=1)
    for write in writes:
        write.wait()


def assemble(orders, levels, sides, arrays, width, earlier=(), smalls=(), last=None):
    tail = []
    modes = "l" * len(arrays)
    if last is not None:
        experts, heads, buckets = last
        tail = [((width,), F32), ((width,), F32), ((heads, buckets), F32), ((experts, width), F32)]
        modes += "ll"
        last = (experts, heads)
    first = len(modes)
    modes += "r" * len(earlier)
    return call(
        functools.partial(assemble_kernel, orders, levels, sides, bool(earlier), last),
        [((width, width), F32)] * 4 + tail,
        (*arrays, *smalls, *earlier),
        modes + "rrrr" + "h" * len(tail),
        vmem=16,
        aliases={first + i: i for i in range(len(earlier))},
        scratch=[
            pltpu.VMEM((len(arrays), 4, width // 6, width // 2), F32),
            pltpu.SemaphoreType.DMA((4 * len(arrays),)),
        ],
        nbytes=8000000,
    )


def swap(x):
    return lax.ppermute(x, "ffn", [(0, 1), (1, 0)])


def flip(x, step):
    pairs = []
    for chip in range(lax.axis_size("expert")):
        for core in range(2):
            pairs.append((chip * 2 + core, (chip ^ (1 << step[core])) * 2 + core))
    return lax.ppermute(x, ("expert", "ffn"), pairs)


def add_low(left, right):
    return (left.astype(F32) + right.astype(F32)).astype(BF16)


def sum_over_chips(keeps, sends, orders, levels, small, beside):
    count = len(orders[0])
    todo = [set(step[core] for step in orders[0]) for core in range(2)]
    ridden = set()

    def exchange(phase, x, bit):
        nonlocal small
        fresh = all(bit[core] in todo[core] for core in range(2))
        if not fresh or phase in ridden or phase < 2 or phase > 2 * count - 3:
            return flip(x, bit)
        for core in range(2):
            todo[core].discard(bit[core])
        ridden.add(phase)
        sent = small.astype(BF16)
        got = flip(jnp.concatenate([x, sent]), bit)
        rows = x.shape[0]
        small = sent.astype(F32) + got[rows:].astype(F32)
        return got[:rows]

    def mine(bit):
        return (lax.axis_index("expert") >> bit_of(bit)) & 1

    whole = [None] * len(orders)
    for k in range(count - 1):
        for p, order in enumerate(orders):
            keep, got = keeps[p], exchange(k, sends[p], order[k])
            half = keep.shape[0] // 2
            if k + 2 == count:
                whole[p] = add_low(keep, got)
            elif k + 1 < levels:
                keeps[p] = add_low(keep[:half], got[:half])
                sends[p] = add_low(keep[half:], got[half:])
            else:
                both = add_low(keep, got)
                upper = mine(order[k + 1])
                keeps[p] = lax.dynamic_slice_in_dim(both, upper * half, half, 0)
                sends[p] = lax.dynamic_slice_in_dim(both, (1 - upper) * half, half, 0)
    ended = [None] * len(orders)
    for p, order in enumerate(orders):
        ended[p] = exchange(count - 1, whole[p], order[-1])
    for p, ahead in ((1, None), (2, 1), (0, 1)):
        x = whole[p]
        if ahead is not None:
            x, whole[ahead] = lax.optimization_barrier((x, whole[ahead]))
        whole[p] = add_low(x, ended[p])
    got = [None] * len(orders)
    for k in reversed(range(count - 1)):
        for p, order in enumerate(orders):
            x = whole[p]
            got[p] = exchange(2 * count - 2 - k, x, order[k])
            if k == 0:
                continue
            if k < levels:
                whole[p] = jnp.concatenate([x, got[p]])
            else:
                whole[p] = jnp.where(
                    mine(order[k]) == 1,
                    jnp.concatenate([got[p], x]),
                    jnp.concatenate([x, got[p]]),
                )
    for bit in zip(sorted(todo[0]), sorted(todo[1])):
        sent = small.astype(BF16)
        small = sent.astype(F32) + flip(sent, bit).astype(F32)
    return whole, got, small, beside


def shards(
    tokens,
    norm_first,
    w_query,
    w_key,
    w_value,
    w_out,
    bucket_bias_table,
    norm_second,
    w_router,
    w_in,
    w_down,
    expert_ids,
    cotangent,
):
    rows, width = tokens.shape
    buckets, heads = bucket_bias_table.shape
    pair = lax.axis_size("ffn")
    experts = w_router.shape[1]
    total = 2 * rows
    capacity = 5 * rows * pair // 4
    hidden = w_in.shape[2]
    part = width // 2
    hot = jnp.asarray(bucket_windows(rows, buckets, REACH))
    router = w_router.T

    other = swap(tokens)
    ids = expert_ids.reshape(1, rows)
    ids_other = swap(ids)
    middle, gate, outgoing, mixed, windows, fetch, fetch_other, root = call(
        functools.partial(forward_kernel, heads),
        [
            ((rows, width), F32),
            ((rows, LANES), F32),
            ((total, 2 * width + LANES), BF16),
            ((rows, width), BF16),
            ((heads, 6 * rows), F32),
            ((rows, total), BF16),
            ((rows, total), BF16),
            ((rows, LANES), F32),
        ],
        (
            tokens,
            other,
            norm_first,
            ids,
            ids_other,
            bucket_bias_table.T,
            hot,
            w_key,
            w_value,
            w_query,
            w_out,
            norm_second,
            router,
            cotangent,
        ),
        "hhhhhhhlllslll" + "hhrhhhhh",
        vmem=64,
        flops=3000000000,
        scratch=[
            pltpu.VMEM((heads, rows, 2 * rows), F32),
            pltpu.VMEM((total, 2 * width + LANES), BF16),
            pltpu.SemaphoreType.DMA((2,)),
        ],
    )
    arrived = lax.all_to_all(outgoing, "expert", 0, 0, tiled=True)
    gate, w_in, w_down, cot_own = lax.optimization_barrier((gate, w_in, w_down, cotangent))
    in_own, down_own = w_in[0], w_down[0]
    in_other, down_other = swap(in_own), swap(down_own)
    cot_other = swap(cot_own)
    mixed_other, middle_other = swap(mixed), swap(middle)
    act, queries, keys, values, probs = call(
        functools.partial(halves_kernel, heads),
        [
            ((2 * rows, width), BF16),
            ((2 * rows, part), BF16),
            ((2 * rows, part), BF16),
            ((2 * rows, part), BF16),
            ((heads // 2, 2 * rows, 2 * rows), F32),
        ],
        (tokens, other, norm_first, w_query, w_key, w_value, windows, gate),
        "hhhrrrhr" + "hhhhh",
        vmem=64,
        flops=3000000000,
        scratch=[pltpu.VMEM((width, part), BF16)] * 3 + [pltpu.SemaphoreType.DMA((3,))],
    )
    chunk = hidden // 2
    steps = 2 * hidden // chunk
    hid_own, pre_own, sent, bundle, grad_slots, produced, router_part = call(
        functools.partial(expert_kernel, capacity, chunk),
        [
            ((total, hidden), BF16),
            ((total, hidden), BF16),
            ((total, width), BF16),
            ((total, 2 * width + 2 * hidden), BF16),
            ((total, width), BF16),
            ((total, width), BF16),
            ((experts, width), F32),
        ],
        (arrived, router, in_own, in_other, down_own, down_other, act),
        "llrrrrr" + "hhhrhhh",
        vmem=64,
        flops=6000000000,
        scratch=[
            pltpu.VMEM((steps, width, chunk), BF16),
            pltpu.VMEM((steps, chunk, width), BF16),
            pltpu.VMEM((total, 2 * width + 2 * hidden), BF16),
            pltpu.SemaphoreType.DMA((3, steps + 1)),
        ],
    )
    bundle_other = swap(bundle)
    grad_returned = lax.all_to_all(grad_slots, "expert", 0, 0, tiled=True)
    grad_w_in, grad_w_down = expert_weights(arrived, sent, hid_own, pre_own, bundle_other, 256)
    produced, grad_returned, grad_w_in = lax.optimization_barrier(
        (produced, grad_returned, grad_w_in)
    )
    produced_returned = lax.all_to_all(produced, "expert", 0, 0, tiled=True)
    bits = experts.bit_length() - 1
    levels = min(bits - 1, 3)
    rest = [(bit, bit) for bit in range(3, bits)]
    orders = [
        [(0, 2), (1, 0), (2, 1)] + rest,
        [(1, 0), (2, 1), (0, 2)] + rest,
        [(2, 1), (0, 2), (1, 0)] + rest,
    ]
    third = 4 * width // 3
    *halves, grad_middle, small, input_own, input_other = call(
        functools.partial(backward_kernel, heads, orders, levels),
        [((third // 2, part), BF16)] * 6
        + [
            ((rows, width), F32),
            ((16 + 2 * experts, part), BF16),
            ((rows, width), F32),
            ((rows, width), BF16),
        ],
        (
            grad_returned,
            swap(grad_returned),
            fetch,
            fetch_other,
            middle,
            middle_other,
            cotangent,
            cot_other,
            norm_second,
            mixed,
            mixed_other,
            values,
            probs,
            keys,
            queries,
            act,
            hot,
            tokens,
            other,
            router_part,
            grad_w_in,
            w_out,
            w_query,
            w_key,
            w_value,
        ),
        "l" * 20 + "rrrrr" + "rrrrrr" + "hhhh",
        vmem=56,
        flops=4000000000,
        scratch=[
            pltpu.VMEM((part, width), BF16),
            *[pltpu.VMEM((width, part), BF16)] * 3,
            *[pltpu.VMEM((third, part), BF16)] * 3,
            pltpu.VMEM((16 + 2 * experts, part), F32),
            pltpu.SemaphoreType.DMA((10,)),
        ],
    )
    keeps, grad_middle, small, input_own, input_other, produced_returned = (
        lax.optimization_barrier(
            (halves[0::2], grad_middle, small, input_own, input_other, produced_returned)
        )
    )
    beside = (grad_middle, input_own, swap(input_other), produced_returned)
    kept, got, small, beside = sum_over_chips(
        list(keeps), list(halves[1::2]), orders, levels, small, beside
    )
    grad_middle, input_own, input_swapped, produced_returned = beside
    root = root[:, :1]
    scaled = tokens.astype(F32) * root
    up = norm_first * (input_own + input_swapped.astype(F32))
    grad_input = grad_middle + root * (
        up - scaled * jnp.mean(up * scaled, axis=-1, keepdims=True)
    )
    expert_branch = gate[:, :1] * dot(fetch, produced_returned)
    output = (middle + expert_branch).astype(BF16)
    near = []
    for rows_kept in kept:
        near += [rows_kept, swap(rows_kept)]
    small_other = swap(small)
    *matrices, gain_first, gain_second, table, router_sum = assemble(
        orders,
        levels,
        (0, 1),
        near,
        width,
        smalls=(small, small_other),
        last=(experts, heads, buckets),
    )
    got, matrices, output, expert_branch, grad_input = lax.optimization_barrier(
        (got, matrices, output, expert_branch, grad_input)
    )
    far = [swap(rows_got) for rows_got in got]
    matrices = assemble(orders, levels, (0,), got, width, matrices)
    matrices = assemble(orders, levels, (1,), far, width, matrices)
    return (
        output,
        grad_input,
        gain_first,
        *matrices,
        table.T,
        gain_second,
        router_sum.T,
        grad_w_in,
        grad_w_down,
        expert_branch,
    )


def solution(mesh):
    placed = (
        P(("expert", "ffn"), None),
        P(),
        P(),
        P(),
        P(),
        P(),
        P(),
        P(),
        P(),
        P("expert", None, "ffn"),
        P("expert", "ffn", None),
        P(("expert", "ffn")),
        P(("expert", "ffn"), None),
    )
    return jax.shard_map(
        shards,
        mesh=mesh,
        in_specs=placed,
        out_specs=(
            P(("expert", "ffn"), None),
            P(("expert", "ffn"), None),
            P(),
            P(),
            P(),
            P(),
            P(),
            P(),
            P(),
            P(),
            P("expert", None, "ffn"),
            P("expert", "ffn", None),
            P(("expert", "ffn"), None),
        ),
        check_vma=False,
    )
```

```python
import functools
import math

import jax
import jax.numpy as jnp
import numpy as np
from jax import lax
from jax.experimental import pallas as pl
from jax.experimental.pallas import tpu as pltpu
from jax.sharding import PartitionSpec as P

REACH = 128
EPS = 1e-06
TOP_PRECISION = lax.Precision.HIGHEST
LANES = 128
F32 = jnp.float32
BF16 = jnp.bfloat16


def bucket_of(distance, buckets, reach):
    half = buckets // 2
    exact = half // 2
    result = np.where(distance < 0, half, 0)
    magnitude = np.abs(distance)
    spread = exact + np.floor(
        np.log(np.maximum(magnitude, 1) / exact) / np.log(reach / exact) * (half - exact)
    )
    spread = np.minimum(spread, half - 1)
    return result + np.where(magnitude < exact, magnitude, spread)


def bucket_windows(rows, buckets, reach):
    lane = np.arange(2 * rows)
    offset = np.where(lane < rows, -lane, 2 * rows - lane)
    windows = []
    for shift in (0, rows, -rows):
        hot = bucket_of(offset + shift, buckets, reach)[None, :] == np.arange(buckets)[:, None]
        hot[:, rows] = False
        windows.append(hot)
    return np.concatenate(windows, axis=1).astype(np.float32)


def rows_by_rows(left, right):
    return lax.dot_general(left, right, (((0,), (0,)), ((), ())), preferred_element_type=F32)


def cols_by_cols(left, right):
    return lax.dot_general(left, right, (((1,), (1,)), ((), ())), preferred_element_type=F32)


def dot(left, right):
    return jnp.dot(left, right, preferred_element_type=F32)


def root_mean(x):
    return lax.rsqrt(jnp.mean(x * x, axis=-1, keepdims=True) + EPS)


def call(body, outs, args, modes, vmem=16, flops=0, scratch=(), aliases=None, nbytes=1000000):
    count, total = len(args), len(args) + len(outs)
    shapes = [(a.shape, a.dtype) for a in args] + list(outs)
    moved = [i for i in range(total) if modes[i] in "hls"]
    buffers = [pltpu.VMEM(*shapes[i]) for i in moved]

    def kernel(*refs):
        bodies = list(refs[:total])
        for i, ref in zip(moved, refs[total : total + len(moved)]):
            bodies[i] = ref
        extra = refs[total + len(moved) : -1]
        sems = refs[-1]
        copies = {}
        for i in moved:
            ends = (refs[i], bodies[i]) if i < count else (bodies[i], refs[i])
            copies[i] = pltpu.make_async_copy(*ends, sems.at[i])
        for i in moved:
            if i < count and modes[i] != "s":
                copies[i].start()
        flushed = set()

        def wait(i):
            copies[i].wait()

        wait.start = lambda i: copies[i].start()

        def flush(i):
            flushed.add(i)
            copies[count + i].start()

        for i in moved:
            if i < count and modes[i] == "h":
                wait(i)
        body(wait, flush, *bodies, *extra)
        for i in moved:
            if i >= count and i - count not in flushed:
                copies[i].start()
        for i in moved:
            if i >= count:
                copies[i].wait()

    specs = [pl.BlockSpec(memory_space=pltpu.HBM)] * total
    return pl.pallas_call(
        kernel,
        out_shape=[jax.ShapeDtypeStruct(s, d) for s, d in outs],
        in_specs=specs[:count],
        out_specs=specs[count:],
        scratch_shapes=buffers + list(scratch) + [pltpu.SemaphoreType.DMA((total,))],
        input_output_aliases=aliases or {},
        compiler_params=pltpu.CompilerParams(vmem_limit_bytes=vmem * 2**20),
        cost_estimate=pl.CostEstimate(flops=flops, bytes_accessed=nbytes, transcendentals=0),
    )(*args)


def toeplitz(window, rows):
    wide = jnp.broadcast_to(window, (rows, 2 * rows))
    return pltpu.roll(wide, 0, 1, stride=1, stride_axis=0)[:, :rows]


def diagonal_sums(square, rows):
    wide = jnp.concatenate([square, jnp.zeros_like(square)], axis=1)
    height = rows
    while height > 1:
        height //= 2
        wide = wide[:height] + pltpu.roll(wide[height:], 2 * rows - height, 1)
    return wide


def placement(ids, experts, total):
    rows = ids.shape[1]
    slots = total // experts
    choose = (lax.broadcasted_iota(jnp.int32, (experts, rows), 0) == ids).astype(F32)
    earlier = (
        lax.broadcasted_iota(jnp.int32, (rows, rows), 0)
        < lax.broadcasted_iota(jnp.int32, (rows, rows), 1)
    ).astype(F32)
    ranks = dot(choose.astype(BF16), earlier.astype(BF16))
    rank = jnp.sum(choose * ranks, axis=0, keepdims=True)
    target = ids * slots + rank.astype(jnp.int32)
    place = (lax.broadcasted_iota(jnp.int32, (total, rows), 0) == target).astype(F32)
    return choose, place


def attend(query_pair, key_pair, scale, bias, side, low_half):
    own = jnp.where(low_half if side == 0 else jnp.logical_not(low_half), query_pair, 0)
    scores = cols_by_cols(own.astype(BF16), key_pair) * scale + bias
    grown = jnp.exp(scores - jnp.max(scores, axis=-1, keepdims=True))
    return grown * (1.0 / jnp.sum(grown, axis=-1, keepdims=True))


def forward_kernel(
    heads,
    wait,
    flush,
    own_ref,
    other_ref,
    gain_first_ref,
    ids_ref,
    ids_other_ref,
    table_ref,
    hot_ref,
    wk,
    wv,
    wq,
    wo,
    gain_second_ref,
    router_ref,
    cot_ref,
    middle_ref,
    gate_ref,
    out_ref,
    mixed_ref,
    win_ref,
    fetch_ref,
    fetch_other_ref,
    root_ref,
    bias,
    staged,
    sems,
):
    rows, width = own_ref.shape
    size = width // heads
    scale = 1.0 / math.sqrt(size)
    core = lax.axis_index("ffn")
    wait.start(10)
    total = out_ref.shape[0]
    experts = router_ref.shape[0]
    sends = [
        pltpu.make_async_copy(staged.at[:, span], out_ref.at[:, span], sems.at[i])
        for i, span in enumerate((pl.ds(width, width + LANES), pl.ds(0, width)))
    ]
    choose, place = placement(ids_ref[...], experts, total)
    _, place_other = placement(ids_other_ref[...], experts, total)
    fetch_ref[...] = place.T.astype(BF16)
    fetch_other_ref[...] = place_other.T.astype(BF16)
    choose = choose.T
    lane = lax.broadcasted_iota(jnp.int32, (total, LANES), 1)
    staged[:, 2 * width :] = jnp.where(
        lane == 0,
        jnp.sum(place, axis=1, keepdims=True),
        jnp.sum(place_other, axis=1, keepdims=True),
    ).astype(BF16)
    place = place.astype(BF16)
    windows = jnp.dot(
        table_ref[...], hot_ref[...], precision=TOP_PRECISION, preferred_element_type=F32
    )
    win_ref[...] = windows
    for i in (4, 5, 6):
        flush(i)
    same = windows[:, : 2 * rows]
    apart = jnp.where(core == 1, windows[:, 2 * rows : 4 * rows], windows[:, 4 * rows :])
    for head in range(heads):
        bias[head, :, :rows] = toeplitz(same[head : head + 1], rows)
        bias[head, :, rows:] = toeplitz(apart[head : head + 1], rows)
    x = own_ref[...].astype(F32)
    y = other_ref[...].astype(F32)
    gain = gain_first_ref[...].reshape(1, width)
    root = root_mean(x)
    root_ref[...] = jnp.broadcast_to(root, root_ref.shape)
    flush(7)
    act_own = (x * root * gain).astype(BF16)
    act_other = (y * root_mean(y) * gain).astype(BF16)
    act = jnp.concatenate([act_own, act_other], axis=0)
    wait(13)
    staged[:, width : 2 * width] = dot(place, cot_ref[...]).astype(BF16)
    sends[0].start()
    wait(7)
    keys = dot(act, wk[...]).astype(BF16)
    wait(8)
    values = dot(act, wv[...]).astype(BF16)
    wait(9)
    queries = dot(act_own, wq[...]).astype(BF16)
    low_half = lax.broadcasted_iota(jnp.int32, (rows, 2 * size), 1) < size
    mixed = []
    for pair in range(heads // 2):
        lanes = slice(pair * 2 * size, (pair + 1) * 2 * size)
        outs = []
        for side in range(2):
            probs = attend(
                queries[:, lanes], keys[:, lanes], scale, bias[2 * pair + side], side, low_half
            )
            outs.append(dot(probs.astype(BF16), values[:, lanes]))
        mixed.append(jnp.where(low_half, outs[0], outs[1]).astype(BF16))
    mixed = jnp.concatenate(mixed, axis=1)
    mixed_ref[...] = mixed
    flush(3)
    for i in (10, 11, 12):
        wait(i)
    middle = x + dot(mixed, wo[...])
    middle_ref[...] = middle
    flush(0)
    gain_second = gain_second_ref[...].reshape(1, width)
    act_second = (middle * root_mean(middle) * gain_second).astype(BF16)
    staged[:, :width] = dot(place, act_second).astype(BF16)
    sends[1].start()
    logits = cols_by_cols(act_second, router_ref[...])
    grown = jnp.exp(logits - jnp.max(logits, axis=-1, keepdims=True))
    gate = jnp.sum(grown * choose, axis=-1, keepdims=True) / jnp.sum(
        grown, axis=-1, keepdims=True
    )
    gate_ref[...] = jnp.broadcast_to(gate, gate_ref.shape)
    flush(1)
    for send in sends:
        send.wait()


def halves_kernel(
    heads,
    wait,
    flush,
    own_ref,
    other_ref,
    gain_first_ref,
    wq_ref,
    wk_ref,
    wv_ref,
    win_ref,
    after_ref,
    act_ref,
    query_ref,
    key_ref,
    value_ref,
    probs_ref,
    wq_half,
    wk_half,
    wv_half,
    sems,
):
    rows, width = own_ref.shape
    size = width // heads
    part = width // 2
    scale = 1.0 / math.sqrt(size)
    core = lax.axis_index("ffn")
    columns = pl.ds(pl.multiple_of(core * part, LANES), part)
    copies = [
        pltpu.make_async_copy(ref.at[:, columns], half, sems.at[i])
        for i, (ref, half) in enumerate(((wq_ref, wq_half), (wk_ref, wk_half), (wv_ref, wv_half)))
    ]
    for copy in copies:
        copy.start()
    x = own_ref[...].astype(F32)
    y = other_ref[...].astype(F32)
    gain = gain_first_ref[...].reshape(1, width)
    act = jnp.concatenate(
        [(x * root_mean(x) * gain).astype(BF16), (y * root_mean(y) * gain).astype(BF16)], axis=0
    )
    act_ref[...] = act
    for copy in copies:
        copy.wait()
    queries = dot(act, wq_half[...]).astype(BF16)
    keys = dot(act, wk_half[...]).astype(BF16)
    values = dot(act, wv_half[...]).astype(BF16)
    query_ref[...] = queries
    key_ref[...] = keys
    value_ref[...] = values
    for i in range(4):
        flush(i)
    low_half = lax.broadcasted_iota(jnp.int32, (2 * rows, 2 * size), 1) < size
    for pair in range(heads // 4):
        lanes = slice(pair * 2 * size, (pair + 1) * 2 * size)
        for side in range(2):
            head = 2 * pair + side
            window = win_ref[pl.ds(core * (heads // 2) + head, 1), :]
            same = toeplitz(window[:, : 2 * rows], rows)
            ahead = toeplitz(window[:, 2 * rows : 4 * rows], rows)
            behind = toeplitz(window[:, 4 * rows :], rows)
            first = jnp.where(core == 1, ahead, behind)
            second = jnp.where(core == 1, behind, ahead)
            bias = jnp.concatenate(
                [
                    jnp.concatenate([same, first], axis=1),
                    jnp.concatenate([second, same], axis=1),
                ],
                axis=0,
            )
            probs_ref[head] = attend(
                queries[:, lanes], keys[:, lanes], scale, bias, side, low_half
            )


def expert_kernel(
    capacity,
    chunk,
    wait,
    flush,
    arrived_ref,
    router_ref,
    in_own_ref,
    in_other_ref,
    down_own_ref,
    down_other_ref,
    after_ref,
    hid_own_ref,
    pre_own_ref,
    sent_ref,
    bundle_ref,
    grad_ref,
    produced_ref,
    router_grad_ref,
    in_vmem,
    down_vmem,
    bundle,
    sems,
):
    total = arrived_ref.shape[0]
    experts, width = router_ref.shape
    slots = total // experts
    hidden = in_own_ref.shape[1]
    steps = hidden // chunk
    mine = lax.axis_index("expert")
    core = lax.axis_index("ffn")
    copies = []
    for side, (win, wdown) in enumerate(
        ((in_own_ref, down_own_ref), (in_other_ref, down_other_ref))
    ):
        for step in range(steps):
            i = side * steps + step
            span = pl.ds(step * chunk, chunk)
            copies.append(
                (
                    pltpu.make_async_copy(win.at[:, span], in_vmem.at[i], sems.at[0, i]),
                    pltpu.make_async_copy(wdown.at[span, :], down_vmem.at[i], sems.at[1, i]),
                )
            )
    for copy in copies[0]:
        copy.start()
    for i in (0, 1):
        wait(i)
    for pair in copies[1:]:
        for copy in pair:
            copy.start()
    flat = arrived_ref[:, :width]
    cot = arrived_ref[:, width : 2 * width]
    filled = arrived_ref[:, 2 * width :]
    row = lax.broadcasted_iota(jnp.int32, (total, total), 0)
    col = lax.broadcasted_iota(jnp.int32, (total, total), 1)
    shift = slots.bit_length() - 1
    row_block = jnp.right_shift(row, shift)
    col_block = jnp.right_shift(col, shift)
    before = (col_block < row_block).astype(F32).astype(BF16)
    ahead = (col_block < row_block + core).astype(F32).astype(BF16)
    slot = jnp.bitwise_and(lax.broadcasted_iota(jnp.int32, (total, 1), 0), slots - 1)
    position = dot(before, filled)[:, 0:1] + dot(ahead, filled)[:, 1:2] + slot.astype(F32)
    keep = jnp.where(position < capacity, 1.0, 0.0)
    logits = cols_by_cols(flat, router_ref[...])
    grown = jnp.exp(logits - jnp.max(logits, axis=-1, keepdims=True))
    router_probs = grown / jnp.sum(grown, axis=-1, keepdims=True)
    onehot = (lax.broadcasted_iota(jnp.int32, (total, experts), 1) == mine).astype(F32)
    gate = jnp.sum(router_probs * onehot, axis=-1, keepdims=True)
    sent = (cot.astype(F32) * (gate * keep)).astype(BF16)
    sent_ref[...] = sent
    flush(2)
    bundle[:, :width] = flat
    bundle[:, width : 2 * width] = sent
    writes = []

    def forward(first, size):
        span = pl.ds(first, size)
        write = pltpu.make_async_copy(
            bundle.at[:, span], bundle_ref.at[:, span], sems.at[2, len(writes)]
        )
        write.start()
        writes.append(write)

    forward(0, 2 * width)
    produced = jnp.zeros((total, width), F32)
    grad = jnp.zeros((total, width), F32)
    inner = math.sqrt(2.0 / math.pi)
    for i, pair in enumerate(copies):
        own_side = i < steps
        first = (i % steps) * chunk
        for copy in pair:
            copy.wait()
        win, wdown = in_vmem[i], down_vmem[i]
        pre = dot(flat, win)
        square = pre * pre
        curve = jnp.tanh(inner * pre * (1.0 + 0.044715 * square))
        half_up = 0.5 + 0.5 * curve
        act = (pre * half_up).astype(BF16)
        slope = half_up + (0.5 * inner) * pre * (1.0 - curve * curve) * (
            1.0 + (3 * 0.044715) * square
        )
        grad_pre = (slope * cols_by_cols(sent, wdown)).astype(BF16)
        if own_side:
            hid_own_ref[:, first : first + chunk] = act
            pre_own_ref[:, first : first + chunk] = grad_pre
        else:
            first += 2 * width
            bundle[:, first : first + chunk] = act
            bundle[:, first + hidden : first + hidden + chunk] = grad_pre
            forward(first, chunk)
            forward(first + hidden, chunk)
        if i + 1 == steps:
            flush(0)
            flush(1)
        produced = produced + dot(act, wdown)
        grad = grad + cols_by_cols(grad_pre, win)
    produced_low = produced.astype(BF16)
    kept = produced_low.astype(F32) * keep
    produced_ref[...] = kept.astype(BF16)
    flush(5)
    grad_gate = jnp.sum(cot.astype(F32) * kept, axis=-1, keepdims=True)
    grad_logits = ((grad_gate * gate) * (onehot - router_probs)).astype(BF16)
    grad_ref[...] = (grad * keep + dot(grad_logits, router_ref[...])).astype(BF16)
    flush(4)
    router_grad_ref[...] = rows_by_rows(grad_logits, flat)
    for write in writes:
        write.wait()


def expert_weights_kernel(
    flat_own, sent_own, hid_own, pre_own, flat_other, sent_other, hid_other, pre_other, in_ref, down_ref
):
    in_ref[0] = rows_by_rows(flat_own[...], pre_own[...]) + rows_by_rows(
        flat_other[...], pre_other[...]
    )
    down_ref[0] = rows_by_rows(hid_own[...], sent_own[...]) + rows_by_rows(
        hid_other[...], sent_other[...]
    )


def expert_weights(flat, sent, hid, pre, bundle, chunk):
    total, width = sent.shape
    hidden = hid.shape[1]
    steps = hidden // chunk
    skip = 2 * width // chunk
    whole = pl.BlockSpec((total, width), lambda i: (0, 0))
    second = pl.BlockSpec((total, width), lambda i: (0, 1))
    part = pl.BlockSpec((total, chunk), lambda i: (0, i))
    return pl.pallas_call(
        expert_weights_kernel,
        grid=(steps,),
        out_shape=[
            jax.ShapeDtypeStruct((1, width, hidden), F32),
            jax.ShapeDtypeStruct((1, hidden, width), F32),
        ],
        in_specs=[
            whole,
            whole,
            part,
            part,
            whole,
            second,
            pl.BlockSpec((total, chunk), lambda i: (0, i + skip)),
            pl.BlockSpec((total, chunk), lambda i: (0, i + skip + steps)),
        ],
        out_specs=[
            pl.BlockSpec((1, width, chunk), lambda i: (0, 0, i)),
            pl.BlockSpec((1, chunk, width), lambda i: (0, i, 0)),
        ],
        compiler_params=pltpu.CompilerParams(vmem_limit_bytes=64 * 2**20),
        cost_estimate=pl.CostEstimate(
            flops=8 * total * width * hidden, bytes_accessed=14000000, transcendentals=0
        ),
    )(flat, sent, hid, pre, bundle, bundle, bundle, bundle)


def middle_back(returned, fetch, middle, gain, cot):
    grad = dot(fetch, returned)
    root = root_mean(middle)
    scaled = middle * root
    up = gain * grad
    grad_middle = cot.astype(F32) + root * (
        up - scaled * jnp.mean(up * scaled, axis=-1, keepdims=True)
    )
    return grad_middle, grad * scaled


def bit_of(step, other=0):
    return jnp.where(lax.axis_index("ffn") == other, step[0], step[1])


def chunk_place(chunk, order, levels, other=0):
    chip = lax.axis_index("expert")
    mine = 0
    for step in order[:levels]:
        mine = mine * 2 + jnp.bitwise_and(jnp.right_shift(chip, bit_of(step, other)), 1)
    return jnp.bitwise_xor(mine, chunk)


def small_rows(experts):
    return [0, 2, 4, 16, 16 + experts, 16 + 2 * experts]


def backward_kernel(
    heads,
    orders,
    levels,
    wait,
    flush,
    returned_ref,
    returned_other_ref,
    fetch_ref,
    fetch_other_ref,
    middle_ref,
    middle_other_ref,
    cot_ref,
    cot_other_ref,
    gain_second_ref,
    mixed_own_ref,
    mixed_other_ref,
    value_ref,
    probs_ref,
    key_ref,
    query_ref,
    act_ref,
    hot_ref,
    own_ref,
    other_ref,
    router_ref,
    after_ref,
    wo_ref,
    wq_ref,
    wk_ref,
    wv_ref,
    keep_0_ref,
    send_0_ref,
    keep_1_ref,
    send_1_ref,
    keep_2_ref,
    send_2_ref,
    grad_middle_ref,
    small_ref,
    input_own_ref,
    input_other_ref,
    wo_half,
    wq_half,
    wk_half,
    wv_half,
    part_0,
    part_1,
    part_2,
    small,
    sems,
):
    rows, width = middle_ref.shape
    size = width // heads
    part = width // 2
    experts = router_ref.shape[0]
    scale = 1.0 / math.sqrt(size)
    core = lax.axis_index("ffn")
    span = pl.ds(pl.multiple_of(core * part, LANES), part)
    copies = [
        pltpu.make_async_copy(src, half, sems.at[6 + i])
        for i, (src, half) in enumerate(
            (
                (wo_ref.at[span, :], wo_half),
                (wq_ref.at[:, span], wq_half),
                (wk_ref.at[:, span], wk_half),
                (wv_ref.at[:, span], wv_half),
            )
        )
    ]
    for copy in copies:
        copy.start()
    parts = (part_0, part_1, part_2)
    halves = ((keep_0_ref, send_0_ref), (keep_1_ref, send_1_ref), (keep_2_ref, send_2_ref))
    third = width // 3
    height = third >> levels
    writes = []
    for p, pair in enumerate(halves):
        rows_half = pair[0].shape[0]
        for i, ref in enumerate(pair):
            writes.append(
                pltpu.make_async_copy(
                    parts[p].at[pl.ds(i * rows_half, rows_half), :], ref, sems.at[2 * p + i]
                )
            )
    places = [
        [chunk_place(chunk, order, levels) * (4 * height) for chunk in range(2**levels)]
        for order in orders
    ]

    def pack(matrix, value):
        for p, ref in enumerate(parts):
            for chunk in range(2**levels):
                first = p * third + chunk * height
                at = pl.multiple_of(places[p][chunk] + matrix * height, 16)
                ref[pl.ds(at, height), :] = value[first : first + height]

    for i in range(9):
        wait(i)
    copies[0].wait()
    gain = gain_second_ref[...].reshape(1, width)
    grad_own, gain_terms = middle_back(
        returned_ref[...], fetch_ref[...], middle_ref[...], gain, cot_ref[...]
    )
    grad_other, _ = middle_back(
        returned_other_ref[...], fetch_other_ref[...], middle_other_ref[...], gain, cot_other_ref[...]
    )
    gain_second = jnp.sum(gain_terms, axis=0, keepdims=True)
    grad_middle_ref[...] = grad_own
    flush(6)
    grad_low = jnp.concatenate([grad_own, grad_other], axis=0).astype(BF16)
    grad_mixed = cols_by_cols(grad_low, wo_half[...]).astype(BF16)
    for i in range(9, 20):
        wait(i)
    for copy in copies[1:]:
        copy.wait()
    mixed = jnp.concatenate([mixed_own_ref[...], mixed_other_ref[...]], axis=0)
    grad_columns = jnp.where(core == 0, grad_low[:, :part], grad_low[:, part:])
    pack(3, rows_by_rows(mixed, grad_columns).astype(BF16))
    low_half = lax.broadcasted_iota(jnp.int32, (2 * rows, 2 * size), 1) < size
    grad_q, grad_k, grad_v = [], [], []
    same, ahead, behind = [], [], []
    for pair in range(heads // 4):
        lanes = slice(pair * 2 * size, (pair + 1) * 2 * size)
        query, key, value = query_ref[:, lanes], key_ref[:, lanes], value_ref[:, lanes]
        grad_pair = grad_mixed[:, lanes]
        got_q, got_k, got_v = [], [], []
        for side in range(2):
            probs = probs_ref[2 * pair + side]
            keep_lanes = low_half if side == 0 else jnp.logical_not(low_half)
            own_grad = jnp.where(keep_lanes, grad_pair, 0).astype(BF16)
            grad_probs = cols_by_cols(own_grad, value)
            got_v.append(rows_by_rows(probs.astype(BF16), grad_pair))
            inner = jnp.sum(probs * grad_probs, axis=-1, keepdims=True)
            grad_scores = probs * (grad_probs - inner)
            same.append(
                diagonal_sums(grad_scores[:rows, :rows] + grad_scores[rows:, rows:], rows)
            )
            first = diagonal_sums(grad_scores[:rows, rows:], rows)
            second = diagonal_sums(grad_scores[rows:, :rows], rows)
            ahead.append(jnp.where(core == 1, first, second))
            behind.append(jnp.where(core == 1, second, first))
            grad_raw = (grad_scores * scale).astype(BF16)
            got_q.append(dot(grad_raw, key))
            got_k.append(rows_by_rows(grad_raw, query))
        grad_q.append(jnp.where(low_half, got_q[0], got_q[1]).astype(BF16))
        grad_k.append(jnp.where(low_half, got_k[0], got_k[1]).astype(BF16))
        grad_v.append(jnp.where(low_half, got_v[0], got_v[1]).astype(BF16))
    grad_q = jnp.concatenate(grad_q, axis=1)
    grad_k = jnp.concatenate(grad_k, axis=1)
    grad_v = jnp.concatenate(grad_v, axis=1)
    act = act_ref[...]
    pack(0, rows_by_rows(act, grad_q).astype(BF16))
    pack(1, rows_by_rows(act, grad_k).astype(BF16))
    pack(2, rows_by_rows(act, grad_v).astype(BF16))
    for write in writes:
        write.start()
    grad_act = (
        cols_by_cols(grad_q, wq_half[...])
        + cols_by_cols(grad_k, wk_half[...])
        + cols_by_cols(grad_v, wv_half[...])
    )
    input_other_ref[...] = grad_act[rows:].astype(BF16)
    flush(9)
    input_own_ref[...] = grad_act[:rows]
    flush(8)
    x = own_ref[...].astype(F32)
    y = other_ref[...].astype(F32)
    gain_first = jnp.sum(
        grad_act[:rows] * (x * root_mean(x)) + grad_act[rows:] * (y * root_mean(y)),
        axis=0,
        keepdims=True,
    )
    sums = jnp.concatenate(
        [jnp.concatenate(part_sums, axis=0) for part_sums in (same, ahead, behind)], axis=1
    )
    table = lax.dot_general(
        sums,
        hot_ref[...],
        (((1,), (1,)), ((), ())),
        precision=TOP_PRECISION,
        preferred_element_type=F32,
    )
    at = small_rows(experts)
    small[: at[3]] = jnp.zeros((at[3], part), F32)
    for i, value in enumerate((gain_first, gain_second)):
        small[at[i] : at[i] + 1] = value[:, :part]
        small[at[i] + 1 : at[i] + 2] = value[:, part:]
    small[at[2] : at[2] + heads // 2, : table.shape[1]] = table
    small[at[3] : at[4]] = router_ref[:, :part]
    small[at[4] : at[5]] = router_ref[:, part:]
    small_ref[...] = small[...].astype(BF16)
    flush(7)
    for write in writes:
        write.wait()


def assemble_kernel(orders, levels, sides, upper, last, wait, flush, *refs):
    count = len(orders) * len(sides)
    arrays, refs = refs[:count], refs[count:]
    if last is not None:
        experts, heads = last
        (small_own_ref, small_other_ref), refs = refs[:2], refs[2:]
        last_inputs = (count, count + 1)
    if upper:
        refs = refs[4:]
    outs, (wide, sems) = refs[:4], refs[-2:]
    if last is not None:
        gain_first_ref, gain_second_ref, table_ref, router_ref = refs[4:8]
    width = outs[0].shape[1]
    part = width // 2
    third = width // 3
    span = third // 2
    height = third >> levels
    half = 2 ** (levels - 1)
    core = lax.axis_index("ffn")
    mine = lax.axis_index("expert")
    columns = [
        pl.ds(pl.multiple_of((1 - core if side else core) * part, LANES), part) for side in sides
    ]
    writes = []
    for p, order in enumerate(orders):
        for i, side in enumerate(sides):
            n = len(sides) * p + i
            wait(n)
            bit = jnp.bitwise_and(jnp.right_shift(mine, bit_of(order[0], side)), 1)
            if upper:
                bit = 1 - bit
            first = pl.multiple_of(p * third + bit * span, span)
            places = [
                jnp.bitwise_and(chunk_place(low, order, levels, side), half - 1)
                for low in range(half)
            ]
            for matrix in range(4):
                for low in range(half):
                    at = pl.multiple_of((places[low] * 4 + matrix) * height, height)
                    wide[n, matrix, pl.ds(low * height, height)] = arrays[n][
                        pl.ds(at, height), :
                    ].astype(F32)
                write = pltpu.make_async_copy(
                    wide.at[n, matrix],
                    outs[matrix].at[pl.ds(first, span), columns[i]],
                    sems.at[4 * n + matrix],
                )
                write.start()
                writes.append(write)
    if last is not None:
        for i in last_inputs:
            wait(i)
        at = small_rows(experts)
        mine, other = small_own_ref[...], small_other_ref[...]
        both = mine + other
        gain_first_ref[...] = jnp.concatenate([both[0:1], both[1:2]], axis=1).reshape(width)
        gain_second_ref[...] = jnp.concatenate([both[2:3], both[3:4]], axis=1).reshape(width)
        buckets = table_ref.shape[1]
        low = mine[at[2] : at[2] + heads // 2, :buckets]
        high = other[at[2] : at[2] + heads // 2, :buckets]
        table_ref[...] = jnp.where(
            core == 0,
            jnp.concatenate([low, high], axis=0),
            jnp.concatenate([high, low], axis=0),
        )
        router_ref[...] = jnp.concatenate([both[at[3] : at[4]], both[at[4] : at[5]]], axis=1)
    for write in writes:
        write.wait()


def assemble(orders, levels, sides, arrays, width, earlier=(), smalls=(), last=None):
    tail = []
    modes = "l" * len(arrays)
    if last is not None:
        experts, heads, buckets = last
        tail = [((width,), F32), ((width,), F32), ((heads, buckets), F32), ((experts, width), F32)]
        modes += "ll"
        last = (experts, heads)
    first = len(modes)
    modes += "r" * len(earlier)
    return call(
        functools.partial(assemble_kernel, orders, levels, sides, bool(earlier), last),
        [((width, width), F32)] * 4 + tail,
        (*arrays, *smalls, *earlier),
        modes + "rrrr" + "h" * len(tail),
        vmem=16,
        aliases={first + i: i for i in range(len(earlier))},
        scratch=[
            pltpu.VMEM((len(arrays), 4, width // 6, width // 2), F32),
            pltpu.SemaphoreType.DMA((4 * len(arrays),)),
        ],
        nbytes=8000000,
    )


def swap(x):
    return lax.ppermute(x, "ffn", [(0, 1), (1, 0)])


def flip(x, step):
    pairs = []
    for chip in range(lax.axis_size("expert")):
        for core in range(2):
            pairs.append((chip * 2 + core, (chip ^ (1 << step[core])) * 2 + core))
    return lax.ppermute(x, ("expert", "ffn"), pairs)


def add_low(left, right):
    return (left.astype(F32) + right.astype(F32)).astype(BF16)


def sum_over_chips(keeps, sends, orders, levels, small, beside):
    count = len(orders[0])
    todo = [set(step[core] for step in orders[0]) for core in range(2)]
    ridden = set()

    def exchange(phase, x, bit):
        nonlocal small
        fresh = all(bit[core] in todo[core] for core in range(2))
        if not fresh or phase in ridden or phase < 2 or phase > 2 * count - 3:
            return flip(x, bit)
        for core in range(2):
            todo[core].discard(bit[core])
        ridden.add(phase)
        sent = small.astype(BF16)
        got = flip(jnp.concatenate([x, sent]), bit)
        rows = x.shape[0]
        small = sent.astype(F32) + got[rows:].astype(F32)
        return got[:rows]

    def mine(bit):
        return (lax.axis_index("expert") >> bit_of(bit)) & 1

    whole = [None] * len(orders)
    for k in range(count - 1):
        for p, order in enumerate(orders):
            keep, got = keeps[p], exchange(k, sends[p], order[k])
            half = keep.shape[0] // 2
            if k + 2 == count:
                whole[p] = add_low(keep, got)
            elif k + 1 < levels:
                keeps[p] = add_low(keep[:half], got[:half])
                sends[p] = add_low(keep[half:], got[half:])
            else:
                both = add_low(keep, got)
                upper = mine(order[k + 1])
                keeps[p] = lax.dynamic_slice_in_dim(both, upper * half, half, 0)
                sends[p] = lax.dynamic_slice_in_dim(both, (1 - upper) * half, half, 0)
    ended = [None] * len(orders)
    for p, order in enumerate(orders):
        ended[p] = exchange(count - 1, whole[p], order[-1])
    for p, ahead in ((1, None), (2, 1), (0, 1)):
        x = whole[p]
        if ahead is not None:
            x, whole[ahead] = lax.optimization_barrier((x, whole[ahead]))
        whole[p] = add_low(x, ended[p])
    got = [None] * len(orders)
    for k in reversed(range(count - 1)):
        for p, order in enumerate(orders):
            x = whole[p]
            got[p] = exchange(2 * count - 2 - k, x, order[k])
            if k == 0:
                continue
            if k < levels:
                whole[p] = jnp.concatenate([x, got[p]])
            else:
                whole[p] = jnp.where(
                    mine(order[k]) == 1,
                    jnp.concatenate([got[p], x]),
                    jnp.concatenate([x, got[p]]),
                )
    for bit in zip(sorted(todo[0]), sorted(todo[1])):
        sent = small.astype(BF16)
        small = sent.astype(F32) + flip(sent, bit).astype(F32)
    return whole, got, small, beside


def shards(
    tokens,
    norm_first,
    w_query,
    w_key,
    w_value,
    w_out,
    bucket_bias_table,
    norm_second,
    w_router,
    w_in,
    w_down,
    expert_ids,
    cotangent,
):
    rows, width = tokens.shape
    buckets, heads = bucket_bias_table.shape
    pair = lax.axis_size("ffn")
    experts = w_router.shape[1]
    total = 2 * rows
    capacity = 5 * rows * pair // 4
    hidden = w_in.shape[2]
    part = width // 2
    hot = jnp.asarray(bucket_windows(rows, buckets, REACH))
    router = w_router.T

    other = swap(tokens)
    ids = expert_ids.reshape(1, rows)
    ids_other = swap(ids)
    middle, gate, outgoing, mixed, windows, fetch, fetch_other, root = call(
        functools.partial(forward_kernel, heads),
        [
            ((rows, width), F32),
            ((rows, LANES), F32),
            ((total, 2 * width + LANES), BF16),
            ((rows, width), BF16),
            ((heads, 6 * rows), F32),
            ((rows, total), BF16),
            ((rows, total), BF16),
            ((rows, LANES), F32),
        ],
        (
            tokens,
            other,
            norm_first,
            ids,
            ids_other,
            bucket_bias_table.T,
            hot,
            w_key,
            w_value,
            w_query,
            w_out,
            norm_second,
            router,
            cotangent,
        ),
        "hhhhhhhlllslll" + "hhrhhhhh",
        vmem=64,
        flops=3000000000,
        scratch=[
            pltpu.VMEM((heads, rows, 2 * rows), F32),
            pltpu.VMEM((total, 2 * width + LANES), BF16),
            pltpu.SemaphoreType.DMA((2,)),
        ],
    )
    arrived = lax.all_to_all(outgoing, "expert", 0, 0, tiled=True)
    gate, w_in, w_down, cot_own = lax.optimization_barrier((gate, w_in, w_down, cotangent))
    in_own, down_own = w_in[0], w_down[0]
    in_other, down_other = swap(in_own), swap(down_own)
    cot_other = swap(cot_own)
    mixed_other, middle_other = swap(mixed), swap(middle)
    act, queries, keys, values, probs = call(
        functools.partial(halves_kernel, heads),
        [
            ((2 * rows, width), BF16),
            ((2 * rows, part), BF16),
            ((2 * rows, part), BF16),
            ((2 * rows, part), BF16),
            ((heads // 2, 2 * rows, 2 * rows), F32),
        ],
        (tokens, other, norm_first, w_query, w_key, w_value, windows, gate),
        "hhhrrrhr" + "hhhhh",
        vmem=64,
        flops=3000000000,
        scratch=[pltpu.VMEM((width, part), BF16)] * 3 + [pltpu.SemaphoreType.DMA((3,))],
    )
    act, cot_other, mixed_other, middle_other = lax.optimization_barrier(
        (act, cot_other, mixed_other, middle_other)
    )
    chunk = hidden // 2
    steps = 2 * hidden // chunk
    hid_own, pre_own, sent, bundle, grad_slots, produced, router_part = call(
        functools.partial(expert_kernel, capacity, chunk),
        [
            ((total, hidden), BF16),
            ((total, hidden), BF16),
            ((total, width), BF16),
            ((total, 2 * width + 2 * hidden), BF16),
            ((total, width), BF16),
            ((total, width), BF16),
            ((experts, width), F32),
        ],
        (arrived, router, in_own, in_other, down_own, down_other, act),
        "llrrrrr" + "hhhrhhh",
        vmem=64,
        flops=6000000000,
        scratch=[
            pltpu.VMEM((steps, width, chunk), BF16),
            pltpu.VMEM((steps, chunk, width), BF16),
            pltpu.VMEM((total, 2 * width + 2 * hidden), BF16),
            pltpu.SemaphoreType.DMA((3, steps + 1)),
        ],
    )
    bundle_other = swap(bundle)
    grad_returned = lax.all_to_all(grad_slots, "expert", 0, 0, tiled=True)
    grad_w_in, grad_w_down = expert_weights(arrived, sent, hid_own, pre_own, bundle_other, 256)
    produced, grad_returned, grad_w_in = lax.optimization_barrier(
        (produced, grad_returned, grad_w_in)
    )
    produced_returned = lax.all_to_all(produced, "expert", 0, 0, tiled=True)
    bits = experts.bit_length() - 1
    levels = min(bits - 1, 3)
    rest = [(bit, bit) for bit in range(3, bits)]
    orders = [
        [(0, 2), (1, 0), (2, 1)] + rest,
        [(1, 0), (2, 1), (0, 2)] + rest,
        [(2, 1), (0, 2), (1, 0)] + rest,
    ]
    third = 4 * width // 3
    *halves, grad_middle, small, input_own, input_other = call(
        functools.partial(backward_kernel, heads, orders, levels),
        [((third // 2, part), BF16)] * 6
        + [
            ((rows, width), F32),
            ((16 + 2 * experts, part), BF16),
            ((rows, width), F32),
            ((rows, width), BF16),
        ],
        (
            grad_returned,
            swap(grad_returned),
            fetch,
            fetch_other,
            middle,
            middle_other,
            cotangent,
            cot_other,
            norm_second,
            mixed,
            mixed_other,
            values,
            probs,
            keys,
            queries,
            act,
            hot,
            tokens,
            other,
            router_part,
            grad_w_in,
            w_out,
            w_query,
            w_key,
            w_value,
        ),
        "l" * 20 + "rrrrr" + "rrrrrr" + "hhhh",
        vmem=56,
        flops=4000000000,
        scratch=[
            pltpu.VMEM((part, width), BF16),
            *[pltpu.VMEM((width, part), BF16)] * 3,
            *[pltpu.VMEM((third, part), BF16)] * 3,
            pltpu.VMEM((16 + 2 * experts, part), F32),
            pltpu.SemaphoreType.DMA((10,)),
        ],
    )
    keeps, grad_middle, small, input_own, input_other, produced_returned = (
        lax.optimization_barrier(
            (halves[0::2], grad_middle, small, input_own, input_other, produced_returned)
        )
    )
    beside = (grad_middle, input_own, swap(input_other), produced_returned)
    kept, got, small, beside = sum_over_chips(
        list(keeps), list(halves[1::2]), orders, levels, small, beside
    )
    grad_middle, input_own, input_swapped, produced_returned = beside
    root = root[:, :1]
    scaled = tokens.astype(F32) * root
    up = norm_first * (input_own + input_swapped.astype(F32))
    grad_input = grad_middle + root * (
        up - scaled * jnp.mean(up * scaled, axis=-1, keepdims=True)
    )
    expert_branch = gate[:, :1] * dot(fetch, produced_returned)
    output = (middle + expert_branch).astype(BF16)
    near = []
    for rows_kept in kept:
        near += [rows_kept, swap(rows_kept)]
    small_other = swap(small)
    *matrices, gain_first, gain_second, table, router_sum = assemble(
        orders,
        levels,
        (0, 1),
        near,
        width,
        smalls=(small, small_other),
        last=(experts, heads, buckets),
    )
    got, matrices, output, expert_branch, grad_input = lax.optimization_barrier(
        (got, matrices, output, expert_branch, grad_input)
    )
    far = [swap(rows_got) for rows_got in got]
    matrices = assemble(orders, levels, (0,), got, width, matrices)
    matrices = assemble(orders, levels, (1,), far, width, matrices)
    return (
        output,
        grad_input,
        gain_first,
        *matrices,
        table.T,
        gain_second,
        router_sum.T,
        grad_w_in,
        grad_w_down,
        expert_branch,
    )


def solution(mesh):
    placed = (
        P(("expert", "ffn"), None),
        P(),
        P(),
        P(),
        P(),
        P(),
        P(),
        P(),
        P(),
        P("expert", None, "ffn"),
        P("expert", "ffn", None),
        P(("expert", "ffn")),
        P(("expert", "ffn"), None),
    )
    return jax.shard_map(
        shards,
        mesh=mesh,
        in_specs=placed,
        out_specs=(
            P(("expert", "ffn"), None),
            P(("expert", "ffn"), None),
            P(),
            P(),
            P(),
            P(),
            P(),
            P(),
            P(),
            P(),
            P("expert", None, "ffn"),
            P("expert", "ffn", None),
            P(("expert", "ffn"), None),
        ),
        check_vma=False,
    )
```

```python
import functools
import math

import jax
import jax.numpy as jnp
import numpy as np
from jax import lax
from jax.experimental import pallas as pl
from jax.experimental.pallas import tpu as pltpu
from jax.sharding import PartitionSpec as P

REACH = 128
EPS = 1e-06
TOP_PRECISION = lax.Precision.HIGHEST
LANES = 128
F32 = jnp.float32
BF16 = jnp.bfloat16


def bucket_of(distance, buckets, reach):
    half = buckets // 2
    exact = half // 2
    result = np.where(distance < 0, half, 0)
    magnitude = np.abs(distance)
    spread = exact + np.floor(
        np.log(np.maximum(magnitude, 1) / exact) / np.log(reach / exact) * (half - exact)
    )
    spread = np.minimum(spread, half - 1)
    return result + np.where(magnitude < exact, magnitude, spread)


def bucket_windows(rows, buckets, reach):
    lane = np.arange(2 * rows)
    offset = np.where(lane < rows, -lane, 2 * rows - lane)
    windows = []
    for shift in (0, rows, -rows):
        hot = bucket_of(offset + shift, buckets, reach)[None, :] == np.arange(buckets)[:, None]
        hot[:, rows] = False
        windows.append(hot)
    return np.concatenate(windows, axis=1).astype(np.float32)


def rows_by_rows(left, right):
    return lax.dot_general(left, right, (((0,), (0,)), ((), ())), preferred_element_type=F32)


def cols_by_cols(left, right):
    return lax.dot_general(left, right, (((1,), (1,)), ((), ())), preferred_element_type=F32)


def dot(left, right):
    return jnp.dot(left, right, preferred_element_type=F32)


def root_mean(x):
    return lax.rsqrt(jnp.mean(x * x, axis=-1, keepdims=True) + EPS)


def call(body, outs, args, modes, vmem=16, flops=0, scratch=(), aliases=None, nbytes=1000000):
    count, total = len(args), len(args) + len(outs)
    shapes = [(a.shape, a.dtype) for a in args] + list(outs)
    moved = [i for i in range(total) if modes[i] in "hls"]
    buffers = [pltpu.VMEM(*shapes[i]) for i in moved]

    def kernel(*refs):
        bodies = list(refs[:total])
        for i, ref in zip(moved, refs[total : total + len(moved)]):
            bodies[i] = ref
        extra = refs[total + len(moved) : -1]
        sems = refs[-1]
        copies = {}
        for i in moved:
            ends = (refs[i], bodies[i]) if i < count else (bodies[i], refs[i])
            copies[i] = pltpu.make_async_copy(*ends, sems.at[i])
        for i in moved:
            if i < count and modes[i] != "s":
                copies[i].start()
        flushed = set()

        def wait(i):
            copies[i].wait()

        wait.start = lambda i: copies[i].start()

        def flush(i):
            flushed.add(i)
            copies[count + i].start()

        for i in moved:
            if i < count and modes[i] == "h":
                wait(i)
        body(wait, flush, *bodies, *extra)
        for i in moved:
            if i >= count and i - count not in flushed:
                copies[i].start()
        for i in moved:
            if i >= count:
                copies[i].wait()

    specs = [pl.BlockSpec(memory_space=pltpu.HBM)] * total
    return pl.pallas_call(
        kernel,
        out_shape=[jax.ShapeDtypeStruct(s, d) for s, d in outs],
        in_specs=specs[:count],
        out_specs=specs[count:],
        scratch_shapes=buffers + list(scratch) + [pltpu.SemaphoreType.DMA((total,))],
        input_output_aliases=aliases or {},
        compiler_params=pltpu.CompilerParams(vmem_limit_bytes=vmem * 2**20),
        cost_estimate=pl.CostEstimate(flops=flops, bytes_accessed=nbytes, transcendentals=0),
    )(*args)


def toeplitz(window, rows):
    wide = jnp.broadcast_to(window, (rows, 2 * rows))
    return pltpu.roll(wide, 0, 1, stride=1, stride_axis=0)[:, :rows]


def diagonal_sums(square, rows):
    wide = jnp.concatenate([square, jnp.zeros_like(square)], axis=1)
    height = rows
    while height > 1:
        height //= 2
        wide = wide[:height] + pltpu.roll(wide[height:], 2 * rows - height, 1)
    return wide


def placement(ids, experts, total):
    rows = ids.shape[1]
    slots = total // experts
    choose = (lax.broadcasted_iota(jnp.int32, (experts, rows), 0) == ids).astype(F32)
    earlier = (
        lax.broadcasted_iota(jnp.int32, (rows, rows), 0)
        < lax.broadcasted_iota(jnp.int32, (rows, rows), 1)
    ).astype(F32)
    ranks = dot(choose.astype(BF16), earlier.astype(BF16))
    rank = jnp.sum(choose * ranks, axis=0, keepdims=True)
    target = ids * slots + rank.astype(jnp.int32)
    place = (lax.broadcasted_iota(jnp.int32, (total, rows), 0) == target).astype(F32)
    return choose, place


def attend(query_pair, key_pair, scale, bias, side, low_half):
    own = jnp.where(low_half if side == 0 else jnp.logical_not(low_half), query_pair, 0)
    scores = cols_by_cols(own.astype(BF16), key_pair) * scale + bias
    grown = jnp.exp(scores - jnp.max(scores, axis=-1, keepdims=True))
    return grown * (1.0 / jnp.sum(grown, axis=-1, keepdims=True))


def forward_kernel(
    heads,
    wait,
    flush,
    own_ref,
    other_ref,
    gain_first_ref,
    ids_ref,
    ids_other_ref,
    table_ref,
    hot_ref,
    wk,
    wv,
    wq,
    wo,
    gain_second_ref,
    router_ref,
    cot_ref,
    middle_ref,
    gate_ref,
    out_ref,
    mixed_ref,
    win_ref,
    fetch_ref,
    fetch_other_ref,
    root_ref,
    bias,
    staged,
    sems,
):
    rows, width = own_ref.shape
    size = width // heads
    scale = 1.0 / math.sqrt(size)
    core = lax.axis_index("ffn")
    wait.start(10)
    total = out_ref.shape[0]
    experts = router_ref.shape[0]
    sends = [
        pltpu.make_async_copy(staged.at[:, span], out_ref.at[:, span], sems.at[i])
        for i, span in enumerate((pl.ds(width, width + LANES), pl.ds(0, width)))
    ]
    choose, place = placement(ids_ref[...], experts, total)
    _, place_other = placement(ids_other_ref[...], experts, total)
    fetch_ref[...] = place.T.astype(BF16)
    fetch_other_ref[...] = place_other.T.astype(BF16)
    choose = choose.T
    lane = lax.broadcasted_iota(jnp.int32, (total, LANES), 1)
    staged[:, 2 * width :] = jnp.where(
        lane == 0,
        jnp.sum(place, axis=1, keepdims=True),
        jnp.sum(place_other, axis=1, keepdims=True),
    ).astype(BF16)
    place = place.astype(BF16)
    windows = jnp.dot(
        table_ref[...], hot_ref[...], precision=TOP_PRECISION, preferred_element_type=F32
    )
    win_ref[...] = windows
    for i in (4, 5, 6):
        flush(i)
    same = windows[:, : 2 * rows]
    apart = jnp.where(core == 1, windows[:, 2 * rows : 4 * rows], windows[:, 4 * rows :])
    for head in range(heads):
        bias[head, :, :rows] = toeplitz(same[head : head + 1], rows)
        bias[head, :, rows:] = toeplitz(apart[head : head + 1], rows)
    x = own_ref[...].astype(F32)
    y = other_ref[...].astype(F32)
    gain = gain_first_ref[...].reshape(1, width)
    root = root_mean(x)
    root_ref[...] = jnp.broadcast_to(root, root_ref.shape)
    flush(7)
    act_own = (x * root * gain).astype(BF16)
    act_other = (y * root_mean(y) * gain).astype(BF16)
    act = jnp.concatenate([act_own, act_other], axis=0)
    wait(13)
    staged[:, width : 2 * width] = dot(place, cot_ref[...]).astype(BF16)
    sends[0].start()
    wait(7)
    keys = dot(act, wk[...]).astype(BF16)
    wait(8)
    values = dot(act, wv[...]).astype(BF16)
    wait(9)
    queries = dot(act_own, wq[...]).astype(BF16)
    low_half = lax.broadcasted_iota(jnp.int32, (rows, 2 * size), 1) < size
    mixed = []
    for pair in range(heads // 2):
        lanes = slice(pair * 2 * size, (pair + 1) * 2 * size)
        outs = []
        for side in range(2):
            probs = attend(
                queries[:, lanes], keys[:, lanes], scale, bias[2 * pair + side], side, low_half
            )
            outs.append(dot(probs.astype(BF16), values[:, lanes]))
        mixed.append(jnp.where(low_half, outs[0], outs[1]).astype(BF16))
    mixed = jnp.concatenate(mixed, axis=1)
    mixed_ref[...] = mixed
    flush(3)
    for i in (10, 11, 12):
        wait(i)
    middle = x + dot(mixed, wo[...])
    middle_ref[...] = middle
    flush(0)
    gain_second = gain_second_ref[...].reshape(1, width)
    act_second = (middle * root_mean(middle) * gain_second).astype(BF16)
    staged[:, :width] = dot(place, act_second).astype(BF16)
    sends[1].start()
    logits = cols_by_cols(act_second, router_ref[...])
    grown = jnp.exp(logits - jnp.max(logits, axis=-1, keepdims=True))
    gate = jnp.sum(grown * choose, axis=-1, keepdims=True) / jnp.sum(
        grown, axis=-1, keepdims=True
    )
    gate_ref[...] = jnp.broadcast_to(gate, gate_ref.shape)
    flush(1)
    for send in sends:
        send.wait()


def halves_kernel(
    heads,
    wait,
    flush,
    own_ref,
    other_ref,
    gain_first_ref,
    wq_ref,
    wk_ref,
    wv_ref,
    win_ref,
    after_ref,
    act_ref,
    query_ref,
    key_ref,
    value_ref,
    probs_ref,
    wq_half,
    wk_half,
    wv_half,
    sems,
):
    rows, width = own_ref.shape
    size = width // heads
    part = width // 2
    scale = 1.0 / math.sqrt(size)
    core = lax.axis_index("ffn")
    columns = pl.ds(pl.multiple_of(core * part, LANES), part)
    copies = [
        pltpu.make_async_copy(ref.at[:, columns], half, sems.at[i])
        for i, (ref, half) in enumerate(((wq_ref, wq_half), (wk_ref, wk_half), (wv_ref, wv_half)))
    ]
    for copy in copies:
        copy.start()
    x = own_ref[...].astype(F32)
    y = other_ref[...].astype(F32)
    gain = gain_first_ref[...].reshape(1, width)
    act = jnp.concatenate(
        [(x * root_mean(x) * gain).astype(BF16), (y * root_mean(y) * gain).astype(BF16)], axis=0
    )
    act_ref[...] = act
    for copy in copies:
        copy.wait()
    queries = dot(act, wq_half[...]).astype(BF16)
    keys = dot(act, wk_half[...]).astype(BF16)
    values = dot(act, wv_half[...]).astype(BF16)
    query_ref[...] = queries
    key_ref[...] = keys
    value_ref[...] = values
    for i in range(4):
        flush(i)
    low_half = lax.broadcasted_iota(jnp.int32, (2 * rows, 2 * size), 1) < size
    for pair in range(heads // 4):
        lanes = slice(pair * 2 * size, (pair + 1) * 2 * size)
        for side in range(2):
            head = 2 * pair + side
            window = win_ref[pl.ds(core * (heads // 2) + head, 1), :]
            same = toeplitz(window[:, : 2 * rows], rows)
            ahead = toeplitz(window[:, 2 * rows : 4 * rows], rows)
            behind = toeplitz(window[:, 4 * rows :], rows)
            first = jnp.where(core == 1, ahead, behind)
            second = jnp.where(core == 1, behind, ahead)
            bias = jnp.concatenate(
                [
                    jnp.concatenate([same, first], axis=1),
                    jnp.concatenate([second, same], axis=1),
                ],
                axis=0,
            )
            probs_ref[head] = attend(
                queries[:, lanes], keys[:, lanes], scale, bias, side, low_half
            ).astype(BF16)


def expert_kernel(
    capacity,
    chunk,
    wait,
    flush,
    arrived_ref,
    router_ref,
    in_own_ref,
    in_other_ref,
    down_own_ref,
    down_other_ref,
    after_ref,
    hid_own_ref,
    pre_own_ref,
    sent_ref,
    bundle_ref,
    grad_ref,
    produced_ref,
    router_grad_ref,
    in_vmem,
    down_vmem,
    bundle,
    sems,
):
    total = arrived_ref.shape[0]
    experts, width = router_ref.shape
    slots = total // experts
    hidden = in_own_ref.shape[1]
    steps = hidden // chunk
    mine = lax.axis_index("expert")
    core = lax.axis_index("ffn")
    copies = []
    for side, (win, wdown) in enumerate(
        ((in_own_ref, down_own_ref), (in_other_ref, down_other_ref))
    ):
        for step in range(steps):
            i = side * steps + step
            span = pl.ds(step * chunk, chunk)
            copies.append(
                (
                    pltpu.make_async_copy(win.at[:, span], in_vmem.at[i], sems.at[0, i]),
                    pltpu.make_async_copy(wdown.at[span, :], down_vmem.at[i], sems.at[1, i]),
                )
            )
    for copy in copies[0]:
        copy.start()
    for i in (0, 1):
        wait(i)
    for pair in copies[1:]:
        for copy in pair:
            copy.start()
    flat = arrived_ref[:, :width]
    cot = arrived_ref[:, width : 2 * width]
    filled = arrived_ref[:, 2 * width :]
    row = lax.broadcasted_iota(jnp.int32, (total, total), 0)
    col = lax.broadcasted_iota(jnp.int32, (total, total), 1)
    shift = slots.bit_length() - 1
    row_block = jnp.right_shift(row, shift)
    col_block = jnp.right_shift(col, shift)
    before = (col_block < row_block).astype(F32).astype(BF16)
    ahead = (col_block < row_block + core).astype(F32).astype(BF16)
    slot = jnp.bitwise_and(lax.broadcasted_iota(jnp.int32, (total, 1), 0), slots - 1)
    position = dot(before, filled)[:, 0:1] + dot(ahead, filled)[:, 1:2] + slot.astype(F32)
    keep = jnp.where(position < capacity, 1.0, 0.0)
    logits = cols_by_cols(flat, router_ref[...])
    grown = jnp.exp(logits - jnp.max(logits, axis=-1, keepdims=True))
    router_probs = grown / jnp.sum(grown, axis=-1, keepdims=True)
    onehot = (lax.broadcasted_iota(jnp.int32, (total, experts), 1) == mine).astype(F32)
    gate = jnp.sum(router_probs * onehot, axis=-1, keepdims=True)
    sent = (cot.astype(F32) * (gate * keep)).astype(BF16)
    sent_ref[...] = sent
    flush(2)
    bundle[:, :width] = flat
    bundle[:, width : 2 * width] = sent
    writes = []

    def forward(first, size):
        span = pl.ds(first, size)
        write = pltpu.make_async_copy(
            bundle.at[:, span], bundle_ref.at[:, span], sems.at[2, len(writes)]
        )
        write.start()
        writes.append(write)

    forward(0, 2 * width)
    produced = jnp.zeros((total, width), F32)
    grad = jnp.zeros((total, width), F32)
    inner = math.sqrt(2.0 / math.pi)
    for i, pair in enumerate(copies):
        own_side = i < steps
        first = (i % steps) * chunk
        for copy in pair:
            copy.wait()
        win, wdown = in_vmem[i], down_vmem[i]
        pre = dot(flat, win)
        square = pre * pre
        curve = jnp.tanh(inner * pre * (1.0 + 0.044715 * square))
        half_up = 0.5 + 0.5 * curve
        act = (pre * half_up).astype(BF16)
        slope = half_up + (0.5 * inner) * pre * (1.0 - curve * curve) * (
            1.0 + (3 * 0.044715) * square
        )
        grad_pre = (slope * cols_by_cols(sent, wdown)).astype(BF16)
        if own_side:
            hid_own_ref[:, first : first + chunk] = act
            pre_own_ref[:, first : first + chunk] = grad_pre
        else:
            first += 2 * width
            bundle[:, first : first + chunk] = act
            bundle[:, first + hidden : first + hidden + chunk] = grad_pre
            forward(first, chunk)
            forward(first + hidden, chunk)
        if i + 1 == steps:
            flush(0)
            flush(1)
        produced = produced + dot(act, wdown)
        grad = grad + cols_by_cols(grad_pre, win)
    produced_low = produced.astype(BF16)
    kept = produced_low.astype(F32) * keep
    produced_ref[...] = kept.astype(BF16)
    flush(5)
    grad_gate = jnp.sum(cot.astype(F32) * kept, axis=-1, keepdims=True)
    grad_logits = ((grad_gate * gate) * (onehot - router_probs)).astype(BF16)
    grad_ref[...] = (grad * keep + dot(grad_logits, router_ref[...])).astype(BF16)
    flush(4)
    router_grad_ref[...] = rows_by_rows(grad_logits, flat)
    for write in writes:
        write.wait()


def expert_weights_kernel(
    flat_own, sent_own, hid_own, pre_own, flat_other, sent_other, hid_other, pre_other, in_ref, down_ref
):
    in_ref[0] = rows_by_rows(flat_own[...], pre_own[...]) + rows_by_rows(
        flat_other[...], pre_other[...]
    )
    down_ref[0] = rows_by_rows(hid_own[...], sent_own[...]) + rows_by_rows(
        hid_other[...], sent_other[...]
    )


def expert_weights(flat, sent, hid, pre, bundle, chunk):
    total, width = sent.shape
    hidden = hid.shape[1]
    steps = hidden // chunk
    skip = 2 * width // chunk
    whole = pl.BlockSpec((total, width), lambda i: (0, 0))
    second = pl.BlockSpec((total, width), lambda i: (0, 1))
    part = pl.BlockSpec((total, chunk), lambda i: (0, i))
    return pl.pallas_call(
        expert_weights_kernel,
        grid=(steps,),
        out_shape=[
            jax.ShapeDtypeStruct((1, width, hidden), F32),
            jax.ShapeDtypeStruct((1, hidden, width), F32),
        ],
        in_specs=[
            whole,
            whole,
            part,
            part,
            whole,
            second,
            pl.BlockSpec((total, chunk), lambda i: (0, i + skip)),
            pl.BlockSpec((total, chunk), lambda i: (0, i + skip + steps)),
        ],
        out_specs=[
            pl.BlockSpec((1, width, chunk), lambda i: (0, 0, i)),
            pl.BlockSpec((1, chunk, width), lambda i: (0, i, 0)),
        ],
        compiler_params=pltpu.CompilerParams(vmem_limit_bytes=64 * 2**20),
        cost_estimate=pl.CostEstimate(
            flops=8 * total * width * hidden, bytes_accessed=14000000, transcendentals=0
        ),
    )(flat, sent, hid, pre, bundle, bundle, bundle, bundle)


def middle_back(returned, fetch, middle, gain, cot):
    grad = dot(fetch, returned)
    root = root_mean(middle)
    scaled = middle * root
    up = gain * grad
    grad_middle = cot.astype(F32) + root * (
        up - scaled * jnp.mean(up * scaled, axis=-1, keepdims=True)
    )
    return grad_middle, grad * scaled


def bit_of(step, other=0):
    return jnp.where(lax.axis_index("ffn") == other, step[0], step[1])


def chunk_place(chunk, order, levels, other=0):
    chip = lax.axis_index("expert")
    mine = 0
    for step in order[:levels]:
        mine = mine * 2 + jnp.bitwise_and(jnp.right_shift(chip, bit_of(step, other)), 1)
    return jnp.bitwise_xor(mine, chunk)


def small_rows(experts):
    return [0, 2, 4, 16, 16 + experts, 16 + 2 * experts]


def backward_kernel(
    heads,
    orders,
    levels,
    wait,
    flush,
    returned_ref,
    returned_other_ref,
    fetch_ref,
    fetch_other_ref,
    middle_ref,
    middle_other_ref,
    cot_ref,
    cot_other_ref,
    gain_second_ref,
    mixed_own_ref,
    mixed_other_ref,
    value_ref,
    probs_ref,
    key_ref,
    query_ref,
    act_ref,
    hot_ref,
    gain_first_ref,
    router_ref,
    after_ref,
    wo_ref,
    wq_ref,
    wk_ref,
    wv_ref,
    keep_0_ref,
    send_0_ref,
    keep_1_ref,
    send_1_ref,
    keep_2_ref,
    send_2_ref,
    grad_middle_ref,
    small_ref,
    input_own_ref,
    input_other_ref,
    wo_half,
    wq_half,
    wk_half,
    wv_half,
    part_0,
    part_1,
    part_2,
    small,
    sems,
):
    rows, width = middle_ref.shape
    size = width // heads
    part = width // 2
    experts = router_ref.shape[0]
    scale = 1.0 / math.sqrt(size)
    core = lax.axis_index("ffn")
    span = pl.ds(pl.multiple_of(core * part, LANES), part)
    copies = [
        pltpu.make_async_copy(src, half, sems.at[6 + i])
        for i, (src, half) in enumerate(
            (
                (wo_ref.at[span, :], wo_half),
                (wq_ref.at[:, span], wq_half),
                (wk_ref.at[:, span], wk_half),
                (wv_ref.at[:, span], wv_half),
            )
        )
    ]
    for copy in copies:
        copy.start()
    parts = (part_0, part_1, part_2)
    halves = ((keep_0_ref, send_0_ref), (keep_1_ref, send_1_ref), (keep_2_ref, send_2_ref))
    third = width // 3
    height = third >> levels
    writes = []
    for p, pair in enumerate(halves):
        rows_half = pair[0].shape[0]
        for i, ref in enumerate(pair):
            writes.append(
                pltpu.make_async_copy(
                    parts[p].at[pl.ds(i * rows_half, rows_half), :], ref, sems.at[2 * p + i]
                )
            )
    places = [
        [chunk_place(chunk, order, levels) * (4 * height) for chunk in range(2**levels)]
        for order in orders
    ]

    def pack(matrix, value):
        for p, ref in enumerate(parts):
            for chunk in range(2**levels):
                first = p * third + chunk * height
                at = pl.multiple_of(places[p][chunk] + matrix * height, 16)
                ref[pl.ds(at, height), :] = value[first : first + height]

    for i in range(9):
        wait(i)
    copies[0].wait()
    gain = gain_second_ref[...].reshape(1, width)
    grad_own, gain_terms = middle_back(
        returned_ref[...], fetch_ref[...], middle_ref[...], gain, cot_ref[...]
    )
    grad_other, _ = middle_back(
        returned_other_ref[...], fetch_other_ref[...], middle_other_ref[...], gain, cot_other_ref[...]
    )
    gain_second = jnp.sum(gain_terms, axis=0, keepdims=True)
    grad_middle_ref[...] = grad_own
    flush(6)
    grad_low = jnp.concatenate([grad_own, grad_other], axis=0).astype(BF16)
    grad_mixed = cols_by_cols(grad_low, wo_half[...]).astype(BF16)
    for i in range(9, 19):
        wait(i)
    for copy in copies[1:]:
        copy.wait()
    mixed = jnp.concatenate([mixed_own_ref[...], mixed_other_ref[...]], axis=0)
    grad_columns = jnp.where(core == 0, grad_low[:, :part], grad_low[:, part:])
    pack(3, rows_by_rows(mixed, grad_columns).astype(BF16))
    low_half = lax.broadcasted_iota(jnp.int32, (2 * rows, 2 * size), 1) < size
    grad_q, grad_k, grad_v = [], [], []
    same, ahead, behind = [], [], []
    for pair in range(heads // 4):
        lanes = slice(pair * 2 * size, (pair + 1) * 2 * size)
        query, key, value = query_ref[:, lanes], key_ref[:, lanes], value_ref[:, lanes]
        grad_pair = grad_mixed[:, lanes]
        got_q, got_k, got_v = [], [], []
        for side in range(2):
            probs_low = probs_ref[2 * pair + side]
            probs = probs_low.astype(F32)
            keep_lanes = low_half if side == 0 else jnp.logical_not(low_half)
            own_grad = jnp.where(keep_lanes, grad_pair, 0).astype(BF16)
            grad_probs = cols_by_cols(own_grad, value)
            got_v.append(rows_by_rows(probs_low, grad_pair))
            inner = jnp.sum(probs * grad_probs, axis=-1, keepdims=True)
            grad_scores = probs * (grad_probs - inner)
            same.append(
                diagonal_sums(grad_scores[:rows, :rows] + grad_scores[rows:, rows:], rows)
            )
            first = diagonal_sums(grad_scores[:rows, rows:], rows)
            second = diagonal_sums(grad_scores[rows:, :rows], rows)
            ahead.append(jnp.where(core == 1, first, second))
            behind.append(jnp.where(core == 1, second, first))
            grad_raw = (grad_scores * scale).astype(BF16)
            got_q.append(dot(grad_raw, key))
            got_k.append(rows_by_rows(grad_raw, query))
        grad_q.append(jnp.where(low_half, got_q[0], got_q[1]).astype(BF16))
        grad_k.append(jnp.where(low_half, got_k[0], got_k[1]).astype(BF16))
        grad_v.append(jnp.where(low_half, got_v[0], got_v[1]).astype(BF16))
    grad_q = jnp.concatenate(grad_q, axis=1)
    grad_k = jnp.concatenate(grad_k, axis=1)
    grad_v = jnp.concatenate(grad_v, axis=1)
    act = act_ref[...]
    pack(0, rows_by_rows(act, grad_q).astype(BF16))
    pack(1, rows_by_rows(act, grad_k).astype(BF16))
    pack(2, rows_by_rows(act, grad_v).astype(BF16))
    for write in writes:
        write.start()
    grad_act = (
        cols_by_cols(grad_q, wq_half[...])
        + cols_by_cols(grad_k, wk_half[...])
        + cols_by_cols(grad_v, wv_half[...])
    )
    input_other_ref[...] = grad_act[rows:].astype(BF16)
    flush(9)
    input_own_ref[...] = grad_act[:rows].astype(BF16)
    flush(8)
    gain_first = jnp.sum(grad_act * act.astype(F32), axis=0, keepdims=True)
    gain_first = gain_first / gain_first_ref[...].reshape(1, width)
    sums = jnp.concatenate(
        [jnp.concatenate(part_sums, axis=0) for part_sums in (same, ahead, behind)], axis=1
    )
    table = lax.dot_general(
        sums,
        hot_ref[...],
        (((1,), (1,)), ((), ())),
        precision=TOP_PRECISION,
        preferred_element_type=F32,
    )
    at = small_rows(experts)
    small[: at[3]] = jnp.zeros((at[3], part), F32)
    for i, value in enumerate((gain_first, gain_second)):
        small[at[i] : at[i] + 1] = value[:, :part]
        small[at[i] + 1 : at[i] + 2] = value[:, part:]
    small[at[2] : at[2] + heads // 2, : table.shape[1]] = table
    small[at[3] : at[4]] = router_ref[:, :part]
    small[at[4] : at[5]] = router_ref[:, part:]
    small_ref[...] = small[...].astype(BF16)
    flush(7)
    for write in writes:
        write.wait()


def assemble_kernel(orders, levels, sides, upper, last, wait, flush, *refs):
    count = len(orders) * len(sides)
    arrays, refs = refs[:count], refs[count:]
    if last is not None:
        experts, heads = last
        (small_own_ref, small_other_ref), refs = refs[:2], refs[2:]
        last_inputs = (count, count + 1)
    if upper:
        refs = refs[4:]
    outs, (wide, sems) = refs[:4], refs[-2:]
    if last is not None:
        gain_first_ref, gain_second_ref, table_ref, router_ref = refs[4:8]
    width = outs[0].shape[1]
    part = width // 2
    third = width // 3
    span = third // 2
    height = third >> levels
    half = 2 ** (levels - 1)
    core = lax.axis_index("ffn")
    mine = lax.axis_index("expert")
    columns = [
        pl.ds(pl.multiple_of((1 - core if side else core) * part, LANES), part) for side in sides
    ]
    writes = []
    for p, order in enumerate(orders):
        for i, side in enumerate(sides):
            n = len(sides) * p + i
            wait(n)
            bit = jnp.bitwise_and(jnp.right_shift(mine, bit_of(order[0], side)), 1)
            if upper:
                bit = 1 - bit
            first = pl.multiple_of(p * third + bit * span, span)
            places = [
                jnp.bitwise_and(chunk_place(low, order, levels, side), half - 1)
                for low in range(half)
            ]
            for matrix in range(4):
                for low in range(half):
                    at = pl.multiple_of((places[low] * 4 + matrix) * height, height)
                    wide[n, matrix, pl.ds(low * height, height)] = arrays[n][
                        pl.ds(at, height), :
                    ].astype(F32)
                write = pltpu.make_async_copy(
                    wide.at[n, matrix],
                    outs[matrix].at[pl.ds(first, span), columns[i]],
                    sems.at[4 * n + matrix],
                )
                write.start()
                writes.append(write)
    if last is not None:
        for i in last_inputs:
            wait(i)
        at = small_rows(experts)
        mine, other = small_own_ref[...], small_other_ref[...]
        both = mine + other
        gain_first_ref[...] = jnp.concatenate([both[0:1], both[1:2]], axis=1).reshape(width)
        gain_second_ref[...] = jnp.concatenate([both[2:3], both[3:4]], axis=1).reshape(width)
        buckets = table_ref.shape[1]
        low = mine[at[2] : at[2] + heads // 2, :buckets]
        high = other[at[2] : at[2] + heads // 2, :buckets]
        table_ref[...] = jnp.where(
            core == 0,
            jnp.concatenate([low, high], axis=0),
            jnp.concatenate([high, low], axis=0),
        )
        router_ref[...] = jnp.concatenate([both[at[3] : at[4]], both[at[4] : at[5]]], axis=1)
    for write in writes:
        write.wait()


def assemble(orders, levels, sides, arrays, width, earlier=(), smalls=(), last=None):
    tail = []
    modes = "l" * len(arrays)
    if last is not None:
        experts, heads, buckets = last
        tail = [((width,), F32), ((width,), F32), ((heads, buckets), F32), ((experts, width), F32)]
        modes += "ll"
        last = (experts, heads)
    first = len(modes)
    modes += "r" * len(earlier)
    return call(
        functools.partial(assemble_kernel, orders, levels, sides, bool(earlier), last),
        [((width, width), F32)] * 4 + tail,
        (*arrays, *smalls, *earlier),
        modes + "rrrr" + "h" * len(tail),
        vmem=16,
        aliases={first + i: i for i in range(len(earlier))},
        scratch=[
            pltpu.VMEM((len(arrays), 4, width // 6, width // 2), F32),
            pltpu.SemaphoreType.DMA((4 * len(arrays),)),
        ],
        nbytes=8000000,
    )


def swap(x):
    return lax.ppermute(x, "ffn", [(0, 1), (1, 0)])


def flip(x, step):
    pairs = []
    for chip in range(lax.axis_size("expert")):
        for core in range(2):
            pairs.append((chip * 2 + core, (chip ^ (1 << step[core])) * 2 + core))
    return lax.ppermute(x, ("expert", "ffn"), pairs)


def add_low(left, right):
    return (left.astype(F32) + right.astype(F32)).astype(BF16)


def sum_over_chips(keeps, sends, orders, levels, small, beside):
    count = len(orders[0])
    todo = [set(step[core] for step in orders[0]) for core in range(2)]
    ridden = set()

    def exchange(phase, x, bit):
        nonlocal small
        fresh = all(bit[core] in todo[core] for core in range(2))
        if not fresh or phase in ridden or phase < 2 or phase > 2 * count - 3:
            return flip(x, bit)
        for core in range(2):
            todo[core].discard(bit[core])
        ridden.add(phase)
        sent = small.astype(BF16)
        got = flip(jnp.concatenate([x, sent]), bit)
        rows = x.shape[0]
        small = sent.astype(F32) + got[rows:].astype(F32)
        return got[:rows]

    def mine(bit):
        return (lax.axis_index("expert") >> bit_of(bit)) & 1

    whole = [None] * len(orders)
    for k in range(count - 1):
        for p, order in enumerate(orders):
            keep, got = keeps[p], exchange(k, sends[p], order[k])
            half = keep.shape[0] // 2
            if k + 2 == count:
                whole[p] = add_low(keep, got)
            elif k + 1 < levels:
                keeps[p] = add_low(keep[:half], got[:half])
                sends[p] = add_low(keep[half:], got[half:])
            else:
                both = add_low(keep, got)
                upper = mine(order[k + 1])
                keeps[p] = lax.dynamic_slice_in_dim(both, upper * half, half, 0)
                sends[p] = lax.dynamic_slice_in_dim(both, (1 - upper) * half, half, 0)
    ended = [None] * len(orders)
    for p, order in enumerate(orders):
        ended[p] = exchange(count - 1, whole[p], order[-1])
    for p, ahead in ((1, None), (2, 1), (0, 1)):
        x = whole[p]
        if ahead is not None:
            x, whole[ahead] = lax.optimization_barrier((x, whole[ahead]))
        whole[p] = add_low(x, ended[p])
    got = [None] * len(orders)
    for k in reversed(range(count - 1)):
        for p, order in enumerate(orders):
            x = whole[p]
            got[p] = exchange(2 * count - 2 - k, x, order[k])
            if k == 0:
                continue
            if k < levels:
                whole[p] = jnp.concatenate([x, got[p]])
            else:
                whole[p] = jnp.where(
                    mine(order[k]) == 1,
                    jnp.concatenate([got[p], x]),
                    jnp.concatenate([x, got[p]]),
                )
    for bit in zip(sorted(todo[0]), sorted(todo[1])):
        sent = small.astype(BF16)
        small = sent.astype(F32) + flip(sent, bit).astype(F32)
    return whole, got, small, beside


def shards(
    tokens,
    norm_first,
    w_query,
    w_key,
    w_value,
    w_out,
    bucket_bias_table,
    norm_second,
    w_router,
    w_in,
    w_down,
    expert_ids,
    cotangent,
):
    rows, width = tokens.shape
    buckets, heads = bucket_bias_table.shape
    pair = lax.axis_size("ffn")
    experts = w_router.shape[1]
    total = 2 * rows
    capacity = 5 * rows * pair // 4
    hidden = w_in.shape[2]
    part = width // 2
    hot = jnp.asarray(bucket_windows(rows, buckets, REACH))
    router = w_router.T

    other = swap(tokens)
    ids = expert_ids.reshape(1, rows)
    ids_other = swap(ids)
    middle, gate, outgoing, mixed, windows, fetch, fetch_other, root = call(
        functools.partial(forward_kernel, heads),
        [
            ((rows, width), F32),
            ((rows, LANES), F32),
            ((total, 2 * width + LANES), BF16),
            ((rows, width), BF16),
            ((heads, 6 * rows), F32),
            ((rows, total), BF16),
            ((rows, total), BF16),
            ((rows, LANES), F32),
        ],
        (
            tokens,
            other,
            norm_first,
            ids,
            ids_other,
            bucket_bias_table.T,
            hot,
            w_key,
            w_value,
            w_query,
            w_out,
            norm_second,
            router,
            cotangent,
        ),
        "hhhhhhhlllslll" + "hhrhhhhh",
        vmem=64,
        flops=3000000000,
        scratch=[
            pltpu.VMEM((heads, rows, 2 * rows), F32),
            pltpu.VMEM((total, 2 * width + LANES), BF16),
            pltpu.SemaphoreType.DMA((2,)),
        ],
    )
    arrived = lax.all_to_all(outgoing, "expert", 0, 0, tiled=True)
    gate, w_in, w_down, cot_own = lax.optimization_barrier((gate, w_in, w_down, cotangent))
    in_own, down_own = w_in[0], w_down[0]
    in_other, down_other = swap(in_own), swap(down_own)
    cot_other = swap(cot_own)
    mixed_other, middle_other = swap(mixed), swap(middle)
    act, queries, keys, values, probs = call(
        functools.partial(halves_kernel, heads),
        [
            ((2 * rows, width), BF16),
            ((2 * rows, part), BF16),
            ((2 * rows, part), BF16),
            ((2 * rows, part), BF16),
            ((heads // 2, 2 * rows, 2 * rows), BF16),
        ],
        (tokens, other, norm_first, w_query, w_key, w_value, windows, gate),
        "hhhrrrhr" + "hhhhh",
        vmem=64,
        flops=3000000000,
        scratch=[pltpu.VMEM((width, part), BF16)] * 3 + [pltpu.SemaphoreType.DMA((3,))],
    )
    act, cot_other, mixed_other, middle_other = lax.optimization_barrier(
        (act, cot_other, mixed_other, middle_other)
    )
    chunk = hidden // 2
    steps = 2 * hidden // chunk
    hid_own, pre_own, sent, bundle, grad_slots, produced, router_part = call(
        functools.partial(expert_kernel, capacity, chunk),
        [
            ((total, hidden), BF16),
            ((total, hidden), BF16),
            ((total, width), BF16),
            ((total, 2 * width + 2 * hidden), BF16),
            ((total, width), BF16),
            ((total, width), BF16),
            ((experts, width), F32),
        ],
        (arrived, router, in_own, in_other, down_own, down_other, act),
        "llrrrrr" + "hhhrhhh",
        vmem=64,
        flops=6000000000,
        scratch=[
            pltpu.VMEM((steps, width, chunk), BF16),
            pltpu.VMEM((steps, chunk, width), BF16),
            pltpu.VMEM((total, 2 * width + 2 * hidden), BF16),
            pltpu.SemaphoreType.DMA((3, steps + 1)),
        ],
    )
    bundle_other = swap(bundle)
    grad_returned = lax.all_to_all(grad_slots, "expert", 0, 0, tiled=True)
    grad_w_in, grad_w_down = expert_weights(arrived, sent, hid_own, pre_own, bundle_other, 256)
    produced, grad_returned, grad_w_in = lax.optimization_barrier(
        (produced, grad_returned, grad_w_in)
    )
    produced_returned = lax.all_to_all(produced, "expert", 0, 0, tiled=True)
    bits = experts.bit_length() - 1
    levels = min(bits - 1, 3)
    rest = [(bit, bit) for bit in range(3, bits)]
    orders = [
        [(0, 2), (1, 0), (2, 1)] + rest,
        [(1, 0), (2, 1), (0, 2)] + rest,
        [(2, 1), (0, 2), (1, 0)] + rest,
    ]
    third = 4 * width // 3
    *halves, grad_middle, small, input_own, input_other = call(
        functools.partial(backward_kernel, heads, orders, levels),
        [((third // 2, part), BF16)] * 6
        + [
            ((rows, width), F32),
            ((16 + 2 * experts, part), BF16),
            ((rows, width), BF16),
            ((rows, width), BF16),
        ],
        (
            grad_returned,
            swap(grad_returned),
            fetch,
            fetch_other,
            middle,
            middle_other,
            cotangent,
            cot_other,
            norm_second,
            mixed,
            mixed_other,
            values,
            probs,
            keys,
            queries,
            act,
            hot,
            norm_first,
            router_part,
            grad_w_in,
            w_out,
            w_query,
            w_key,
            w_value,
        ),
        "l" * 19 + "rrrrr" + "rrrrrr" + "hhhh",
        vmem=56,
        flops=4000000000,
        scratch=[
            pltpu.VMEM((part, width), BF16),
            *[pltpu.VMEM((width, part), BF16)] * 3,
            *[pltpu.VMEM((third, part), BF16)] * 3,
            pltpu.VMEM((16 + 2 * experts, part), F32),
            pltpu.SemaphoreType.DMA((10,)),
        ],
    )
    keeps, grad_middle, small, input_own, input_other, produced_returned = (
        lax.optimization_barrier(
            (halves[0::2], grad_middle, small, input_own, input_other, produced_returned)
        )
    )
    beside = (grad_middle, input_own, swap(input_other), produced_returned)
    kept, got, small, beside = sum_over_chips(
        list(keeps), list(halves[1::2]), orders, levels, small, beside
    )
    grad_middle, input_own, input_swapped, produced_returned = beside
    root = root[:, :1]
    scaled = tokens.astype(F32) * root
    up = norm_first * (input_own.astype(F32) + input_swapped.astype(F32))
    grad_input = grad_middle + root * (
        up - scaled * jnp.mean(up * scaled, axis=-1, keepdims=True)
    )
    expert_branch = gate[:, :1] * dot(fetch, produced_returned)
    output = (middle + expert_branch).astype(BF16)
    near = []
    for rows_kept in kept:
        near += [rows_kept, swap(rows_kept)]
    small_other = swap(small)
    *matrices, gain_first, gain_second, table, router_sum = assemble(
        orders,
        levels,
        (0, 1),
        near,
        width,
        smalls=(small, small_other),
        last=(experts, heads, buckets),
    )
    got, matrices, output, expert_branch, grad_input = lax.optimization_barrier(
        (got, matrices, output, expert_branch, grad_input)
    )
    far = [swap(rows_got) for rows_got in got]
    matrices = assemble(orders, levels, (0,), got, width, matrices)
    matrices = assemble(orders, levels, (1,), far, width, matrices)
    return (
        output,
        grad_input,
        gain_first,
        *matrices,
        table.T,
        gain_second,
        router_sum.T,
        grad_w_in,
        grad_w_down,
        expert_branch,
    )


def solution(mesh):
    placed = (
        P(("expert", "ffn"), None),
        P(),
        P(),
        P(),
        P(),
        P(),
        P(),
        P(),
        P(),
        P("expert", None, "ffn"),
        P("expert", "ffn", None),
        P(("expert", "ffn")),
        P(("expert", "ffn"), None),
    )
    return jax.shard_map(
        shards,
        mesh=mesh,
        in_specs=placed,
        out_specs=(
            P(("expert", "ffn"), None),
            P(("expert", "ffn"), None),
            P(),
            P(),
            P(),
            P(),
            P(),
            P(),
            P(),
            P(),
            P("expert", None, "ffn"),
            P("expert", "ffn", None),
            P(("expert", "ffn"), None),
        ),
        check_vma=False,
    )
```
